32 devices in a mesh: rows: 8 (over z, y), seq: 4 (over x, core).
Axes of the slice: x: 2, y: 2, z: 4, core: 2. Of those that a mesh axis runs over, the one named last changes fastest.
Arguments:
- inputs: bfloat16 [32, 1024, 768], P('rows', 'seq'), may hold values from -6 to 6
- segment_ids: int32 [32, 1024], P('rows'), may hold values from 0 to 3, as said below
- gain_one: float32 [768], replicated, may hold values from 0.1 to 1.9
- w_query: bfloat16 [768, 768], replicated, may hold values from -0.4375 to 0.4375
- w_key: bfloat16 [768, 768], replicated, may hold values from -0.21875 to 0.21875
- w_value: bfloat16 [768, 768], replicated, may hold values from -0.21875 to 0.21875
- w_out: bfloat16 [768, 768], replicated, may hold values from -0.875 to 0.875
- mix_logits: bfloat16 [12, 12], replicated, may hold values from -1.75 to 1.75
- mix_weights: bfloat16 [12, 12], replicated, may hold values from -1.75 to 1.75
- gain_two: float32 [768], replicated, may hold values from 0.1 to 1.9
- w_hidden: bfloat16 [768, 3072], replicated, may hold values from -0.21875 to 0.21875
- w_back: bfloat16 [3072, 768], replicated, may hold values from -0.15625 to 0.15625
- cotangent: bfloat16 [32, 1024, 768], P('rows', 'seq'), may hold values from -6 to 6
Outputs:
- block_out: bfloat16 [32, 1024, 768], P('rows', 'seq')
- grad_inputs: bfloat16 [32, 1024, 768], P('rows', 'seq')
- grad_gain_one: float32 [768], replicated
- grad_w_query: float32 [768, 768], replicated
- grad_w_key: float32 [768, 768], replicated
- grad_w_value: float32 [768, 768], replicated
- grad_w_out: float32 [768, 768], replicated
- grad_mix_logits: float32 [12, 12], replicated
- grad_mix_weights: float32 [12, 12], replicated
- grad_gain_two: float32 [768], replicated
- grad_w_hidden: float32 [768, 3072], replicated
- grad_w_back: float32 [3072, 768], replicated
The draws below stay inside these ranges and needn't reach their ends.
Inputs may be any that keep to these rules, and one draw needn't show every extreme that they name: `segment_ids`: in each row the ids never fall and name four documents 0, 1, 2, 3, each nonempty; document 2 starts before token 256, and document 3 starts at token 3 * (256) or later.
All inputs are finite; a program needn't handle non-finite values.
Results may differ from the reference program's by a relative error of at most 0.017.
The reference program's roundings to bfloat16 on the way count: a program that leaves them out, or rounds other values in their place, can miss the bound.
Values may be sent and summed in bfloat16 or wider, within the bound.
No kernel may reach another device: no remote copies, remote signals or barrier semaphores. Data moves between devices by JAX's collectives and lax.ppermute only.
A program may use at most 320 MiB of HBM per device.

```python
import jax
import jax.numpy as jnp
from jax import lax

D = 768
H = 12
DH = 64
FF = 3072
LEN = 1024
QBLOCK = 512
ROWS_DEV = 4
ROWS = 32


def draw_segment_ids(key, part):
    key = jax.random.fold_in(key, 7)
    subkeys = jax.random.split(key, 3)
    quarter = LEN // 4
    long_start = 2 + jax.random.randint(subkeys[0], (ROWS, 1), 0, quarter - 2)
    first_cut = 1 + jax.random.randint(subkeys[1], (ROWS, 1), 0, 1 << 20) % (long_start - 1)
    long_end = 3 * quarter + jax.random.randint(subkeys[2], (ROWS, 1), 0, quarter)
    positions = jnp.arange(LEN, dtype=jnp.int32)[None, :]
    return (positions >= first_cut).astype(jnp.int32) + (positions >= long_start).astype(jnp.int32) + (positions >= long_end).astype(jnp.int32)


def levels(own_key, extent, cuts, low, high):
    def one(position, blocks):
        heights = jax.random.uniform(jax.random.fold_in(jax.random.fold_in(own_key, 6), position), (blocks,), jnp.float32, low / len(cuts), high / len(cuts))
        return jnp.repeat(jnp.exp(heights), extent[position] // blocks).reshape((-1,) + (1,) * (len(extent) - position - 1))

    level = one(*cuts[0])
    for cut in cuts[1:]:
        level = level * one(*cut)
    return level


def bell_draw(key, shape, scale, reach, shards=(), held_as=jnp.bfloat16):
    values = scale * jax.random.normal(key, shape, jnp.float32)
    if shards:
        values = values * levels(key, shape, shards, -0.22, 0.18)
    return jnp.clip(values, -reach, reach).astype(held_as)


def setup_inputs(seed: int = 0) -> dict:
    arg_keys = jax.random.split(jax.random.key(seed), 14)
    return {
        "inputs": bell_draw(arg_keys[0], (ROWS, LEN, D), 1.0, 6.0, ((0, 8), (1, 4))),
        "segment_ids": draw_segment_ids(jax.random.fold_in(arg_keys[13], 71), 0),
        "gain_one": jnp.clip(1.0 + 0.18 * jax.random.normal(arg_keys[2], (D,), jnp.float32), 0.1, 1.9),
        "w_query": bell_draw(arg_keys[3], (D, D), (D // 4) ** -0.5, 0.4375),
        "w_key": bell_draw(arg_keys[4], (D, D), D ** -0.5, 0.21875),
        "w_value": bell_draw(arg_keys[5], (D, D), D ** -0.5, 0.21875),
        "w_out": bell_draw(arg_keys[6], (D, D), (D // 16) ** -0.5, 0.875),
        "mix_logits": bell_draw(arg_keys[7], (H, H), H ** -0.5, 1.75),
        "mix_weights": bell_draw(arg_keys[8], (H, H), H ** -0.5, 1.75),
        "gain_two": jnp.clip(1.0 + 0.18 * jax.random.normal(arg_keys[9], (D,), jnp.float32), 0.1, 1.9),
        "w_hidden": bell_draw(arg_keys[10], (D, FF), D ** -0.5, 0.21875),
        "w_back": bell_draw(arg_keys[11], (FF, D), (FF // 2) ** -0.5, 0.15625),
        "cotangent": bell_draw(arg_keys[12], (ROWS, LEN, D), 1.0, 6.0, ((0, 8), (1, 4))),
    }


epsilon = 1e-06
highest = lax.Precision.HIGHEST

@jax.custom_vjp
def low(v):
    return lax.optimization_barrier(v.astype(jnp.bfloat16)).astype(jnp.float32)

@jax.custom_vjp
def low_back(v):
    return v

def low_keep(v):
    return (low(v), None)

def low_pass(kept, grad):
    return (grad,)

def back_keep(v):
    return (v, None)

def back_low(kept, grad):
    return (low(grad),)
low.defvjp(low_keep, low_pass)
low_back.defvjp(back_keep, back_low)

def rounded_both(value):
    return low(low_back(value))

def matmul(left, right):
    return jnp.matmul(left, right, precision=highest)

def rms_norm(values, gain):
    return values * lax.rsqrt(lax.optimization_barrier(jnp.mean(values * values, axis=-1, keepdims=True)) + epsilon) * gain

def attend_row(queries, keys_row, values_row, row_ids, mix_logits, mix_weights):
    score_scale = DH ** (-0.5)
    key_heads = keys_row.reshape(LEN, H, DH)
    value_heads = values_row.reshape(LEN, H, DH)
    positions = jnp.arange(LEN, dtype=jnp.int32)

    def one_block(offset):
        query_block = lax.dynamic_slice_in_dim(queries, offset, QBLOCK, 0).reshape(QBLOCK, H, DH)
        block_ids = lax.dynamic_slice_in_dim(row_ids, offset, QBLOCK, 0)
        block_pos = offset + jnp.arange(QBLOCK, dtype=jnp.int32)
        scores = rounded_both(jnp.einsum('qhd,khd->hqk', query_block, key_heads, precision=highest) * score_scale)
        logits = low_back(jnp.einsum('hqk,hj->jqk', scores, mix_logits, precision=highest))
        allowed = (block_pos[:, None] >= positions[None, :]) & (block_ids[:, None] == row_ids[None, :])
        logits = jnp.where(allowed[None], logits, -1e+30)
        shifted = jnp.exp(logits - lax.optimization_barrier(jnp.max(logits, axis=-1, keepdims=True)))
        softmax = shifted / lax.optimization_barrier(jnp.sum(shifted, axis=-1, keepdims=True))
        soft_low = low(softmax)
        blended = rounded_both(jnp.einsum('jqk,ji->iqk', soft_low, mix_weights, precision=highest))
        return jnp.einsum('iqk,kid->qid', blended, value_heads, precision=highest).reshape(QBLOCK, D)
    offsets = jnp.arange(LEN // QBLOCK, dtype=jnp.int32) * QBLOCK
    return lax.map(jax.checkpoint(one_block), offsets).reshape(LEN, D)

def forward(params, inputs_f, segment_ids):
    gain_one, w_query, w_key, w_value, w_out, mix_logits, mix_weights, gain_two, w_hidden, w_back = params

    def group(packed):
        group_in, group_ids = packed
        normed = low(rms_norm(group_in, gain_one))
        queries = rounded_both(matmul(normed, w_query))
        keys_all = rounded_both(matmul(normed, w_key))
        values_all = rounded_both(matmul(normed, w_value))

        def one_row(row_pack):
            return attend_row(row_pack[0], row_pack[1], row_pack[2], row_pack[3], mix_logits, mix_weights)
        attended = rounded_both(lax.map(one_row, (queries, keys_all, values_all, group_ids)))
        attn_out = low_back(matmul(attended, w_out))
        middle = group_in + attn_out
        normed_two = low(rms_norm(middle, gain_two))
        hidden = low_back(matmul(normed_two, w_hidden))
        activated = low(jax.nn.gelu(hidden, approximate=True))
        return middle + low_back(matmul(activated, w_back))
    groups = ROWS // ROWS_DEV
    result = lax.map(jax.checkpoint(group), (inputs_f.reshape(groups, ROWS_DEV, LEN, D), segment_ids.reshape(groups, ROWS_DEV, LEN)))
    return result.reshape(ROWS, LEN, D)

def reference(inputs, segment_ids, gain_one, w_query, w_key, w_value, w_out, mix_logits, mix_weights, gain_two, w_hidden, w_back, cotangent):
    params = tuple((argument.astype(jnp.float32) for argument in (gain_one, w_query, w_key, w_value, w_out, mix_logits, mix_weights, gain_two, w_hidden, w_back)))
    inputs_f = inputs.astype(jnp.float32)

    def whole(weights_in, values_in):
        return forward(weights_in, values_in, segment_ids)
    output, pullback = jax.vjp(whole, params, inputs_f)
    weight_grads, grad_in = pullback(cotangent.astype(jnp.float32))
    return (output.astype(jnp.bfloat16), grad_in.astype(jnp.bfloat16), weight_grads[0], weight_grads[1], weight_grads[2], weight_grads[3], weight_grads[4], weight_grads[5], weight_grads[6], weight_grads[7], weight_grads[8], weight_grads[9])
```

```python
from functools import partial

import jax
import jax.numpy as jnp
from jax import lax
from jax.experimental import pallas as pl
from jax.experimental.pallas import tpu as pltpu
from jax.sharding import PartitionSpec as P

D, H, DH, LEN, TILE = 768, 12, 64, 1024, 256
TILES = LEN // TILE
F32, BF16 = jnp.float32, jnp.bfloat16
HEADS_PER_STEP = 1
VMEM_LIMIT = 60 * 1024 * 1024


def span(i):
    return slice(i * TILE, (i + 1) * TILE)


def head_rows(h):
    return slice(h * DH, (h + 1) * DH)


def mm(a, b):
    return jnp.dot(a, b, preferred_element_type=F32)


def scale_rows(dst, src, weights, pick):
    for h in range(H):
        w = pick(weights, h)
        dst[head_rows(h), :] = (src[head_rows(h), :].astype(F32) * w).astype(BF16)


def soft_kernel(mix, id_row, id_col, q_t, k, soft, bias, scaled):
    j = pl.program_id(0)

    @pl.when(j == 0)
    def build_bias():
        for t in range(TILES):
            for u in range(t + 1):
                allowed = id_col[span(u), :] == id_row[:, span(t)]
                if u == t:
                    key = lax.broadcasted_iota(jnp.int32, (TILE, TILE), 0)
                    query = lax.broadcasted_iota(jnp.int32, (TILE, TILE), 1)
                    allowed = allowed & (key <= query)
                bias[span(u), span(t)] = jnp.where(allowed, 0.0, -1e30)

    scale_rows(scaled, q_t, mix, lambda w, h: w[h, j])
    for t in range(TILES):
        n = (t + 1) * TILE
        logits = mm(k[:n, :], scaled[:, span(t)]) + bias[:n, span(t)]
        top = jnp.max(logits, axis=0, keepdims=True)
        e = jnp.exp(logits - top)
        inv = 1.0 / jnp.sum(e, axis=0, keepdims=True)
        soft[0, :n, span(t)] = (e * inv).astype(BF16)


def attend_kernel(mix, soft, v_t, out, acc):
    j = pl.program_id(0)

    @pl.when(j == 0)
    def zero():
        acc[...] = jnp.zeros_like(acc)

    for t in range(TILES):
        n = (t + 1) * TILE
        part = mm(v_t[:, :n], soft[0, :n, span(t)])
        for h in range(H):
            acc[head_rows(h), span(t)] += part[head_rows(h), :] * mix[j, h]

    @pl.when(j == H - 1)
    def finish():
        for t in range(TILES):
            out[span(t), :] = acc[:, span(t)].T.astype(BF16)


def values_kernel(mix_row, soft, v, g, out, mix_grad, acc):
    j = pl.program_id(0)

    @pl.when(j == 0)
    def zero():
        acc[...] = jnp.zeros_like(acc)

    w = mix_row[0]
    total = jnp.zeros((1, D), F32)
    for u in range(TILES):
        part = mm(soft[0, span(u), u * TILE:], g[u * TILE:, :])
        acc[span(u), :] += part * w
        total = total + jnp.sum(part * v[span(u), :].astype(F32), axis=0, keepdims=True)
    mix_grad[0] = total

    @pl.when(j == H - 1)
    def finish():
        out[...] = acc[...].astype(BF16)


def queries_kernel(mix_w, mix_l, soft, v, g_t, k_t, q_t, out, grad_logits, mix_grad, acc, scaled):
    j = pl.program_id(0)

    @pl.when(j == 0)
    def zero():
        acc[...] = jnp.zeros_like(acc)

    scale_rows(scaled, g_t, mix_w, lambda w, h: w[j, h])
    total = jnp.zeros((D, 128), F32)
    for t in range(TILES):
        n = (t + 1) * TILE
        grad_soft = mm(v[:n, :], scaled[:, span(t)])
        p = soft[0, :n, span(t)].astype(F32)
        weighted = p * grad_soft
        dots = jnp.sum(weighted, axis=0, keepdims=True)
        gl = (weighted - p * dots).astype(BF16)
        grad_logits[0, :n, span(t)] = gl
        part = mm(k_t[:, :n], gl)
        for h in range(H):
            acc[head_rows(h), span(t)] += part[head_rows(h), :] * mix_l[h, j]
        prod = part * q_t[:, span(t)].astype(F32)
        total = total + prod[:, :128] + prod[:, 128:]
    mix_grad[0] = jnp.sum(total, axis=1, keepdims=True)

    @pl.when(j == H - 1)
    def finish():
        for t in range(TILES):
            out[span(t), :] = acc[:, span(t)].T.astype(BF16)


def keys_kernel(mix_row, grad_logits, q, out, acc):
    j = pl.program_id(0)

    @pl.when(j == 0)
    def zero():
        acc[...] = jnp.zeros_like(acc)

    w = mix_row[0]
    for u in range(TILES):
        acc[span(u), :] += mm(grad_logits[0, span(u), u * TILE:], q[u * TILE:, :]) * w

    @pl.when(j == H - 1)
    def finish():
        out[...] = acc[...].astype(BF16)


def whole(shape):
    return pl.BlockSpec(shape, lambda j: (0,) * len(shape), pipeline_mode=pl.Buffered(1))


def per_head(shape):
    return pl.BlockSpec((1,) + shape, lambda j: (j,) + (0,) * len(shape))


SMEM = pl.BlockSpec(memory_space=pltpu.SMEM)


def params():
    return pltpu.CompilerParams(dimension_semantics=("arbitrary",), vmem_limit_bytes=VMEM_LIMIT)


def call(kernel, in_specs, out_specs, out_shape, scratch, name):
    return pl.pallas_call(
        kernel, grid=(H,), in_specs=in_specs, out_specs=out_specs, out_shape=out_shape,
        scratch_shapes=scratch, compiler_params=params(), name=name)


def shape(s, t=BF16):
    return jax.ShapeDtypeStruct(s, t)


def softmaxes(mix, ids, q_t, k):
    return call(
        soft_kernel,
        [SMEM, whole((1, LEN)), whole((LEN, 1)), whole((D, LEN)), whole((LEN, D))],
        per_head((LEN, LEN)), shape((H, LEN, LEN)),
        [pltpu.VMEM((LEN, LEN), F32), pltpu.VMEM((D, LEN), BF16)], "softmaxes",
    )(mix, ids.reshape(1, LEN), ids.reshape(LEN, 1), q_t, k)


def attend(mix, soft, v_t):
    return call(
        attend_kernel, [SMEM, per_head((LEN, LEN)), whole((D, LEN))], whole((LEN, D)), shape((LEN, D)),
        [pltpu.VMEM((D, LEN), F32)], "attend")(mix, soft, v_t)


def value_grads(mix_rows, soft, v, g):
    return call(
        values_kernel, [per_head((1, D)), per_head((LEN, LEN)), whole((LEN, D)), whole((LEN, D))],
        [whole((LEN, D)), per_head((1, D))], [shape((LEN, D)), shape((H, 1, D), F32)],
        [pltpu.VMEM((LEN, D), F32)], "value_grads")(mix_rows, soft, v, g)


def query_grads(mix_w, mix_l, soft, v, g_t, k_t, q_t):
    return call(
        queries_kernel,
        [SMEM, SMEM, per_head((LEN, LEN)), whole((LEN, D)), whole((D, LEN)), whole((D, LEN)), whole((D, LEN))],
        [whole((LEN, D)), per_head((LEN, LEN)), per_head((D, 1))],
        [shape((LEN, D)), shape((H, LEN, LEN)), shape((H, D, 1), F32)],
        [pltpu.VMEM((D, LEN), F32), pltpu.VMEM((D, LEN), BF16)], "query_grads",
    )(mix_w, mix_l, soft, v, g_t, k_t, q_t)


def key_grads(mix_rows, grad_logits, q):
    return call(
        keys_kernel, [per_head((1, D)), per_head((LEN, LEN)), whole((LEN, D))], whole((LEN, D)), shape((LEN, D)),
        [pltpu.VMEM((LEN, D), F32)], "key_grads")(mix_rows, grad_logits, q)


epsilon = 1e-06


def cross_rows(left, right):
    return lax.dot_general(left, right, (((0,), (0,)), ((), ())), preferred_element_type=F32)


def against(left, right):
    return lax.dot_general(left, right, (((1,), (1,)), ((), ())), preferred_element_type=F32)


def norm_parts(values, gain):
    inverse = lax.rsqrt(jnp.mean(values * values, axis=-1, keepdims=True) + epsilon)
    return (values * inverse * gain, inverse)


def norm_back(values, inverse, gain, upstream):
    weighted = upstream * gain
    grad_gain = jnp.sum(upstream * values * inverse, axis=0)
    grad_values = inverse * weighted - values * inverse * inverse * inverse * jnp.mean(
        weighted * values, axis=-1, keepdims=True
    )
    return (grad_values, grad_gain)


def to_rows(values):
    return lax.all_to_all(values, "seq", split_axis=0, concat_axis=1, tiled=True).reshape(LEN, D)


def to_tokens(values):
    return lax.all_to_all(values.reshape(1, LEN, D), "seq", split_axis=1, concat_axis=0, tiled=True)


def per_device(
    inputs,
    segment_ids,
    gain_one,
    w_query,
    w_key,
    w_value,
    w_out,
    mix_logits,
    mix_weights,
    gain_two,
    w_hidden,
    w_back,
    cotangent,
):
    ids = lax.dynamic_slice_in_dim(segment_ids, lax.axis_index("seq"), 1, 0)
    x_row = to_rows(inputs)
    cot = to_rows(cotangent)
    x = x_row.astype(F32)
    normed_f, inverse_one = norm_parts(x, gain_one)
    normed = normed_f.astype(BF16)
    q = mm(normed, w_query).astype(BF16)
    k = mm(normed, w_key).astype(BF16)
    v = mm(normed, w_value).astype(BF16)
    scale = DH ** -0.5
    ml = mix_logits.astype(F32) * scale
    mw = mix_weights.astype(F32)
    ml_rows = jnp.repeat(ml.T, DH, axis=1)[:, None, :]
    mw_rows = jnp.repeat(mw, DH, axis=1)[:, None, :]
    q_t = q.T
    soft = softmaxes(ml, ids, q_t, k)
    attended = attend(mw, soft, v.T)
    middle = x + mm(attended, w_out)
    normed_two_f, inverse_two = norm_parts(middle, gain_two)
    normed_two = normed_two_f.astype(BF16)
    hidden = mm(normed_two, w_hidden)
    activated = jax.nn.gelu(hidden, approximate=True).astype(BF16)
    block_out = to_tokens((middle + mm(activated, w_back)).astype(BF16))
    grad_w_back = cross_rows(activated, cot)
    grad_act = against(cot, w_back)
    unused, gelu_pull = jax.vjp(partial(jax.nn.gelu, approximate=True), hidden)
    grad_hidden = gelu_pull(grad_act)[0].astype(BF16)
    grad_w_hidden = cross_rows(normed_two, grad_hidden)
    grad_n2 = against(grad_hidden, w_hidden)
    grad_middle_norm, grad_gain_two = norm_back(middle, inverse_two, gain_two, grad_n2)
    grad_middle = cot.astype(F32) + grad_middle_norm
    grad_attn = grad_middle.astype(BF16)
    grad_w_out = cross_rows(attended, grad_attn)
    grad_attended = against(grad_attn, w_out).astype(BF16)
    gv, mw_parts = value_grads(mw_rows, soft, v, grad_attended)
    gq, grad_logits, ml_parts = query_grads(mw, ml, soft, v, grad_attended.T, k.T, q_t)
    gk = key_grads(ml_rows, grad_logits, q)
    grad_mix_weights = mw_parts.reshape(H, H, DH).sum(-1)
    grad_mix_logits = ml_parts.reshape(H, H, DH).sum(-1).T * scale
    grad_w_query = cross_rows(normed, gq)
    grad_w_key = cross_rows(normed, gk)
    grad_w_value = cross_rows(normed, gv)
    grad_normed = against(gq, w_query) + against(gk, w_key) + against(gv, w_value)
    grad_in_norm, grad_gain_one = norm_back(x, inverse_one, gain_one, grad_normed)
    grad_inputs = to_tokens((grad_middle + grad_in_norm).astype(BF16))
    grads = lax.psum(
        (
            grad_gain_one,
            grad_w_query,
            grad_w_key,
            grad_w_value,
            grad_w_out,
            grad_mix_logits,
            grad_mix_weights,
            grad_gain_two,
            grad_w_hidden,
            grad_w_back,
        ),
        ("rows", "seq"),
    )
    return (block_out, grad_inputs) + tuple(grads)


def solution(mesh):
    sharded, copied = P("rows", "seq", None), P()
    in_specs = (sharded, P("rows", None)) + (copied,) * 10 + (sharded,)
    out_specs = (sharded, sharded) + (copied,) * 10
    return jax.shard_map(
        per_device, mesh=mesh, in_specs=in_specs, out_specs=out_specs, check_vma=False
    )
```

```python
from functools import partial

from jax import lax
import jax
import jax.numpy as jnp
from jax.experimental import pallas as pl
from jax.experimental.pallas import tpu as pltpu
from jax.sharding import PartitionSpec as P

D, H, DH, LEN, TILE = 768, 12, 64, 1024, 256
TILES = LEN // TILE
F32, BF16 = jnp.float32, jnp.bfloat16
FORWARD_HEADS, BACKWARD_HEADS = 4, 2
VMEM_LIMIT = 60 * 1024 * 1024
MATMUL_FLOPS = 2 * H * 10 * TILE * TILE * D


def span(i):
    return slice(i * TILE, (i + 1) * TILE)


def head_rows(h):
    return slice(h * DH, (h + 1) * DH)


def mm(a, b):
    return jnp.dot(a, b, preferred_element_type=F32)


def whole(shape):
    return pl.BlockSpec(shape, lambda i: (0,) * len(shape), pipeline_mode=pl.Buffered(1))


def some_heads(count, shape):
    return pl.BlockSpec((count,) + shape, lambda i: (i,) + (0,) * len(shape))


SMEM = pl.BlockSpec(memory_space=pltpu.SMEM)


def params():
    return pltpu.CompilerParams(dimension_semantics=("arbitrary",), vmem_limit_bytes=VMEM_LIMIT)


def shape(s, t=BF16):
    return jax.ShapeDtypeStruct(s, t)


def attend_kernel(mix_l, mix_w, id_row, id_col, q_t, k, v_t, soft, out, bias, scaled, acc):
    step = pl.program_id(0)

    @pl.when(step == 0)
    def start():
        acc[...] = jnp.zeros_like(acc)
        for t in range(TILES):
            for u in range(t + 1):
                allowed = id_col[span(u), :] == id_row[:, span(t)]
                if u == t:
                    key = lax.broadcasted_iota(jnp.int32, (TILE, TILE), 0)
                    query = lax.broadcasted_iota(jnp.int32, (TILE, TILE), 1)
                    allowed = allowed & (key <= query)
                bias[span(u), span(t)] = jnp.where(allowed, 0.0, -1e30)

    for i in range(FORWARD_HEADS):
        j = step * FORWARD_HEADS + i
        for h in range(H):
            scaled[i, head_rows(h), :] = (q_t[head_rows(h), :].astype(F32) * mix_l[h, j]).astype(BF16)
        for t in reversed(range(TILES)):
            n = (t + 1) * TILE
            logits = mm(k[:n, :], scaled[i, :, span(t)]) + bias[:n, span(t)]
            e = jnp.exp(logits - jnp.max(logits, axis=0, keepdims=True))
            p = (e * (1.0 / jnp.sum(e, axis=0, keepdims=True))).astype(BF16)
            soft[i, :n, span(t)] = p
            part = mm(v_t[:, :n], p)
            for h in range(H):
                acc[head_rows(h), span(t)] += part[head_rows(h), :] * mix_w[j, h]

    @pl.when(step == H // FORWARD_HEADS - 1)
    def finish():
        for t in range(TILES):
            out[span(t), :] = acc[:, span(t)].T.astype(BF16)


def attend(mix_l, mix_w, ids, q_t, k, v_t):
    heads = FORWARD_HEADS
    return pl.pallas_call(
        attend_kernel,
        grid=(H // heads,),
        in_specs=[SMEM, SMEM, whole((1, LEN)), whole((LEN, 1)), whole((D, LEN)), whole((LEN, D)), whole((D, LEN))],
        out_specs=[some_heads(heads, (LEN, LEN)), whole((LEN, D))],
        out_shape=[shape((H, LEN, LEN)), shape((LEN, D))],
        scratch_shapes=[
            pltpu.VMEM((LEN, LEN), F32), pltpu.VMEM((heads, D, LEN), BF16), pltpu.VMEM((D, LEN), F32)
        ],
        compiler_params=params(),
        cost_estimate=pl.CostEstimate(flops=2 * MATMUL_FLOPS, bytes_accessed=2 * H * LEN * LEN, transcendentals=0),
        name="attend",
    )(mix_l, mix_w, ids.reshape(1, LEN), ids.reshape(LEN, 1), q_t, k, v_t)


def value_grads_kernel(mix_row, soft, v, g, *rest):
    out, mix_grad, acc = rest[-3:]
    step = pl.program_id(0)

    @pl.when(step == 0)
    def start():
        acc[...] = jnp.zeros_like(acc)

    for i in range(BACKWARD_HEADS):
        total = jnp.zeros((1, D), F32)
        for u in range(TILES):
            part = mm(soft[i, span(u), u * TILE :], g[u * TILE :, :])
            acc[span(u), :] += part * mix_row[i]
            total = total + jnp.sum(part * v[span(u), :].astype(F32), axis=0, keepdims=True)
        mix_grad[i] = total

    @pl.when(step == H // BACKWARD_HEADS - 1)
    def finish():
        out[...] = acc[...].astype(BF16)


def query_grads_kernel(heads, mix_w, mix_l, soft, v, g_t, k_t, q_t, *rest):
    before, (out, grad_logits, mix_grad, acc, scaled) = rest[0], rest[-5:]
    step = pl.program_id(0)
    first_head = heads[0] + step * BACKWARD_HEADS

    @pl.when(step == 0)
    def start():
        acc[...] = before[...] if heads[0] else jnp.zeros_like(acc)

    for i in range(BACKWARD_HEADS):
        j = first_head + i
        for h in range(H):
            scaled[i, head_rows(h), :] = (g_t[head_rows(h), :].astype(F32) * mix_w[j, h]).astype(BF16)
    order = [(i, t) for i in range(BACKWARD_HEADS) for t in reversed(range(TILES))]

    def grad_soft(i, t):
        return mm(v[: (t + 1) * TILE, :], scaled[i, :, span(t)])

    coming = grad_soft(*order[0])
    total = jnp.zeros((D, 128), F32)
    for at, (i, t) in enumerate(order):
        n = (t + 1) * TILE
        p = soft[i, :n, span(t)].astype(F32)
        weighted = p * coming
        low = (weighted - p * jnp.sum(weighted, axis=0, keepdims=True)).astype(BF16)
        grad_logits[i, :n, span(t)] = low
        if at + 1 < len(order):
            coming = grad_soft(*order[at + 1])
        part = mm(k_t[:, :n], low)
        for h in range(H):
            acc[head_rows(h), span(t)] += part[head_rows(h), :] * mix_l[h, first_head + i]
        product = part * q_t[:, span(t)].astype(F32)
        total = total + product[:, :128] + product[:, 128:]
        if t == 0:
            mix_grad[i] = jnp.sum(total.T, axis=0, keepdims=True)
            total = jnp.zeros((D, 128), F32)

    @pl.when(step == pl.num_programs(0) - 1)
    def finish():
        if heads[1] < H:
            out[...] = acc[...]
        else:
            for t in range(TILES):
                out[span(t), :] = acc[:, span(t)].T.astype(BF16)


def key_grads_kernel(mix_row, grad_logits, q, *rest):
    out, acc = rest[-2:]
    step = pl.program_id(0)

    @pl.when(step == 0)
    def start():
        acc[...] = jnp.zeros_like(acc)

    for i in range(BACKWARD_HEADS):
        for u in range(TILES):
            acc[span(u), :] += mm(grad_logits[i, span(u), u * TILE :], q[u * TILE :, :]) * mix_row[i]

    @pl.when(step == H // BACKWARD_HEADS - 1)
    def finish():
        out[...] = acc[...].astype(BF16)


def back_call(kernel, heads, in_specs, out_specs, out_shape, scratch, matmuls, name):
    def run(*operands):
        *used, first = operands
        return pl.pallas_call(
            kernel,
            grid=(heads // BACKWARD_HEADS,),
            in_specs=in_specs + [pl.BlockSpec(memory_space=pl.ANY)] * len(first),
            out_specs=out_specs,
            out_shape=out_shape,
            scratch_shapes=scratch,
            compiler_params=params(),
            cost_estimate=pl.CostEstimate(
                flops=matmuls * MATMUL_FLOPS * heads // H, bytes_accessed=2 * heads * LEN * LEN, transcendentals=0
            ),
            name=name,
        )(*used, *first)

    return run


ROW, COLUMN = whole((LEN, D)), whole((D, LEN))
PER_HEAD, PER_HEAD_ROW = some_heads(BACKWARD_HEADS, (LEN, LEN)), some_heads(BACKWARD_HEADS, (1, D))


def value_grads(mix_w, soft, v, g, first):
    mix_row = jnp.repeat(mix_w, DH, axis=1)[:, None, :]
    grads, mix_grad = back_call(
        value_grads_kernel,
        H,
        [PER_HEAD_ROW, PER_HEAD, ROW, ROW],
        [ROW, PER_HEAD_ROW],
        [shape((LEN, D)), shape((H, 1, D), F32)],
        [pltpu.VMEM((LEN, D), F32)],
        1,
        "value_grads",
    )(mix_row, soft, v, g, first)
    return grads, mix_grad.reshape(H, H, DH).sum(-1)


def query_grads(mix_w, mix_l, soft, v, g_t, k_t, q_t, first, heads=(0, H), before=()):
    low, high = heads
    count, last = high - low, high == H
    per_head = pl.BlockSpec((BACKWARD_HEADS, LEN, LEN), lambda i: (i + low // BACKWARD_HEADS, 0, 0))
    grads, grad_logits, mix_grad = back_call(
        partial(query_grads_kernel, heads),
        count,
        [SMEM, SMEM, per_head, ROW, COLUMN, COLUMN, COLUMN] + [COLUMN] * len(before),
        [ROW if last else COLUMN, PER_HEAD, PER_HEAD_ROW],
        [shape((LEN, D)) if last else shape((D, LEN), F32), shape((count, LEN, LEN)), shape((count, 1, D), F32)],
        [pltpu.VMEM((D, LEN), F32), pltpu.VMEM((BACKWARD_HEADS, D, LEN), BF16)],
        2,
        "query_grads",
    )(mix_w, mix_l, soft, v, g_t, k_t, q_t, *before, first)
    return grads, grad_logits, mix_grad


def key_grads(mix_l, grad_logits, q, first):
    mix_row = jnp.repeat(mix_l.T, DH, axis=1)[:, None, :]
    return back_call(
        key_grads_kernel, H, [PER_HEAD_ROW, PER_HEAD, ROW], ROW, shape((LEN, D)), [pltpu.VMEM((LEN, D), F32)], 1,
        "key_grads",
    )(mix_row, grad_logits, q, first)


epsilon = 1e-06
GELU_SCALE = 0.7978845608028654
GELU_CUBIC = 0.044715


def against(left, right):
    return lax.dot_general(left, right, (((1,), (1,)), ((), ())), preferred_element_type=F32)


def inverse_rms(values):
    return lax.rsqrt(jnp.mean(values * values, axis=-1, keepdims=True) + epsilon)


def project_kernel(x, gain, w_query, w_key, w_value, normed_t, q, q_t, k, k_t, v, v_t):
    values = x[...].astype(F32)
    normed = (values * inverse_rms(values) * gain[...]).astype(BF16)
    normed_t[...] = normed.T
    for weight, out, out_t in ((w_query, q, q_t), (w_key, k, k_t), (w_value, v, v_t)):
        part = mm(normed, weight[...]).astype(BF16)
        out[...] = part
        out_t[...] = part.T


def feed_kernel(
    x, attended, cot, w_out, w_hidden, w_back, gain,
    out, normed_two, activated, grad_hidden, grad_middle, grad_attn, g, g_t, gain_grad,
):
    i = pl.program_id(0)

    @pl.when(i == 0)
    def zero():
        gain_grad[...] = jnp.zeros_like(gain_grad)

    scale = gain[...]
    middle = x[...].astype(F32) + mm(attended[...], w_out[...])
    inverse = inverse_rms(middle)
    n2 = (middle * inverse * scale).astype(BF16)
    normed_two[...] = n2
    cotangent = cot[...]
    total = middle
    grad_n2 = jnp.zeros_like(middle)
    width = FEED_COLUMNS
    for c in range(w_hidden.shape[1] // width):
        cols = slice(c * width, (c + 1) * width)
        hidden = mm(n2, w_hidden[:, cols])
        grad_act = against(cotangent, w_back[cols, :])
        squared = hidden * hidden
        tanh = jnp.tanh(GELU_SCALE * hidden * (1.0 + GELU_CUBIC * squared))
        half = 0.5 + 0.5 * tanh
        act = (hidden * half).astype(BF16)
        activated[:, cols] = act
        slope = half + (0.5 * GELU_SCALE) * hidden * (1.0 - tanh * tanh) * (1.0 + 3.0 * GELU_CUBIC * squared)
        grad = (grad_act * slope).astype(BF16)
        grad_hidden[:, cols] = grad
        total = total + mm(act, w_back[cols, :])
        grad_n2 = grad_n2 + against(grad, w_hidden[:, cols])
    out[...] = total.astype(BF16)
    gain_grad[...] += jnp.sum(grad_n2 * middle * inverse, axis=0, keepdims=True)
    weighted = grad_n2 * scale
    mean = jnp.mean(weighted * middle, axis=-1, keepdims=True)
    grad_mid = cotangent.astype(F32) + inverse * weighted - middle * (inverse * inverse * inverse * mean)
    grad_middle[...] = grad_mid
    grad_low = grad_mid.astype(BF16)
    grad_attn[...] = grad_low
    grad = against(grad_low, w_out[...]).astype(BF16)
    g[...] = grad
    g_t[...] = grad.T


FEED_COLUMNS = 1024
TOKEN_TILE = 256


def token_tile(columns):
    return pl.BlockSpec((TOKEN_TILE, columns), lambda i: (i, 0))


def token_tile_t(rows):
    return pl.BlockSpec((rows, TOKEN_TILE), lambda i: (0, i))


def token_call(kernel, in_specs, out_specs, out_shape, flops, name):
    return pl.pallas_call(
        kernel, grid=(LEN // TOKEN_TILE,), in_specs=in_specs, out_specs=out_specs, out_shape=out_shape,
        compiler_params=params(), cost_estimate=pl.CostEstimate(flops=flops, bytes_accessed=16 * LEN * D, transcendentals=0),
        name=name)


def project(x, gain, w_query, w_key, w_value):
    square = whole((D, D))
    return token_call(
        project_kernel, [token_tile(D), whole((1, D)), square, square, square],
        [token_tile_t(D)] + [token_tile(D), token_tile_t(D)] * 3,
        [shape((D, LEN))] + [shape((LEN, D)), shape((D, LEN))] * 3,
        6 * LEN * D * D, "project")(x, gain.reshape(1, D), w_query, w_key, w_value)


def feed(x, attended, cot, w_out, w_hidden, w_back, gain):
    ff = w_hidden.shape[1]
    return token_call(
        feed_kernel,
        [token_tile(D)] * 3 + [whole((D, D)), whole((D, ff)), whole((ff, D)), whole((1, D))],
        [token_tile(D), token_tile(D), token_tile(ff), token_tile(ff), token_tile(D), token_tile(D), token_tile(D), token_tile_t(D), whole((1, D))],
        [shape((LEN, D)), shape((LEN, D)), shape((LEN, ff)), shape((LEN, ff)), shape((LEN, D), F32), shape((LEN, D)), shape((LEN, D)), shape((D, LEN)), shape((1, D), F32)],
        4 * LEN * D * D + 8 * LEN * D * ff, "feed")(x, attended, cot, w_out, w_hidden, w_back, gain.reshape(1, D))


def input_kernel(grad_q, grad_k, grad_v, x, grad_middle, w_query, w_key, w_value, gain, out, gain_grad):
    i = pl.program_id(0)

    @pl.when(i == 0)
    def zero():
        gain_grad[...] = jnp.zeros_like(gain_grad)

    upstream = against(grad_q[...], w_query[...]) + against(grad_k[...], w_key[...]) + against(grad_v[...], w_value[...])
    values = x[...].astype(F32)
    inverse = inverse_rms(values)
    gain_grad[...] += jnp.sum(upstream * values * inverse, axis=0, keepdims=True)
    weighted = upstream * gain[...]
    mean = jnp.mean(weighted * values, axis=-1, keepdims=True)
    out[...] = (grad_middle[...] + inverse * weighted - values * (inverse * inverse * inverse * mean)).astype(BF16)


def input_grads(grad_q, grad_k, grad_v, x, grad_middle, w_query, w_key, w_value, gain):
    square = whole((D, D))
    return token_call(
        input_kernel, [token_tile(D)] * 5 + [square, square, square, whole((1, D))],
        [token_tile(D), whole((1, D))], [shape((LEN, D)), shape((1, D), F32)],
        6 * LEN * D * D, "input_grads")(
            grad_q, grad_k, grad_v, x, grad_middle, w_query, w_key, w_value, gain.reshape(1, D))


HALF = D // 2


def keep_half(core, product, kept, sent):
    kept[0] = product[pl.ds(pl.multiple_of(core[0] * HALF, HALF), HALF), :].astype(BF16)
    sent[0] = product[pl.ds(pl.multiple_of((1 - core[0]) * HALF, HALF), HALF), :].astype(BF16)


def across(left, right):
    return lax.dot_general(left, right, (((0,), (0,)), ((), ())), preferred_element_type=F32)


def back_weights_kernel(core, activated, cot, kept, sent, product):
    product[...] = across(activated[...], cot[...])
    keep_half(core, product, kept, sent)


def hidden_weights_kernel(core, normed_two, grad_hidden, attended, grad_attn, first, kept, sent, product):
    last = pl.program_id(0) == pl.num_programs(0) - 1

    @pl.when(jnp.logical_not(last))
    def hidden():
        product[...] = across(normed_two[...], grad_hidden[...])

    @pl.when(last)
    def out():
        product[...] = across(attended[...], grad_attn[...])

    keep_half(core, product, kept, sent)


def half_call(kernel, core, steps, in_specs, operands, flops, name):
    block = pl.BlockSpec((1, HALF, D), lambda i, core: (i, 0, 0))
    return pl.pallas_call(
        kernel,
        grid_spec=pltpu.PrefetchScalarGridSpec(
            num_scalar_prefetch=1, grid=(steps,), in_specs=in_specs, out_specs=[block, block],
            scratch_shapes=[pltpu.VMEM((D, D), F32)]),
        out_shape=[shape((steps, HALF, D))] * 2,
        compiler_params=params(),
        cost_estimate=pl.CostEstimate(flops=flops, bytes_accessed=16 * LEN * D, transcendentals=0),
        name=name,
    )(core, *operands)


def fixed(s):
    return pl.BlockSpec(s, lambda i, core: (0, 0), pipeline_mode=pl.Buffered(1))


def back_weight_grads(core, activated, cot):
    blocks = activated.shape[1] // D
    return half_call(
        back_weights_kernel, core, blocks, [pl.BlockSpec((LEN, D), lambda i, core: (0, i)), fixed((LEN, D))],
        (activated, cot), 2 * blocks * LEN * D * D, "back_weight_grads")


def hidden_weight_grads(core, normed_two, grad_hidden, attended, grad_attn, first):
    blocks = grad_hidden.shape[1] // D
    row = fixed((LEN, D))
    return half_call(
        hidden_weights_kernel, core, blocks + 1,
        [row, pl.BlockSpec((LEN, D), lambda i, core: (0, jnp.minimum(i, blocks - 1))), row, row,
         pl.BlockSpec(memory_space=pl.ANY)],
        (normed_two, grad_hidden, attended, grad_attn, first), 2 * (blocks + 1) * LEN * D * D, "hidden_weight_grads")


def project_weights_kernel(core, normed_t, *rest):
    *grads, kept, sent, product = rest
    for i, each in enumerate(grads):

        @pl.when(pl.program_id(0) == i)
        def multiply():
            product[...] = mm(normed_t[...], each[...])

    keep_half(core, product, kept, sent)


def project_weight_grads(core, normed_t, *grads):
    return half_call(
        project_weights_kernel, core, len(grads), [fixed((D, LEN))] + [fixed((LEN, D))] * len(grads),
        (normed_t,) + grads, 2 * len(grads) * LEN * D * D, "project_weight_grads")


def split_kernel(wide_count, mine, *refs):
    (kept_one, came_one, kept_two, came_two), outs, total = refs[:4], refs[4:-1], refs[-1]
    matrix, ones = pl.program_id(0), 4
    wide, thin = outs[: len(outs) // 2], outs[len(outs) // 2 :]
    rows = wide[0].shape[1]

    def add(kept, came):
        total[...] = (kept[0].astype(F32) + came[0].astype(F32)).astype(BF16)

    pl.when(matrix < ones)(partial(add, kept_one, came_one))
    pl.when(matrix >= ones)(partial(add, kept_two, came_two))

    def share(outs, place):
        for c, out in enumerate(outs):
            out[0] = total[pl.ds(pl.multiple_of((place ^ c) * rows, rows), rows), :]

    pl.when(matrix < wide_count)(partial(share, wide, mine[0]))
    pl.when(matrix >= wide_count)(partial(share, thin, mine[1]))


def split(mine, kept_one, came_one, kept_two, came_two, wide_count, ways):
    ones, twos = kept_one.shape[0], kept_two.shape[0]
    thin_count, rows = ones + twos - wide_count, HALF // ways
    one = pl.BlockSpec((1, HALF, D), lambda m, mine: (jnp.minimum(m, ones - 1), 0, 0))
    two = pl.BlockSpec((1, HALF, D), lambda m, mine: (jnp.maximum(m - ones, 0), 0, 0))
    wide = pl.BlockSpec((1, rows, D), lambda m, mine: (jnp.minimum(m, wide_count - 1), 0, 0))
    thin = pl.BlockSpec((1, rows, D), lambda m, mine: (jnp.maximum(m - wide_count, 0), 0, 0))
    outs = pl.pallas_call(
        partial(split_kernel, wide_count),
        grid_spec=pltpu.PrefetchScalarGridSpec(
            num_scalar_prefetch=1, grid=(ones + twos,), in_specs=[one, one, two, two],
            out_specs=[wide] * ways + [thin] * ways, scratch_shapes=[pltpu.VMEM((HALF, D), BF16)]),
        out_shape=[shape((wide_count, rows, D))] * ways + [shape((thin_count, rows, D))] * ways,
        compiler_params=params(),
        name="split",
    )(mine, kept_one, came_one, kept_two, came_two)
    return outs[:ways], outs[ways:]


def combine_kernel(groups, waits, mine, *refs):
    ins, outs = refs[: sum(g[0] for g in groups)], refs[sum(g[0] for g in groups) + waits :]
    for index, (count, ways) in enumerate(groups):
        total = sum(ref[...].astype(F32) for ref in ins[:count])
        whole_sum = outs[-1 - index]
        whole_sum[...] = total
        rows = total.shape[1] // ways
        for c in range(ways):
            start = pl.multiple_of((mine[index] ^ c) * rows, rows) if ways > 1 else 0
            outs[c][...] = whole_sum[:, pl.ds(start, rows), :].astype(BF16)
        ins, outs = ins[count:], outs[ways:]


def combine(mine, parts, ways, first=()):
    shapes = [p[0].shape for p in parts]
    vmem = pl.BlockSpec(memory_space=pltpu.VMEM)
    outs = pl.pallas_call(
        partial(combine_kernel, [(len(p), w) for p, w in zip(parts, ways)], len(first)),
        in_specs=[SMEM] + [vmem] * sum(len(p) for p in parts) + [pl.BlockSpec(memory_space=pl.ANY)] * len(first),
        out_specs=[vmem] * sum(ways),
        out_shape=[shape((s[0], s[1] // w, s[2])) for s, w in zip(shapes, ways) for c in range(w)],
        scratch_shapes=[pltpu.VMEM(s, F32) for s in reversed(shapes)],
        compiler_params=pltpu.CompilerParams(vmem_limit_bytes=VMEM_LIMIT),
        name="combine",
    )(mine, *[x for p in parts for x in p], *first)
    found = []
    for w in ways:
        found.append(outs[:w])
        outs = outs[w:]
    return found


def fill_kernel(counts, wide_count, starts, pieces, *outs):
    matrix, begin, rows = pl.program_id(0), 0, pieces.shape[2]
    for out, count in zip(outs, counts):
        for table, low, high in ((0, begin, min(begin + count, wide_count)), (1, max(begin, wide_count), begin + count)):
            if low < high:

                @pl.when((matrix >= low) & (matrix < high))
                def here():
                    for device, start in enumerate(starts[table]):
                        out[start : start + rows, :] = pieces[device, 0].astype(F32)

        begin += count


def fill(pieces, starts, wide_count, down, over, name):
    counts = [d * o for d, o in zip(down, over)]
    out_specs, out_shape, begin = [], [], 0
    for d, o, count in zip(down, over, counts):

        def place_of(m, begin=begin, count=count, o=o):
            at = jnp.clip(m - begin, 0, count - 1)
            return (at // o, at % o)

        out_specs.append(pl.BlockSpec((D, D), place_of))
        out_shape.append(shape((d * D, o * D), F32))
        begin += count
    devices, matrices, rows, _ = pieces.shape
    return pl.pallas_call(
        partial(fill_kernel, tuple(counts), wide_count, starts),
        grid=(begin,),
        in_specs=[pl.BlockSpec((devices, 1, rows, D), lambda m: (0, m, 0, 0))],
        out_specs=out_specs,
        out_shape=out_shape,
        compiler_params=params(),
        name=name,
    )(pieces)


def spread_kernel(counts, sizes, place, own, other, *outs):
    matrix, begin = pl.program_id(0), 0
    plane, line = sizes
    rows = own.shape[2]
    for out, count in zip(outs, counts):

        @pl.when((matrix >= begin) & (matrix < begin + count))
        def here():
            for c, pieces in enumerate((own, other)):
                for p in range(plane):
                    for n in range(line):
                        at = (place[0] ^ c) * plane * line + (place[1] ^ p) * line + (place[2] ^ n)
                        start = pl.multiple_of(at * rows, rows)
                        out[pl.ds(start, rows), :] = pieces[p * line + n, 0].astype(F32)

        begin += count


def spread(place, sizes, own, other, down, over, name):
    counts = [d * o for d, o in zip(down, over)]
    out_specs, out_shape, begin = [], [], 0
    for d, o, count in zip(down, over, counts):

        def place_of(m, place, begin=begin, count=count, o=o):
            at = jnp.clip(m - begin, 0, count - 1)
            return (at // o, at % o)

        out_specs.append(pl.BlockSpec((D, D), place_of))
        out_shape.append(shape((d * D, o * D), F32))
        begin += count
    devices, matrices, rows, _ = own.shape
    block = pl.BlockSpec((devices, 1, rows, D), lambda m, place: (0, m, 0, 0))
    return pl.pallas_call(
        partial(spread_kernel, tuple(counts), sizes),
        grid_spec=pltpu.PrefetchScalarGridSpec(
            num_scalar_prefetch=1, grid=(begin,), in_specs=[block, block], out_specs=out_specs),
        out_shape=out_shape,
        compiler_params=params(),
        name=name,
    )(place, own, other)


BOTH = ("rows", "seq")


def my_index():
    return lax.axis_index(BOTH)


def swap(values, mask):
    n = lax.axis_size("rows") * lax.axis_size("seq")
    return lax.ppermute(values, BOTH, [(s, s ^ mask) for s in range(n)])


def device_bits():
    n = lax.axis_size("rows") * lax.axis_size("seq")
    return [1 << b for b in range(n.bit_length() - 1)]


def masks(dims):
    return [(c, sum(bit for i, bit in enumerate(dims) if c >> i & 1)) for c in range(1 << len(dims))]


def place(dims):
    me = my_index()
    return sum(((me // bit) % 2) << i for i, bit in enumerate(dims))


def to_rows(values):
    n, me = lax.axis_size("seq"), lax.axis_index("seq")
    tokens = values.shape[1]
    row = jnp.zeros((n * tokens, values.shape[2]), values.dtype)
    for k in range(n):
        part = lax.dynamic_index_in_dim(values, me ^ k, 0, keepdims=False)
        part = swap(part, k) if k else part
        row = lax.dynamic_update_slice_in_dim(row, part, (me ^ k) * tokens, 0)
    return row


def to_tokens(row):
    n, me = lax.axis_size("seq"), lax.axis_index("seq")
    tokens = row.shape[0] // n
    values = jnp.zeros((n, tokens, row.shape[1]), row.dtype)
    for k in range(n):
        part = lax.dynamic_slice_in_dim(row, (me ^ k) * tokens, tokens, 0)
        part = swap(part, k) if k else part
        values = lax.dynamic_update_index_in_dim(values, part, me ^ k, 0)
    return values


def chip_groups():
    chips = device_bits()[1:]
    plane, line, rows = chips[:2], [], HALF >> 2
    for bit in chips[2:]:
        if rows >> (len(line) + 1) << (len(line) + 1) == rows and (rows >> (len(line) + 1)) % 8 == 0:
            line.append(bit)
    return plane, line, chips[2 + len(line) :]


def exchange(parts, dims):
    return [swap(part, mask) if mask else part for part, (c, mask) in zip(parts, masks(dims))]


def finish_sum(total, dims):
    for bit in dims:
        total = add_up([total, swap(total, bit)])
    return total


def add_up(parts):
    return sum(p.astype(F32) for p in parts).astype(BF16)


def widen(values, dims):
    return jnp.concatenate([swap(values, mask) if mask else values for c, mask in masks(dims)])


def row_starts(first, second):
    starts = []
    for device in range(1 << len(device_bits())):
        row, size = 0, D
        for dims in ([1], first, second):
            size >>= len(dims)
            row += size * sum(((device // bit) % 2) << i for i, bit in enumerate(dims))
        starts.append(row)
    return tuple(starts)


def sum_small(arrays):
    flat = jnp.concatenate([a.reshape(-1) for a in arrays])
    size = flat.shape[0]
    flat = jnp.pad(flat, (0, -size % 1024)).reshape(-1, 128)
    plane, line, rest = chip_groups()
    for dims in [plane, line, [1]] + [[bit] for bit in rest]:
        mine = place(dims)
        parts = jnp.stack([swap(flat, mask) if mask else flat for c, mask in masks(dims)])
        flat = sum(lax.dynamic_index_in_dim(parts, mine ^ c, 0, keepdims=False) for c in range(len(parts)))
    flat, found, start = flat.reshape(-1), [], 0
    for a in arrays:
        found.append(flat[start : start + a.size].reshape(a.shape))
        start += a.size
    return found


def per_device(
    inputs,
    segment_ids,
    gain_one,
    w_query,
    w_key,
    w_value,
    w_out,
    mix_logits,
    mix_weights,
    gain_two,
    w_hidden,
    w_back,
    cotangent,
):
    ids = lax.dynamic_slice_in_dim(segment_ids, lax.axis_index("seq"), 1, 0)
    x = to_rows(inputs)
    cot = to_rows(cotangent)
    scale = DH ** -0.5
    mix_l = mix_logits.astype(F32) * scale
    mix_w = mix_weights.astype(F32)
    normed_t, q, q_t, k, k_t, v, v_t = project(x, gain_one, w_query, w_key, w_value)
    soft, attended = attend(mix_l, mix_w, ids, q_t, k, v_t)
    out, normed_two, activated, grad_hidden, grad_middle, grad_attn, g, g_t, grad_gain_two = feed(
        x, attended, cot, w_out, w_hidden, w_back, gain_two
    )
    plane, line, others = chip_groups()
    core = place([1]).reshape(1)
    where = jnp.stack([place([1]), place(plane), place(line)])
    across_plane, across_line = 1 << len(plane), 1 << len(line)
    block_out = to_tokens(out)
    kept_one, sent_one = back_weight_grads(core, activated, cot)
    kept_two, sent_two = hidden_weight_grads(core, normed_two, grad_hidden, attended, grad_attn, kept_one)
    wide_count = 2 * (kept_one.shape[0] + kept_two.shape[0]) // 3
    wide, thin = split(where[1:], kept_one, swap(sent_one, 1), kept_two, swap(sent_two, 1), wide_count, across_plane)
    grad_q, grad_logits, grad_mix_logits = query_grads(
        mix_w, mix_l, soft, v, g_t, k_t, q_t, [wide[0], thin[0], block_out])
    grad_mix_logits = grad_mix_logits.reshape(H, H, DH).sum(-1).T * scale
    wide, thin = combine(where[2:0:-1], [exchange(wide, plane), exchange(thin, line)], [across_line, across_plane], [grad_q])
    grad_k = key_grads(mix_l, grad_logits, q, [wide[0]])
    (wide,), (thin,) = combine(where[1:], [exchange(wide, line), exchange(thin, plane)], [1, 1], [grad_k])
    piece = finish_sum(jnp.concatenate([wide, thin]), others)
    grad_v, grad_mix_weights = value_grads(mix_w, soft, v, g, [piece])
    pieces = lax.all_gather(piece, BOTH, axis=0)
    kept, sent = project_weight_grads(core, normed_t, grad_q, grad_k, grad_v)
    grad_in, grad_gain_one = input_grads(grad_q, grad_k, grad_v, x, grad_middle, w_query, w_key, w_value, gain_one)
    (shares,) = combine(where[1:2], [[kept, swap(sent, 1)]], [across_plane])
    (shares,) = combine(where[2:], [exchange(shares, plane)], [across_line])
    own = finish_sum(add_up(exchange(shares, line)), others)[None]
    own = widen(widen(own, line), plane)
    grad_inputs = to_tokens(grad_in)
    grad_w_query, grad_w_key, grad_w_value = spread(
        where, (across_plane, across_line), own, swap(own, 1), (1, 1, 1), (1, 1, 1), "spread")
    grad_gain_one, grad_gain_two, grad_mix_logits, grad_mix_weights = sum_small(
        (grad_gain_one, grad_gain_two, grad_mix_logits, grad_mix_weights)
    )
    grad_w_back, grad_w_hidden, grad_w_out = fill(
        pieces, (row_starts(plane, line), row_starts(line, plane)), wide_count,
        (w_back.shape[0] // D, 1, 1), (1, w_hidden.shape[1] // D, 1), "fill")
    return (
        block_out,
        grad_inputs,
        grad_gain_one.reshape(D),
        grad_w_query,
        grad_w_key,
        grad_w_value,
        grad_w_out,
        grad_mix_logits,
        grad_mix_weights,
        grad_gain_two.reshape(D),
        grad_w_hidden,
        grad_w_back,
    )


def solution(mesh):
    sharded, copied = P("rows", "seq", None), P()
    in_specs = (sharded, P("rows", None)) + (copied,) * 10 + (sharded,)
    out_specs = (sharded, sharded) + (copied,) * 10
    return jax.shard_map(
        per_device, mesh=mesh, in_specs=in_specs, out_specs=out_specs, check_vma=False
    )
```

```python
from functools import partial

from jax import lax
import jax
import jax.numpy as jnp
from jax.experimental import pallas as pl
from jax.experimental.pallas import tpu as pltpu
from jax.sharding import PartitionSpec as P

D, H, DH, LEN, TILE = 768, 12, 64, 1024, 256
TILES = LEN // TILE
F32, BF16 = jnp.float32, jnp.bfloat16
FORWARD_HEADS, BACKWARD_HEADS = 4, 2
VMEM_LIMIT = 60 * 1024 * 1024
MATMUL_FLOPS = 2 * H * 10 * TILE * TILE * D


def span(i):
    return slice(i * TILE, (i + 1) * TILE)


def head_rows(h):
    return slice(h * DH, (h + 1) * DH)


def mm(a, b):
    return jnp.dot(a, b, preferred_element_type=F32)


def whole(shape):
    return pl.BlockSpec(shape, lambda i: (0,) * len(shape), pipeline_mode=pl.Buffered(1))


def some_heads(count, shape):
    return pl.BlockSpec((count,) + shape, lambda i: (i,) + (0,) * len(shape))


SMEM = pl.BlockSpec(memory_space=pltpu.SMEM)


def params():
    return pltpu.CompilerParams(dimension_semantics=("arbitrary",), vmem_limit_bytes=VMEM_LIMIT)


def shape(s, t=BF16):
    return jax.ShapeDtypeStruct(s, t)


def attend_kernel(mix_l, mix_w, id_row, id_col, q_t, k, v_t, soft, out, bias, scaled, acc):
    step = pl.program_id(0)

    @pl.when(step == 0)
    def start():
        acc[...] = jnp.zeros_like(acc)
        for t in range(TILES):
            for u in range(t + 1):
                allowed = id_col[span(u), :] == id_row[:, span(t)]
                if u == t:
                    key = lax.broadcasted_iota(jnp.int32, (TILE, TILE), 0)
                    query = lax.broadcasted_iota(jnp.int32, (TILE, TILE), 1)
                    allowed = allowed & (key <= query)
                bias[span(u), span(t)] = jnp.where(allowed, 0.0, -1e30)

    for i in range(FORWARD_HEADS):
        j = step * FORWARD_HEADS + i
        for h in range(H):
            scaled[i, head_rows(h), :] = (q_t[head_rows(h), :].astype(F32) * mix_l[h, j]).astype(BF16)
        for t in reversed(range(TILES)):
            n = (t + 1) * TILE
            logits = mm(k[:n, :], scaled[i, :, span(t)]) + bias[:n, span(t)]
            e = jnp.exp(logits - jnp.max(logits, axis=0, keepdims=True))
            p = (e * (1.0 / jnp.sum(e, axis=0, keepdims=True))).astype(BF16)
            soft[i, :n, span(t)] = p
            part = mm(v_t[:, :n], p)
            for h in range(H):
                acc[head_rows(h), span(t)] += part[head_rows(h), :] * mix_w[j, h]

    @pl.when(step == H // FORWARD_HEADS - 1)
    def finish():
        for t in range(TILES):
            out[span(t), :] = acc[:, span(t)].T.astype(BF16)


def attend(mix_l, mix_w, ids, q_t, k, v_t):
    heads = FORWARD_HEADS
    return pl.pallas_call(
        attend_kernel,
        grid=(H // heads,),
        in_specs=[SMEM, SMEM, whole((1, LEN)), whole((LEN, 1)), whole((D, LEN)), whole((LEN, D)), whole((D, LEN))],
        out_specs=[some_heads(heads, (LEN, LEN)), whole((LEN, D))],
        out_shape=[shape((H, LEN, LEN)), shape((LEN, D))],
        scratch_shapes=[
            pltpu.VMEM((LEN, LEN), F32), pltpu.VMEM((heads, D, LEN), BF16), pltpu.VMEM((D, LEN), F32)
        ],
        compiler_params=params(),
        cost_estimate=pl.CostEstimate(flops=MATMUL_FLOPS // 4, bytes_accessed=LEN * LEN, transcendentals=0),
        name="attend",
    )(mix_l, mix_w, ids.reshape(1, LEN), ids.reshape(LEN, 1), q_t, k, v_t)


def head_row(weight_of):
    head = lax.broadcasted_iota(jnp.int32, (1, D), 1) // DH
    row = jnp.full((1, D), weight_of(0), F32)
    for h in range(1, H):
        row = jnp.where(head == h, weight_of(h), row)
    return row


def value_grads_kernel(mix_w, soft, v, g, *rest):
    out, mix_grad, acc = rest[-3:]
    step = pl.program_id(0)

    @pl.when(step == 0)
    def start():
        acc[...] = jnp.zeros_like(acc)

    for i in range(BACKWARD_HEADS):
        total = jnp.zeros((1, D), F32)
        mix_row = head_row(lambda h: mix_w[step * BACKWARD_HEADS + i, h])
        for u in range(TILES):
            part = mm(soft[i, span(u), u * TILE :], g[u * TILE :, :])
            acc[span(u), :] += part * mix_row
            total = total + jnp.sum(part * v[span(u), :].astype(F32), axis=0, keepdims=True)
        mix_grad[i] = total

    @pl.when(step == H // BACKWARD_HEADS - 1)
    def finish():
        out[...] = acc[...].astype(BF16)


def query_grads_kernel(heads, mix_w, mix_l, soft, v, g_t, k_t, q_t, *rest):
    before, (out, grad_logits, mix_grad, acc, scaled) = rest[0], rest[-5:]
    step = pl.program_id(0)
    first_head = heads[0] + step * BACKWARD_HEADS

    @pl.when(step == 0)
    def start():
        acc[...] = before[...] if heads[0] else jnp.zeros_like(acc)

    for i in range(BACKWARD_HEADS):
        j = first_head + i
        for h in range(H):
            scaled[i, head_rows(h), :] = (g_t[head_rows(h), :].astype(F32) * mix_w[j, h]).astype(BF16)
    order = [(i, t) for i in range(BACKWARD_HEADS) for t in reversed(range(TILES))]

    def grad_soft(i, t):
        return mm(v[: (t + 1) * TILE, :], scaled[i, :, span(t)])

    coming = grad_soft(*order[0])
    total = jnp.zeros((D, 128), F32)
    for at, (i, t) in enumerate(order):
        n = (t + 1) * TILE
        p = soft[i, :n, span(t)].astype(F32)
        weighted = p * coming
        low = (weighted - p * jnp.sum(weighted, axis=0, keepdims=True)).astype(BF16)
        grad_logits[i, :n, span(t)] = low
        if at + 1 < len(order):
            coming = grad_soft(*order[at + 1])
        part = mm(k_t[:, :n], low)
        for h in range(H):
            acc[head_rows(h), span(t)] += part[head_rows(h), :] * mix_l[h, first_head + i]
        product = part * q_t[:, span(t)].astype(F32)
        total = total + product[:, :128] + product[:, 128:]
        if t == 0:
            mix_grad[i] = jnp.sum(total.T, axis=0, keepdims=True)
            total = jnp.zeros((D, 128), F32)

    @pl.when(step == pl.num_programs(0) - 1)
    def finish():
        if heads[1] < H:
            out[...] = acc[...]
        else:
            for t in range(TILES):
                out[span(t), :] = acc[:, span(t)].T.astype(BF16)


def key_grads_kernel(mix_l, grad_logits, q, *rest):
    out, acc = rest[-2:]
    step = pl.program_id(0)

    @pl.when(step == 0)
    def start():
        acc[...] = jnp.zeros_like(acc)

    for i in range(BACKWARD_HEADS):
        mix_row = head_row(lambda h: mix_l[h, step * BACKWARD_HEADS + i])
        for u in range(TILES):
            acc[span(u), :] += mm(grad_logits[i, span(u), u * TILE :], q[u * TILE :, :]) * mix_row

    @pl.when(step == H // BACKWARD_HEADS - 1)
    def finish():
        out[...] = acc[...].astype(BF16)


def back_call(kernel, heads, in_specs, out_specs, out_shape, scratch, matmuls, name):
    def run(*operands):
        *used, first = operands
        return pl.pallas_call(
            kernel,
            grid=(heads // BACKWARD_HEADS,),
            in_specs=in_specs + [pl.BlockSpec(memory_space=pl.ANY)] * len(first),
            out_specs=out_specs,
            out_shape=out_shape,
            scratch_shapes=scratch,
            compiler_params=params(),
            cost_estimate=pl.CostEstimate(
                flops=matmuls * MATMUL_FLOPS * heads // H // 8, bytes_accessed=LEN * LEN, transcendentals=0
            ),
            name=name,
        )(*used, *first)

    return run


ROW, COLUMN = whole((LEN, D)), whole((D, LEN))
PER_HEAD, PER_HEAD_ROW = some_heads(BACKWARD_HEADS, (LEN, LEN)), some_heads(BACKWARD_HEADS, (1, D))


def value_grads(mix_w, soft, v, g, first):
    grads, mix_grad = back_call(
        value_grads_kernel,
        H,
        [SMEM, PER_HEAD, ROW, ROW],
        [ROW, PER_HEAD_ROW],
        [shape((LEN, D)), shape((H, 1, D), F32)],
        [pltpu.VMEM((LEN, D), F32)],
        1,
        "value_grads",
    )(mix_w, soft, v, g, first)
    return grads, mix_grad


def query_grads(mix_w, mix_l, soft, v, g_t, k_t, q_t, first, heads=(0, H), before=()):
    low, high = heads
    count, last = high - low, high == H
    per_head = pl.BlockSpec((BACKWARD_HEADS, LEN, LEN), lambda i: (i + low // BACKWARD_HEADS, 0, 0))
    grads, grad_logits, mix_grad = back_call(
        partial(query_grads_kernel, heads),
        count,
        [SMEM, SMEM, per_head, ROW, COLUMN, COLUMN, COLUMN] + [COLUMN] * len(before),
        [ROW if last else COLUMN, PER_HEAD, PER_HEAD_ROW],
        [shape((LEN, D)) if last else shape((D, LEN), F32), shape((count, LEN, LEN)), shape((count, 1, D), F32)],
        [pltpu.VMEM((D, LEN), F32), pltpu.VMEM((BACKWARD_HEADS, D, LEN), BF16)],
        2,
        "query_grads",
    )(mix_w, mix_l, soft, v, g_t, k_t, q_t, *before, first)
    return grads, grad_logits, mix_grad


def key_grads(mix_l, grad_logits, q, first):
    return back_call(
        key_grads_kernel, H, [SMEM, PER_HEAD, ROW], ROW, shape((LEN, D)), [pltpu.VMEM((LEN, D), F32)], 1,
        "key_grads",
    )(mix_l, grad_logits, q, first)


epsilon = 1e-06
GELU_SCALE = 0.7978845608028654
GELU_CUBIC = 0.044715
FEED_COLUMNS = 1024
COST_SHARE = 4
HALF = D // 2
ANY = pl.BlockSpec(memory_space=pl.ANY)
VMEM = pl.BlockSpec(memory_space=pltpu.VMEM)


def against(left, right):
    return lax.dot_general(left, right, (((1,), (1,)), ((), ())), preferred_element_type=F32)


def across(left, right):
    return lax.dot_general(left, right, (((0,), (0,)), ((), ())), preferred_element_type=F32)


def inverse_rms(values):
    return lax.rsqrt(jnp.mean(values * values, axis=-1, keepdims=True) + epsilon)


def cost(matrices):
    return pl.CostEstimate(flops=int(matrices * LEN * D * D) // COST_SHARE, bytes_accessed=LEN * D, transcendentals=0)


def fixed(s):
    return pl.BlockSpec(s, lambda i, at: (0,) * len(s), pipeline_mode=pl.Buffered(1))


def tokens(rows, shift=0):
    return pl.BlockSpec((rows, D), lambda i, at: (at[0] ^ (i + shift), 0))


def tokens_t(columns, shift=0):
    return pl.BlockSpec((D, columns), lambda i, at: (0, at[0] ^ (i + shift)))


def step_call(kernel, at, steps, in_specs, operands, out_specs, out_shape, matrices, name, scratch=(), aliases=None):
    return pl.pallas_call(
        kernel,
        grid_spec=pltpu.PrefetchScalarGridSpec(
            num_scalar_prefetch=1, grid=(steps,), in_specs=in_specs, out_specs=out_specs, scratch_shapes=list(scratch)),
        out_shape=out_shape,
        input_output_aliases=aliases or {},
        compiler_params=params(),
        cost_estimate=cost(matrices),
        name=name,
    )(at, *operands)


def chosen(refs, step):
    values = refs[0][...]
    for i, ref in enumerate(refs[1:]):
        values = jnp.where(step == i + 1, ref[...], values)
    return values


def write_parts(outs, step, values):
    for i, out in enumerate(outs[:-1]):

        @pl.when(step == i)
        def write():
            out[...] = values

    far = outs[-1].shape[0]
    for i in range(far):

        @pl.when(step == len(outs) - 1 + i)
        def write_far():
            outs[-1][i] = values


def part_outs(parts, rows):
    near = parts // 2
    specs = [fixed((rows, D))] * near + [fixed((parts - near, rows, D))]
    return specs, [shape((rows, D))] * near + [shape((parts - near, rows, D))]


def project_kernel(steps, waits, shares, at, *refs):
    parts, (gain, w_query, w_key, w_value) = refs[:steps], refs[steps : steps + 4]
    rest = refs[steps + 4 + waits :]
    cotangent, rest = (rest[0], rest[1:]) if shares else (None, rest)
    row, normed_t, q, q_t, k, k_t, v, v_t = rest[:8]
    step = pl.program_id(0)
    low = chosen(parts, step)
    row[...] = low
    values = low.astype(F32)
    normed = (values * inverse_rms(values) * gain[...]).astype(BF16)
    normed_t[...] = normed.T
    for weight, out, out_t in ((w_query, q, q_t), (w_key, k, k_t), (w_value, v, v_t)):
        part = mm(normed, weight[...]).astype(BF16)
        out[...] = part
        out_t[...] = part.T
    if shares:

        @pl.when(step == 0)
        def lay_out():
            for i, out in enumerate(rest[8:]):
                out[...] = cotangent[at[0] ^ i]


def project(at, parts, shift, gain, w_query, w_key, w_value, before=(), cotangent=None):
    count, rows = len(parts), parts[0].shape[0]
    square, ways = fixed((D, D)), 0 if cotangent is None else cotangent.shape[0]
    row, column = (tokens(rows, shift), shape((LEN, D))), (tokens_t(rows, shift), shape((D, LEN)))
    outs = [row, column, row, column, row, column, row, column] + [(fixed((rows, D)), shape((rows, D)))] * ways
    start = 1 + count + 4
    return step_call(
        partial(project_kernel, count, len(before), ways > 0), at, count,
        [fixed((rows, D))] * count + [fixed((1, D)), square, square, square] + [ANY] * len(before)
        + [fixed((ways, rows, D))] * (ways > 0),
        (*parts, gain, w_query, w_key, w_value, *before) + ((cotangent,) if ways else ()),
        [o[0] for o in outs], [o[1] for o in outs], 3 * count / 4, "project",
        aliases={start + i: i for i in range(len(before))})


def feed_kernel(parts, at, x, attended, *refs):
    cots, (w_out, w_hidden, w_back, gain), rest = refs[:parts], refs[parts : parts + 4], refs[parts + 4 :]
    outs, (cot_row, normed_two, activated, grad_hidden, grad_middle, grad_attn, g, g_t) = rest[:-8], rest[-8:]
    step = pl.program_id(0)
    scale = gain[...]
    cotangent = chosen(cots, step)
    cot_row[...] = cotangent
    middle = x[...].astype(F32) + mm(attended[...], w_out[...])
    inverse = inverse_rms(middle)
    n2 = (middle * inverse * scale).astype(BF16)
    normed_two[...] = n2
    total = middle
    grad_n2 = jnp.zeros_like(middle)
    width = FEED_COLUMNS
    for c in range(w_hidden.shape[1] // width):
        cols = slice(c * width, (c + 1) * width)
        hidden = mm(n2, w_hidden[:, cols])
        grad_act = against(cotangent, w_back[cols, :])
        squared = hidden * hidden
        tanh = jnp.tanh(GELU_SCALE * hidden * (1.0 + GELU_CUBIC * squared))
        half = 0.5 + 0.5 * tanh
        act = (hidden * half).astype(BF16)
        activated[:, cols] = act
        slope = half + (0.5 * GELU_SCALE) * hidden * (1.0 - tanh * tanh) * (1.0 + 3.0 * GELU_CUBIC * squared)
        grad = (grad_act * slope).astype(BF16)
        grad_hidden[:, cols] = grad
        total = total + mm(act, w_back[cols, :])
        grad_n2 = grad_n2 + against(grad, w_hidden[:, cols])
    low = total.astype(BF16)
    write_parts(outs, step, low)
    weighted = grad_n2 * scale
    mean = jnp.mean(weighted * middle, axis=-1, keepdims=True)
    grad_mid = cotangent.astype(F32) + inverse * weighted - middle * (inverse * inverse * inverse * mean)
    grad_middle[...] = grad_mid
    grad_low = grad_mid.astype(BF16)
    grad_attn[...] = grad_low
    grad = against(grad_low, w_out[...]).astype(BF16)
    g[...] = grad
    g_t[...] = grad.T


def feed(at, x, attended, cots, w_out, w_hidden, w_back, gain):
    ff, parts, rows = w_hidden.shape[1], len(cots), cots[0].shape[0]
    tile = (tokens(rows), shape((LEN, D)))
    wide = (pl.BlockSpec((rows, ff), lambda i, at: (at[0] ^ i, 0)), shape((LEN, ff)))
    outs = list(zip(*part_outs(parts, rows))) + [
        tile, tile, wide, wide, (tokens(rows), shape((LEN, D), F32)), tile, tile, (tokens_t(rows), shape((D, LEN)))]
    found = step_call(
        partial(feed_kernel, parts), at, parts,
        [tokens(rows), tokens(rows)] + [fixed((rows, D))] * parts
        + [fixed((D, D)), fixed((D, ff)), fixed((ff, D)), fixed((1, D))],
        (x, attended, *cots, w_out, w_hidden, w_back, gain), [o[0] for o in outs], [o[1] for o in outs],
        2 + 4 * ff // D, "feed")
    return found[:-8], found[-8:]


def input_kernel(parts, at, grad_q, grad_k, grad_v, x, grad_middle, w_query, w_key, w_value, gain, first, *outs):
    upstream = against(grad_q[...], w_query[...]) + against(grad_k[...], w_key[...]) + against(grad_v[...], w_value[...])
    values = x[...].astype(F32)
    inverse = inverse_rms(values)
    weighted = upstream * gain[...]
    mean = jnp.mean(weighted * values, axis=-1, keepdims=True)
    low = (grad_middle[...] + inverse * weighted - values * (inverse * inverse * inverse * mean)).astype(BF16)
    write_parts(outs, pl.program_id(0), low)


def input_grads(at, parts, grad_q, grad_k, grad_v, x, grad_middle, w_query, w_key, w_value, gain, first):
    rows, square = LEN // parts, fixed((D, D))
    return step_call(
        partial(input_kernel, parts), at, parts, [tokens(rows)] * 5 + [square, square, square, fixed((1, D)), ANY],
        (grad_q, grad_k, grad_v, x, grad_middle, w_query, w_key, w_value, gain, first),
        *part_outs(parts, rows), 3, "input_grads")


def both_halves(kept, sent, product, left_kept, left_sent, right):
    kept[0, :HALF] = product(left_kept[...], right[...]).astype(BF16)
    sent[0, :HALF] = product(left_sent[...], right[...]).astype(BF16)


def wide_kernel(backs, core, act_kept, act_sent, cot, n2_kept, n2_sent, grad_hidden, kept, sent):
    step = pl.program_id(0)
    pl.when(step < backs)(partial(both_halves, kept, sent, across, act_kept, act_sent, cot))
    pl.when(step >= backs)(partial(both_halves, kept, sent, across, n2_kept, n2_sent, grad_hidden))


def thin_kernel(hiddens, core, n2_kept, n2_sent, grad_hidden, att_kept, att_sent, grad_attn, *refs):
    step, (kept, sent) = pl.program_id(0), refs[-2:]
    pl.when(step < hiddens)(partial(both_halves, kept, sent, across, n2_kept, n2_sent, grad_hidden))
    pl.when(step >= hiddens)(partial(both_halves, kept, sent, across, att_kept, att_sent, grad_attn))


def columns_half(other, at=lambda i: 0):
    return pl.BlockSpec((LEN, HALF), lambda i, core: (0, 2 * at(i) + (core[0] ^ other)))


def rows_half(other):
    return pl.BlockSpec((HALF, LEN), lambda i, core: (core[0] ^ other, 0))


def wide_and_thin(blocks):
    count = 2 * blocks + 1
    return 2 * count // 3, count - 2 * count // 3


def wide_weight_grads(core, activated, cot, normed_two, grad_hidden):
    blocks = activated.shape[1] // D
    count, _ = wide_and_thin(blocks)
    row, half = fixed((LEN, D)), pl.BlockSpec((1, HALF, D), lambda i, core: (i, 0, 0))

    def back(i):
        return jnp.minimum(i, blocks - 1)

    return step_call(
        partial(wide_kernel, blocks), core, count,
        [columns_half(0, back), columns_half(1, back), row, columns_half(0), columns_half(1),
         pl.BlockSpec((LEN, D), lambda i, core: (0, jnp.maximum(i - blocks, 0)))],
        (activated, activated, cot, normed_two, normed_two, grad_hidden),
        [half, half], [shape((count, HALF, D))] * 2, count, "wide_weight_grads")


def thin_weight_grads(core, normed_two, grad_hidden, attended, grad_attn, first):
    blocks = grad_hidden.shape[1] // D
    count, left = wide_and_thin(blocks)
    row, half = fixed((LEN, D)), pl.BlockSpec((1, HALF, D), lambda i, core: (i, 0, 0))
    return step_call(
        partial(thin_kernel, left - 1), core, left,
        [columns_half(0), columns_half(1),
         pl.BlockSpec((LEN, D), lambda i, core: (0, jnp.minimum(i + count - blocks, blocks - 1))),
         columns_half(0), columns_half(1), row] + [ANY] * len(first),
        (normed_two, normed_two, grad_hidden, attended, attended, grad_attn, *first),
        [half, half], [shape((left, HALF, D))] * 2, left, "thin_weight_grads")


SMALL_ROWS = 8


def small_sums(by_logits, by_weights):
    rows = jnp.concatenate([by_logits[:, 0, :], by_weights[:, 0, :]])
    head = lax.broadcasted_iota(jnp.int32, (D, 128), 0) // DH
    select = (head == lax.broadcasted_iota(jnp.int32, (D, 128), 1)).astype(F32)
    sums = jnp.dot(rows, select, precision=lax.Precision.HIGHEST, preferred_element_type=F32)
    groups = [sums[r : r + SMALL_ROWS, :] for r in range(0, 2 * H, SMALL_ROWS)]
    return jnp.concatenate(groups + [jnp.zeros((SMALL_ROWS, D - 128 * len(groups)), F32)], axis=1)


def project_weights_kernel(count, waits, core, nt_kept, nt_sent, *refs):
    grads, small, (kept, sent) = refs[:count], refs[count : -2 - waits], refs[-2:]
    for i, each in enumerate(grads):
        pl.when(pl.program_id(0) == i)(partial(both_halves, kept, sent, mm, nt_kept, nt_sent, each))
    if small:
        rows = jnp.concatenate([small_sums(*small), jnp.zeros((SMALL_ROWS, D), F32)]).astype(BF16)
        kept[0, HALF:] = rows
        sent[0, HALF:] = rows


def project_weight_grads(core, normed_t, grads, small=(), first=()):
    count, rows = len(grads), HALF + 2 * SMALL_ROWS * (len(small) > 0)
    half = pl.BlockSpec((1, rows, D), lambda i, core: (i, 0, 0))
    return step_call(
        partial(project_weights_kernel, count, len(first)), core, count,
        [rows_half(0), rows_half(1)] + [fixed((LEN, D))] * count + [fixed((H, 1, D))] * len(small) + [ANY] * len(first),
        (normed_t, normed_t, *grads, *small, *first), [half, half], [shape((count, rows, D))] * 2, count, "project_weight_grads")


def split_kernel(waits, mine, kept, came, *refs):
    outs, total = refs[waits:-1], refs[-1]
    total[...] = kept[...].astype(F32) + came[...].astype(F32)
    for c, out in enumerate(outs):
        rows = out.shape[1]
        out[...] = total[:, pl.ds(pl.multiple_of((mine[0] ^ c) * rows, 8), rows), :].astype(BF16)


def split(mine, kept, came, ways, name, first=()):
    count, rows, _ = kept.shape
    block = pl.BlockSpec((1, rows, D), lambda m, mine: (m, 0, 0))
    return step_call(
        partial(split_kernel, len(first)), mine, count, [block, block] + [ANY] * len(first), (kept, came, *first),
        [pl.BlockSpec((1, rows // ways, D), lambda m, mine: (m, 0, 0))] * ways,
        [shape((count, rows // ways, D))] * ways, 0, name, [pltpu.VMEM((1, rows, D), F32)])


def lay_out_kernel(waits, mine, kept, came, *refs):
    out = refs[waits]
    ways, _, rows, _ = out.shape
    for m in range(kept.shape[0]):
        total = kept[m].astype(F32) + came[m].astype(F32)
        for c in range(ways):
            out[c, m] = total[c * rows : (c + 1) * rows, :].astype(BF16)


def lay_out(mine, kept, came, ways, per_step, name, first=()):
    count, rows, _ = kept.shape
    block = pl.BlockSpec((per_step, rows, D), lambda m, mine: (m, 0, 0))
    return step_call(
        partial(lay_out_kernel, len(first)), mine, count // per_step, [block, block] + [ANY] * len(first),
        (kept, came, *first),
        pl.BlockSpec((ways, per_step, rows // ways, D), lambda m, mine: (0, m, 0, 0)),
        shape((ways, count, rows // ways, D)), 0, name)


def plain_call(kernel, operands, mine, out_shape, name, scratch=(), first=(), through=()):
    outs = pl.pallas_call(
        kernel,
        in_specs=[SMEM] + [VMEM] * len(operands) + [ANY] * (len(first) + len(through)),
        out_specs=[VMEM] * len(out_shape) + [ANY] * len(through),
        out_shape=list(out_shape) + [shape(t.shape, t.dtype) for t in through],
        input_output_aliases={1 + len(operands) + len(first) + i: len(out_shape) + i for i in range(len(through))},
        scratch_shapes=list(scratch),
        compiler_params=pltpu.CompilerParams(vmem_limit_bytes=VMEM_LIMIT),
        name=name,
    )(mine, *operands, *first, *through)
    return outs[: len(out_shape)], outs[len(out_shape) :]


def added(refs):
    return sum(ref[...].astype(F32) for ref in refs)


def sum_first(ref):
    return sum(ref[i].astype(F32) for i in range(ref.shape[0]))


def reshare_kernel(line, waits, mine, wide, *refs):
    thin, outs, total = refs[:line], refs[line + waits : -1], refs[-1]
    total[...] = sum_first(wide)
    for c in range(line):
        rows = outs[c].shape[1]
        outs[c][...] = total[:, pl.ds(pl.multiple_of((mine[1] ^ c) * rows, 8), rows), :].astype(BF16)
    out = outs[line]
    thin_sum, rows = added(thin), out.shape[2]
    for c in range(out.shape[0]):
        out[c] = thin_sum[:, c * rows : (c + 1) * rows, :].astype(BF16)


def reshare(mine, wide, thin, first):
    plane, count, rows, _ = wide.shape
    line, (left, thin_rows, _) = len(thin), thin[0].shape
    outs, _ = plain_call(
        partial(reshare_kernel, line, len(first)), [wide, *thin], mine,
        [shape((count, rows // line, D))] * line + [shape((plane, left, thin_rows // plane, D))], "reshare",
        [pltpu.VMEM((count, rows, D), F32)], first)
    return outs[:line], outs[line]


def piece_kernel(line, waits, mine, thin, *refs):
    wide, out = refs[:line], refs[line + waits]
    count = wide[0].shape[0]
    out[:count] = added(wide).astype(BF16)
    out[count:] = sum_first(thin).astype(BF16)


def piece_of(mine, wide, thin, first, through):
    (count, rows, _), left = wide[0].shape, thin.shape[1]
    (out,), through = plain_call(
        partial(piece_kernel, len(wide), len(first) + len(through)), [thin, *wide], mine,
        [shape((count + left, rows, D))], "piece", (), first, through)
    return out, through


def split_small_kernel(mine, kept, came, *refs):
    outs, total, share = refs[:-2], refs[-2], refs[-1]
    total[...] = kept[0].astype(F32) + came[0].astype(F32)
    rows = share.shape[0] - SMALL_ROWS
    share[rows:] = total[HALF : HALF + SMALL_ROWS, :]
    for c, out in enumerate(outs):
        share[:rows] = total[pl.ds(pl.multiple_of((mine[0] ^ c) * rows, 8), rows), :]
        out[...] = share[...].astype(BF16)


def split_small(mine, kept, came, ways, name):
    rows = HALF // ways + SMALL_ROWS
    outs, _ = plain_call(
        split_small_kernel, [kept, came], mine, [shape((rows, D))] * ways, name,
        [pltpu.VMEM(kept.shape[1:], F32), pltpu.VMEM((rows, D), F32)])
    return outs


def project_reshare_kernel(ways, waits, mine, *refs):
    line, through = waits
    pairs, ones, outs = refs[:ways], refs[ways : 2 * ways], refs[2 * ways + through : 2 * ways + through + line]
    pair, one, share = refs[-3:]
    pair[...] = added(pairs)
    one[...] = added(ones)
    rows = pair.shape[1] // len(outs)
    share[3 * rows :] = one[pair.shape[1] :, :]
    for c, out in enumerate(outs):
        start = pl.multiple_of((mine[1] ^ c) * rows, 8)
        share[:rows] = pair[0, pl.ds(start, rows), :]
        share[rows : 2 * rows] = pair[1, pl.ds(start, rows), :]
        share[2 * rows : 3 * rows] = one[pl.ds(start, rows), :]
        out[...] = share[...].astype(BF16)


def project_reshare(mine, pairs, ones, ways, through):
    rows = 3 * pairs[0].shape[1] // ways + SMALL_ROWS
    return plain_call(
        partial(project_reshare_kernel, len(pairs), (ways, len(through))), [*pairs, *ones], mine,
        [shape((rows, D))] * ways, "project_reshare",
        [pltpu.VMEM(pairs[0].shape, F32), pltpu.VMEM(ones[0].shape, F32), pltpu.VMEM((rows, D), F32)], (), through)


def project_piece_kernel(mine, *refs):
    parts, (out, small, total) = refs[:-3], refs[-3:]
    total[...] = added(parts)
    rows = out.shape[1]
    for m in range(3):
        out[m] = total[m * rows : (m + 1) * rows, :].astype(BF16)
    small[...] = total[3 * rows :, :]


def project_piece(mine, parts):
    rows = parts[0].shape[0]
    (out, small), _ = plain_call(
        project_piece_kernel, list(parts), mine,
        [shape((3, (rows - SMALL_ROWS) // 3, D)), shape((SMALL_ROWS, D), F32)], "project_piece",
        [pltpu.VMEM((rows, D), F32)])
    return out, small


def stack_kernel(count, waits, mine, *refs):
    out, at = refs[count + waits], 0
    for ref in refs[:count]:
        out[at : at + ref.shape[0]] = ref[...]
        at += ref.shape[0]


def stack(mine, parts, name, first=()):
    rows = sum(p.shape[0] for p in parts)
    (out,), _ = plain_call(
        partial(stack_kernel, len(parts), len(first)), list(parts), mine, [shape((rows,) + parts[0].shape[1:])], name,
        (), first)
    return out


def tokens_kernel(waits, at, *refs):
    near, near_came, far, forwarded, out = *refs[:4], refs[4 + waits]
    for i, ref in enumerate((near, near_came, far.at[0], forwarded)):
        out[at[0] ^ i] = ref[...]


def tokens_of(at, came, name, first=()):
    (out,), _ = plain_call(
        partial(tokens_kernel, len(first)), list(came), at, [shape((4,) + came[0].shape)], name, (), first)
    return out


def weigh(out, weight):
    product = out[...] * weight[...].astype(F32)
    return sum(product[:, c : c + 128] for c in range(0, D, 128))


def as_row(weighed):
    return jnp.sum(weighed[...].T, axis=0, keepdims=True)


def spread_kernel(sizes, place, own, other, w_query, w_key, w_value, gain, *refs):
    outs, by_gain, weighed = refs[-5:-2], refs[-2], refs[-1]
    matrix = pl.program_id(0)
    plane, line = sizes
    rows = own.shape[2]

    @pl.when(matrix == 0)
    def zero():
        weighed[...] = jnp.zeros_like(weighed)

    for i, (out, weight) in enumerate(zip(outs, (w_query, w_key, w_value))):

        @pl.when(matrix == i)
        def here():
            for c, pieces in enumerate((own, other)):
                for p in range(plane):
                    for n in range(line):
                        at = (place[0] ^ c) * plane * line + (place[1] ^ p) * line + (place[2] ^ n)
                        out[pl.ds(pl.multiple_of(at * rows, 8), rows), :] = pieces[p * line + n, 0].astype(F32)
            weighed[...] += weigh(out, weight)

    @pl.when(matrix == 2)
    def finish():
        by_gain[...] = as_row(weighed) / gain[...]


def matrix_outs(down, over):
    specs, shapes, begin, places = [], [], 0, []
    for d, o in zip(down, over):
        count = d * o

        def place_of(m, *at, begin=begin, count=count, o=o):
            within = jnp.clip(m - begin, 0, count - 1)
            return (within // o, within % o)

        places.append(place_of)
        specs.append(pl.BlockSpec((D, D), place_of))
        shapes.append(shape((d * D, o * D), F32))
        begin += count
    return specs, shapes, begin, places


def spread(place, sizes, own, other, w_query, w_key, w_value, gain, first):
    out_specs, out_shape, count, _ = matrix_outs((1, 1, 1), (1, 1, 1))
    devices, matrices, rows, _ = own.shape
    block = pl.BlockSpec((devices, 1, rows, D), lambda m, place: (0, m, 0, 0))
    square = fixed((D, D))
    return step_call(
        partial(spread_kernel, sizes), place, count, [block, block, square, square, square, fixed((1, D))] + [ANY] * len(first),
        (own, other, w_query, w_key, w_value, gain, *first),
        out_specs + [fixed((1, D))], out_shape + [shape((1, D), F32)], 0, "spread", [pltpu.VMEM((D, 128), F32)])


def fill_kernel(counts, wide_count, starts, pieces, w_hidden, gain, *refs):
    outs, by_gain, weighed = refs[:3], refs[3], refs[4]
    matrix, begin, rows = pl.program_id(0), 0, pieces.shape[2]

    @pl.when(matrix == 0)
    def zero():
        weighed[...] = jnp.zeros_like(weighed)

    for index, (out, count) in enumerate(zip(outs, counts)):
        for table, low, high in ((0, begin, min(begin + count, wide_count)), (1, max(begin, wide_count), begin + count)):
            if low < high:

                @pl.when((matrix >= low) & (matrix < high))
                def here():
                    for device, start in enumerate(starts[table]):
                        out[start : start + rows, :] = pieces[device, 0].astype(F32)
                    if index == 1:
                        weighed[...] += weigh(out, w_hidden)

        begin += count

    @pl.when(matrix == begin - 1)
    def finish():
        by_gain[...] = as_row(weighed) / gain[...]


def fill(pieces, starts, w_hidden, gain):
    blocks = w_hidden.shape[1] // D
    down, over = (blocks, 1, 1), (1, blocks, 1)
    out_specs, out_shape, count, places = matrix_outs(down, over)
    devices, matrices, rows, _ = pieces.shape
    line = whole((1, D))
    return pl.pallas_call(
        partial(fill_kernel, tuple(d * o for d, o in zip(down, over)), wide_and_thin(blocks)[0], starts),
        grid=(count,),
        in_specs=[pl.BlockSpec((devices, 1, rows, D), lambda m: (0, m, 0, 0)), pl.BlockSpec((D, D), places[1]), line],
        out_specs=out_specs + [line],
        out_shape=out_shape + [shape((1, D), F32)],
        scratch_shapes=[pltpu.VMEM((D, 128), F32)],
        compiler_params=params(),
        name="fill",
    )(pieces, w_hidden, gain)


BOTH = ("rows", "seq")


def swap(values, mask):
    n = lax.axis_size("rows") * lax.axis_size("seq")
    return lax.ppermute(values, BOTH, [(s, s ^ mask) for s in range(n)])


def device_bits():
    n = lax.axis_size("rows") * lax.axis_size("seq")
    return [1 << b for b in range(n.bit_length() - 1)]


def masks(dims):
    return [(c, sum(bit for i, bit in enumerate(dims) if c >> i & 1)) for c in range(1 << len(dims))]


def place(dims):
    me = lax.axis_index(BOTH)
    return sum(((me // bit) % 2) << i for i, bit in enumerate(dims))


def exchange(parts, dims):
    return [swap(part, mask) if mask else part for part, (c, mask) in zip(parts, masks(dims))]


def chip_groups():
    chips = device_bits()[1:]
    plane, line, rows = chips[:2], [], HALF >> 2
    for bit in chips[2:]:
        if rows >> (len(line) + 1) << (len(line) + 1) == rows and (rows >> (len(line) + 1)) % 8 == 0:
            line.append(bit)
    return plane, line, chips[2 + len(line) :]


def finish_sum(total, dims):
    for bit in dims:
        total = (total.astype(F32) + swap(total, bit).astype(F32)).astype(total.dtype)
    return total


def row_starts(first, second):
    starts = []
    for device in range(1 << len(device_bits())):
        row, size = 0, D
        for dims in ([1], first, second):
            size >>= len(dims)
            row += size * sum(((device // bit) % 2) << i for i, bit in enumerate(dims))
        starts.append(row)
    return tuple(starts)


def trade(values, dims):
    n = lax.axis_size("rows") * lax.axis_size("seq")
    groups, found = [], set()
    for device in range(n):
        if device not in found:
            group = [device ^ mask for c, mask in masks(dims)]
            found.update(group)
            groups.append(group)
    return lax.all_to_all(values, BOTH, split_axis=0, concat_axis=0, tiled=True, axis_index_groups=groups)


def widen(mine, values, dims, name, first=()):
    return stack(mine, exchange([values] * (1 << len(dims)), dims), name, first)


def send_tokens(parts):
    mine, near, far = parts
    return mine, swap(near, 1), swap(far, 2)


def hand_on(came):
    return (*came, swap(came[2][1], 1))


def per_device(
    inputs,
    segment_ids,
    gain_one,
    w_query,
    w_key,
    w_value,
    w_out,
    mix_logits,
    mix_weights,
    gain_two,
    w_hidden,
    w_back,
    cotangent,
):
    plane, line, others = chip_groups()
    where = jnp.stack([place([1]), place(plane), place(line)])
    core, spots = where[:1], where[1:]
    sizes = (1 << len(plane), 1 << len(line))
    parts, seq = lax.axis_size("seq"), lax.axis_index("seq")
    row_bits, at = device_bits()[: parts.bit_length() - 1], seq.reshape(1)
    ids = lax.dynamic_slice_in_dim(segment_ids, seq, 1, 0)
    gain_one, gain_two = gain_one.reshape(1, D), gain_two.reshape(1, D)
    scale = DH ** -0.5
    mix_l = mix_logits.astype(F32) * scale
    mix_w = mix_weights.astype(F32)

    came = exchange([lax.dynamic_index_in_dim(inputs, seq ^ i, 0, keepdims=False) for i in range(parts)], row_bits)
    near = parts // 2
    begun = project(at, came[:near], 0, gain_one, w_query, w_key, w_value)
    done = project(at, came[near:], near, gain_one, w_query, w_key, w_value, begun, cotangent)
    (x, normed_t, q, q_t, k, k_t, v, v_t), cots = done[:8], exchange(done[8:], row_bits)
    soft, attended = attend(mix_l, mix_w, ids, q_t, k, v_t)
    out, (cot, normed_two, activated, grad_hidden, grad_middle, grad_attn, g, g_t) = feed(
        at, x, attended, cots, w_out, w_hidden, w_back, gain_two
    )
    out = send_tokens(out)
    wide_kept, wide_sent = wide_weight_grads(core, activated, cot, normed_two, grad_hidden)
    thin_kept, thin_sent = thin_weight_grads(core, normed_two, grad_hidden, attended, grad_attn, [wide_kept, *out[1:]])
    wide = lay_out(core, wide_kept, swap(wide_sent, 1), sizes[0], 2, "lay_out_wide", [thin_kept])
    thin = split(spots[1:], thin_kept, swap(thin_sent, 1), sizes[1], "split_thin", [wide])
    grad_q, grad_logits, by_logits = query_grads(mix_w, mix_l, soft, v, g_t, k_t, q_t, [wide, thin[0]])
    wide, thin = reshare(spots, trade(wide, plane), exchange(thin, line), [grad_q])
    grad_k = key_grads(mix_l, grad_logits, q, [wide[0]])
    pair_kept, pair_sent = project_weight_grads(core, normed_t, [grad_q, grad_k])
    out = hand_on(out)
    piece, _ = piece_of(spots, exchange(wide, line), trade(thin, plane), [grad_k], [])
    pieces = lax.all_gather(finish_sum(piece, others), BOTH, axis=0)
    pair_kept, pair_sent = project_weight_grads(core, normed_t, [grad_q, grad_k], (), [piece])
    pair = split(spots[:1], pair_kept, swap(pair_sent, 1), sizes[0], "split_pair")
    grad_v, by_weights = value_grads(mix_w, soft, v, g, [piece, pair[0]])
    pair = exchange(pair, plane)
    one_kept, one_sent = project_weight_grads(core, normed_t, [grad_v], [by_logits, by_weights], pair[1:])
    one = split_small(spots[:1], one_kept, swap(one_sent, 1), sizes[0], "split_one")
    grad_in = input_grads(
        at, parts, grad_q, grad_k, grad_v, x, grad_middle, w_query, w_key, w_value, gain_one, one[0])
    shares, grad_in = project_reshare(spots, pair, exchange(one, plane), sizes[1], grad_in)
    own, small = project_piece(spots, exchange(shares, line))
    own, small = finish_sum(own, others)[None], finish_sum(small, others)
    block_out = tokens_of(at, out, "block_out")
    grad_in = send_tokens(grad_in)
    own = widen(spots, own, line, "stack_line", [block_out, *grad_in[1:]])
    grad_w_back, grad_w_hidden, grad_w_out, grad_gain_two = fill(
        pieces, (row_starts(plane, line), row_starts(line, plane)), w_hidden, gain_two)
    grad_inputs = tokens_of(at, hand_on(grad_in), "grad_inputs", [grad_w_out])
    own = widen(spots, own, plane, "stack_plane", [grad_w_out])
    grad_w_query, grad_w_key, grad_w_value, grad_gain_one = spread(
        where, sizes, own, swap(own, 1), w_query, w_key, w_value, gain_one, [grad_w_out])
    small = small[:, : 3 * 128].reshape(SMALL_ROWS, 3, 128).transpose(1, 0, 2).reshape(2, H, 128)[:, :, :H]
    return (
        block_out,
        grad_inputs,
        grad_gain_one.reshape(D),
        grad_w_query,
        grad_w_key,
        grad_w_value,
        grad_w_out,
        small[0].T * scale,
        small[1],
        grad_gain_two.reshape(D),
        grad_w_hidden,
        grad_w_back,
    )


def solution(mesh):
    sharded, copied = P("rows", "seq", None), P()
    in_specs = (sharded, P("rows", None)) + (copied,) * 10 + (sharded,)
    out_specs = (sharded, sharded) + (copied,) * 10
    return jax.shard_map(
        per_device, mesh=mesh, in_specs=in_specs, out_specs=out_specs, check_vma=False
    )
```

```python
from functools import partial

from jax import lax
import jax
import jax.numpy as jnp
from jax.experimental import pallas as pl
from jax.experimental.pallas import tpu as pltpu
from jax.sharding import PartitionSpec as P

D, H, DH, LEN, TILE = 768, 12, 64, 1024, 256
TILES = LEN // TILE
F32, BF16 = jnp.float32, jnp.bfloat16
FORWARD_HEADS, BACKWARD_HEADS = 4, 2
VMEM_LIMIT = 60 * 1024 * 1024
MATMUL_FLOPS = 2 * H * 10 * TILE * TILE * D


def span(i):
    return slice(i * TILE, (i + 1) * TILE)


def head_rows(h):
    return slice(h * DH, (h + 1) * DH)


def mm(a, b):
    return jnp.dot(a, b, preferred_element_type=F32)


def whole(shape):
    return pl.BlockSpec(shape, lambda i: (0,) * len(shape), pipeline_mode=pl.Buffered(1))


def some_heads(count, shape):
    return pl.BlockSpec((count,) + shape, lambda i: (i,) + (0,) * len(shape))


SMEM = pl.BlockSpec(memory_space=pltpu.SMEM)


def params():
    return pltpu.CompilerParams(dimension_semantics=("arbitrary",), vmem_limit_bytes=VMEM_LIMIT)


def shape(s, t=BF16):
    return jax.ShapeDtypeStruct(s, t)


def attend_kernel(mix_l, mix_w, id_row, id_col, q_t, k, v_t, soft, out, bias, scaled, acc):
    step = pl.program_id(0)

    @pl.when(step == 0)
    def start():
        acc[...] = jnp.zeros_like(acc)
        for t in range(TILES):
            for u in range(t + 1):
                allowed = id_col[span(u), :] == id_row[:, span(t)]
                if u == t:
                    key = lax.broadcasted_iota(jnp.int32, (TILE, TILE), 0)
                    query = lax.broadcasted_iota(jnp.int32, (TILE, TILE), 1)
                    allowed = allowed & (key <= query)
                bias[span(u), span(t)] = jnp.where(allowed, 0.0, -1e30)

    for i in range(FORWARD_HEADS):
        j = step * FORWARD_HEADS + i
        for h in range(H):
            scaled[i, head_rows(h), :] = (q_t[head_rows(h), :].astype(F32) * mix_l[h, j]).astype(BF16)
        for t in reversed(range(TILES)):
            n = (t + 1) * TILE
            logits = mm(k[:n, :], scaled[i, :, span(t)]) + bias[:n, span(t)]
            e = jnp.exp(logits - jnp.max(logits, axis=0, keepdims=True))
            p = (e * (1.0 / jnp.sum(e, axis=0, keepdims=True))).astype(BF16)
            soft[i, :n, span(t)] = p
            part = mm(v_t[:, :n], p)
            for h in range(H):
                acc[head_rows(h), span(t)] += part[head_rows(h), :] * mix_w[j, h]

    @pl.when(step == H // FORWARD_HEADS - 1)
    def finish():
        for t in range(TILES):
            out[span(t), :] = acc[:, span(t)].T.astype(BF16)


def attend(mix_l, mix_w, ids, q_t, k, v_t):
    heads = FORWARD_HEADS
    return pl.pallas_call(
        attend_kernel,
        grid=(H // heads,),
        in_specs=[SMEM, SMEM, whole((1, LEN)), whole((LEN, 1)), whole((D, LEN)), whole((LEN, D)), whole((D, LEN))],
        out_specs=[some_heads(heads, (LEN, LEN)), whole((LEN, D))],
        out_shape=[shape((H, LEN, LEN)), shape((LEN, D))],
        scratch_shapes=[
            pltpu.VMEM((LEN, LEN), F32), pltpu.VMEM((heads, D, LEN), BF16), pltpu.VMEM((D, LEN), F32)
        ],
        compiler_params=params(),
        cost_estimate=pl.CostEstimate(flops=MATMUL_FLOPS // 4, bytes_accessed=LEN * LEN, transcendentals=0),
        name="attend",
    )(mix_l, mix_w, ids.reshape(1, LEN), ids.reshape(LEN, 1), q_t, k, v_t)


def head_row(weight_of):
    head = lax.broadcasted_iota(jnp.int32, (1, D), 1) // DH
    row = jnp.full((1, D), weight_of(0), F32)
    for h in range(1, H):
        row = jnp.where(head == h, weight_of(h), row)
    return row


def value_grads_kernel(mix_w, soft, v, g, *rest):
    out, mix_grad, acc = rest[-3:]
    step = pl.program_id(0)

    @pl.when(step == 0)
    def start():
        acc[...] = jnp.zeros_like(acc)

    for i in range(BACKWARD_HEADS):
        total = jnp.zeros((1, D), F32)
        mix_row = head_row(lambda h: mix_w[step * BACKWARD_HEADS + i, h])
        for u in range(TILES):
            part = mm(soft[i, span(u), u * TILE :], g[u * TILE :, :])
            acc[span(u), :] += part * mix_row
            total = total + jnp.sum(part * v[span(u), :].astype(F32), axis=0, keepdims=True)
        mix_grad[i] = total

    @pl.when(step == H // BACKWARD_HEADS - 1)
    def finish():
        out[...] = acc[...].astype(BF16)


def query_grads_kernel(heads, mix_w, mix_l, soft, v, g_t, k_t, q_t, *rest):
    before, (out, grad_logits, mix_grad, acc, scaled) = rest[0], rest[-5:]
    step = pl.program_id(0)
    first_head = heads[0] + step * BACKWARD_HEADS

    @pl.when(step == 0)
    def start():
        acc[...] = before[...] if heads[0] else jnp.zeros_like(acc)

    for i in range(BACKWARD_HEADS):
        j = first_head + i
        for h in range(H):
            scaled[i, head_rows(h), :] = (g_t[head_rows(h), :].astype(F32) * mix_w[j, h]).astype(BF16)
    order = [(i, t) for i in range(BACKWARD_HEADS) for t in reversed(range(TILES))]

    def grad_soft(i, t):
        return mm(v[: (t + 1) * TILE, :], scaled[i, :, span(t)])

    coming = grad_soft(*order[0])
    total = jnp.zeros((D, 128), F32)
    for at, (i, t) in enumerate(order):
        n = (t + 1) * TILE
        p = soft[i, :n, span(t)].astype(F32)
        weighted = p * coming
        low = (weighted - p * jnp.sum(weighted, axis=0, keepdims=True)).astype(BF16)
        grad_logits[i, :n, span(t)] = low
        if at + 1 < len(order):
            coming = grad_soft(*order[at + 1])
        part = mm(k_t[:, :n], low)
        for h in range(H):
            acc[head_rows(h), span(t)] += part[head_rows(h), :] * mix_l[h, first_head + i]
        product = part * q_t[:, span(t)].astype(F32)
        total = total + product[:, :128] + product[:, 128:]
        if t == 0:
            mix_grad[i] = jnp.sum(total.T, axis=0, keepdims=True)
            total = jnp.zeros((D, 128), F32)

    @pl.when(step == pl.num_programs(0) - 1)
    def finish():
        if heads[1] < H:
            out[...] = acc[...]
        else:
            for t in range(TILES):
                out[span(t), :] = acc[:, span(t)].T.astype(BF16)


def key_grads_kernel(mix_l, grad_logits, q, *rest):
    out, acc = rest[-2:]
    step = pl.program_id(0)

    @pl.when(step == 0)
    def start():
        acc[...] = jnp.zeros_like(acc)

    for i in range(BACKWARD_HEADS):
        mix_row = head_row(lambda h: mix_l[h, step * BACKWARD_HEADS + i])
        for u in range(TILES):
            acc[span(u), :] += mm(grad_logits[i, span(u), u * TILE :], q[u * TILE :, :]) * mix_row

    @pl.when(step == H // BACKWARD_HEADS - 1)
    def finish():
        out[...] = acc[...].astype(BF16)


def back_call(kernel, heads, in_specs, out_specs, out_shape, scratch, matmuls, name):
    def run(*operands):
        *used, first = operands
        return pl.pallas_call(
            kernel,
            grid=(heads // BACKWARD_HEADS,),
            in_specs=in_specs + [pl.BlockSpec(memory_space=pl.ANY)] * len(first),
            out_specs=out_specs,
            out_shape=out_shape,
            scratch_shapes=scratch,
            compiler_params=params(),
            cost_estimate=pl.CostEstimate(
                flops=matmuls * MATMUL_FLOPS * heads // H // 8, bytes_accessed=LEN * LEN, transcendentals=0
            ),
            name=name,
        )(*used, *first)

    return run


ROW, COLUMN = whole((LEN, D)), whole((D, LEN))
PER_HEAD, PER_HEAD_ROW = some_heads(BACKWARD_HEADS, (LEN, LEN)), some_heads(BACKWARD_HEADS, (1, D))


def value_grads(mix_w, soft, v, g, first):
    grads, mix_grad = back_call(
        value_grads_kernel,
        H,
        [SMEM, PER_HEAD, ROW, ROW],
        [ROW, PER_HEAD_ROW],
        [shape((LEN, D)), shape((H, 1, D), F32)],
        [pltpu.VMEM((LEN, D), F32)],
        1,
        "value_grads",
    )(mix_w, soft, v, g, first)
    return grads, mix_grad


def query_grads(mix_w, mix_l, soft, v, g_t, k_t, q_t, first, heads=(0, H), before=()):
    low, high = heads
    count, last = high - low, high == H
    per_head = pl.BlockSpec((BACKWARD_HEADS, LEN, LEN), lambda i: (i + low // BACKWARD_HEADS, 0, 0))
    grads, grad_logits, mix_grad = back_call(
        partial(query_grads_kernel, heads),
        count,
        [SMEM, SMEM, per_head, ROW, COLUMN, COLUMN, COLUMN] + [COLUMN] * len(before),
        [ROW if last else COLUMN, PER_HEAD, PER_HEAD_ROW],
        [shape((LEN, D)) if last else shape((D, LEN), F32), shape((count, LEN, LEN)), shape((count, 1, D), F32)],
        [pltpu.VMEM((D, LEN), F32), pltpu.VMEM((BACKWARD_HEADS, D, LEN), BF16)],
        2,
        "query_grads",
    )(mix_w, mix_l, soft, v, g_t, k_t, q_t, *before, first)
    return grads, grad_logits, mix_grad


def key_grads(mix_l, grad_logits, q, first):
    return back_call(
        key_grads_kernel, H, [SMEM, PER_HEAD, ROW], ROW, shape((LEN, D)), [pltpu.VMEM((LEN, D), F32)], 1,
        "key_grads",
    )(mix_l, grad_logits, q, first)


epsilon = 1e-06
GELU_SCALE = 0.7978845608028654
GELU_CUBIC = 0.044715
FEED_COLUMNS = 1024
COST_SHARE = 4
HALF = D // 2
ANY = pl.BlockSpec(memory_space=pl.ANY)
VMEM = pl.BlockSpec(memory_space=pltpu.VMEM)


def against(left, right):
    return lax.dot_general(left, right, (((1,), (1,)), ((), ())), preferred_element_type=F32)


def across(left, right):
    return lax.dot_general(left, right, (((0,), (0,)), ((), ())), preferred_element_type=F32)


def inverse_rms(values):
    return lax.rsqrt(jnp.mean(values * values, axis=-1, keepdims=True) + epsilon)


def cost(matrices):
    return pl.CostEstimate(flops=int(matrices * LEN * D * D) // COST_SHARE, bytes_accessed=LEN * D, transcendentals=0)


def fixed(s):
    return pl.BlockSpec(s, lambda i, at: (0,) * len(s), pipeline_mode=pl.Buffered(1))


def tokens(rows, shift=0):
    return pl.BlockSpec((rows, D), lambda i, at: (at[0] ^ (i + shift), 0))


def tokens_t(columns, shift=0):
    return pl.BlockSpec((D, columns), lambda i, at: (0, at[0] ^ (i + shift)))


def step_call(kernel, at, steps, in_specs, operands, out_specs, out_shape, matrices, name, scratch=(), aliases=None):
    return pl.pallas_call(
        kernel,
        grid_spec=pltpu.PrefetchScalarGridSpec(
            num_scalar_prefetch=1, grid=(steps,), in_specs=in_specs, out_specs=out_specs, scratch_shapes=list(scratch)),
        out_shape=out_shape,
        input_output_aliases=aliases or {},
        compiler_params=params(),
        cost_estimate=cost(matrices),
        name=name,
    )(at, *operands)


def chosen(refs, step):
    values = refs[0][...]
    for i, ref in enumerate(refs[1:]):
        values = jnp.where(step == i + 1, ref[...], values)
    return values


def write_parts(outs, step, values):
    for i, out in enumerate(outs[:-1]):

        @pl.when(step == i)
        def write():
            out[...] = values

    far = outs[-1].shape[0]
    for i in range(far):

        @pl.when(step == len(outs) - 1 + i)
        def write_far():
            outs[-1][i] = values


def part_outs(parts, rows):
    near = parts // 2
    specs = [fixed((rows, D))] * near + [fixed((parts - near, rows, D))]
    return specs, [shape((rows, D))] * near + [shape((parts - near, rows, D))]


def project_kernel(steps, waits, shares, at, *refs):
    parts, (gain, w_query, w_key, w_value) = refs[:steps], refs[steps : steps + 4]
    rest = refs[steps + 4 + waits :]
    cotangent, rest = (rest[0], rest[1:]) if shares else (None, rest)
    row, normed_t, q, q_t, k, k_t, v, v_t = rest[:8]
    step = pl.program_id(0)
    low = chosen(parts, step)
    row[...] = low
    values = low.astype(F32)
    normed = (values * inverse_rms(values) * gain[...]).astype(BF16)
    normed_t[...] = normed.T
    for weight, out, out_t in ((w_query, q, q_t), (w_key, k, k_t), (w_value, v, v_t)):
        part = mm(normed, weight[...]).astype(BF16)
        out[...] = part
        out_t[...] = part.T
    if shares:

        @pl.when(step == 0)
        def lay_out():
            for i, out in enumerate(rest[8:]):
                out[...] = cotangent[at[0] ^ i]


def project(at, parts, shift, gain, w_query, w_key, w_value, before=(), cotangent=None):
    count, rows = len(parts), parts[0].shape[0]
    square, ways = fixed((D, D)), 0 if cotangent is None else cotangent.shape[0]
    row, column = (tokens(rows, shift), shape((LEN, D))), (tokens_t(rows, shift), shape((D, LEN)))
    outs = [row, column, row, column, row, column, row, column] + [(fixed((rows, D)), shape((rows, D)))] * ways
    start = 1 + count + 4
    return step_call(
        partial(project_kernel, count, len(before), ways > 0), at, count,
        [fixed((rows, D))] * count + [fixed((1, D)), square, square, square] + [ANY] * len(before)
        + [fixed((ways, rows, D))] * (ways > 0),
        (*parts, gain, w_query, w_key, w_value, *before) + ((cotangent,) if ways else ()),
        [o[0] for o in outs], [o[1] for o in outs], 3 * count / 4, "project",
        aliases={start + i: i for i in range(len(before))})


def feed_kernel(parts, at, x, attended, *refs):
    cots, (w_out, w_hidden, w_back, gain), rest = refs[:parts], refs[parts : parts + 4], refs[parts + 4 :]
    outs, (cot_row, normed_two, activated, grad_hidden, grad_middle, grad_attn, g, g_t) = rest[:-8], rest[-8:]
    step = pl.program_id(0)
    scale = gain[...]
    cotangent = chosen(cots, step)
    cot_row[...] = cotangent
    middle = x[...].astype(F32) + mm(attended[...], w_out[...])
    inverse = inverse_rms(middle)
    n2 = (middle * inverse * scale).astype(BF16)
    normed_two[...] = n2
    total = middle
    grad_n2 = jnp.zeros_like(middle)
    width = FEED_COLUMNS
    for c in range(w_hidden.shape[1] // width):
        cols = slice(c * width, (c + 1) * width)
        hidden = mm(n2, w_hidden[:, cols])
        grad_act = against(cotangent, w_back[cols, :])
        squared = hidden * hidden
        tanh = jnp.tanh(GELU_SCALE * hidden * (1.0 + GELU_CUBIC * squared))
        half = 0.5 + 0.5 * tanh
        act = (hidden * half).astype(BF16)
        activated[:, cols] = act
        slope = half + (0.5 * GELU_SCALE) * hidden * (1.0 - tanh * tanh) * (1.0 + 3.0 * GELU_CUBIC * squared)
        grad = (grad_act * slope).astype(BF16)
        grad_hidden[:, cols] = grad
        total = total + mm(act, w_back[cols, :])
        grad_n2 = grad_n2 + against(grad, w_hidden[:, cols])
    low = total.astype(BF16)
    write_parts(outs, step, low)
    weighted = grad_n2 * scale
    mean = jnp.mean(weighted * middle, axis=-1, keepdims=True)
    grad_mid = cotangent.astype(F32) + inverse * weighted - middle * (inverse * inverse * inverse * mean)
    grad_middle[...] = grad_mid
    grad_low = grad_mid.astype(BF16)
    grad_attn[...] = grad_low
    grad = against(grad_low, w_out[...]).astype(BF16)
    g[...] = grad
    g_t[...] = grad.T


def feed(at, x, attended, cots, w_out, w_hidden, w_back, gain):
    ff, parts, rows = w_hidden.shape[1], len(cots), cots[0].shape[0]
    tile = (tokens(rows), shape((LEN, D)))
    wide = (pl.BlockSpec((rows, ff), lambda i, at: (at[0] ^ i, 0)), shape((LEN, ff)))
    outs = list(zip(*part_outs(parts, rows))) + [
        tile, tile, wide, wide, (tokens(rows), shape((LEN, D), F32)), tile, tile, (tokens_t(rows), shape((D, LEN)))]
    found = step_call(
        partial(feed_kernel, parts), at, parts,
        [tokens(rows), tokens(rows)] + [fixed((rows, D))] * parts
        + [fixed((D, D)), fixed((D, ff)), fixed((ff, D)), fixed((1, D))],
        (x, attended, *cots, w_out, w_hidden, w_back, gain), [o[0] for o in outs], [o[1] for o in outs],
        2 + 4 * ff // D, "feed")
    return found[:-8], found[-8:]


def input_kernel(parts, at, grad_q, grad_k, grad_v, x, grad_middle, w_query, w_key, w_value, gain, first, *outs):
    upstream = against(grad_q[...], w_query[...]) + against(grad_k[...], w_key[...]) + against(grad_v[...], w_value[...])
    values = x[...].astype(F32)
    inverse = inverse_rms(values)
    weighted = upstream * gain[...]
    mean = jnp.mean(weighted * values, axis=-1, keepdims=True)
    low = (grad_middle[...] + inverse * weighted - values * (inverse * inverse * inverse * mean)).astype(BF16)
    write_parts(outs, pl.program_id(0), low)


def input_grads(at, parts, grad_q, grad_k, grad_v, x, grad_middle, w_query, w_key, w_value, gain, first):
    rows, square = LEN // parts, fixed((D, D))
    return step_call(
        partial(input_kernel, parts), at, parts, [tokens(rows)] * 5 + [square, square, square, fixed((1, D)), ANY],
        (grad_q, grad_k, grad_v, x, grad_middle, w_query, w_key, w_value, gain, first),
        *part_outs(parts, rows), 3, "input_grads")


def both_halves(kept, sent, product, left_kept, left_sent, right):
    kept[0, :HALF] = product(left_kept[...], right[...]).astype(BF16)
    sent[0, :HALF] = product(left_sent[...], right[...]).astype(BF16)


def wide_kernel(backs, core, act_kept, act_sent, cot, n2_kept, n2_sent, grad_hidden, kept, sent):
    step = pl.program_id(0)
    pl.when(step < backs)(partial(both_halves, kept, sent, across, act_kept, act_sent, cot))
    pl.when(step >= backs)(partial(both_halves, kept, sent, across, n2_kept, n2_sent, grad_hidden))


def thin_kernel(hiddens, core, n2_kept, n2_sent, grad_hidden, att_kept, att_sent, grad_attn, *refs):
    step, (kept, sent) = pl.program_id(0), refs[-2:]
    pl.when(step < hiddens)(partial(both_halves, kept, sent, across, n2_kept, n2_sent, grad_hidden))
    pl.when(step >= hiddens)(partial(both_halves, kept, sent, across, att_kept, att_sent, grad_attn))


def columns_half(other, at=lambda i: 0):
    return pl.BlockSpec((LEN, HALF), lambda i, core: (0, 2 * at(i) + (core[0] ^ other)))


def rows_half(other):
    return pl.BlockSpec((HALF, LEN), lambda i, core: (core[0] ^ other, 0))


def wide_and_thin(blocks):
    count = 2 * blocks + 1
    return 2 * count // 3, count - 2 * count // 3


def wide_weight_grads(core, activated, cot, normed_two, grad_hidden):
    blocks = activated.shape[1] // D
    count, _ = wide_and_thin(blocks)
    row, half = fixed((LEN, D)), pl.BlockSpec((1, HALF, D), lambda i, core: (i, 0, 0))

    def back(i):
        return jnp.minimum(i, blocks - 1)

    return step_call(
        partial(wide_kernel, blocks), core, count,
        [columns_half(0, back), columns_half(1, back), row, columns_half(0), columns_half(1),
         pl.BlockSpec((LEN, D), lambda i, core: (0, jnp.maximum(i - blocks, 0)))],
        (activated, activated, cot, normed_two, normed_two, grad_hidden),
        [half, half], [shape((count, HALF, D))] * 2, count, "wide_weight_grads")


def thin_weight_grads(core, normed_two, grad_hidden, attended, grad_attn, first):
    blocks = grad_hidden.shape[1] // D
    count, left = wide_and_thin(blocks)
    row, half = fixed((LEN, D)), pl.BlockSpec((1, HALF, D), lambda i, core: (i, 0, 0))
    return step_call(
        partial(thin_kernel, left - 1), core, left,
        [columns_half(0), columns_half(1),
         pl.BlockSpec((LEN, D), lambda i, core: (0, jnp.minimum(i + count - blocks, blocks - 1))),
         columns_half(0), columns_half(1), row] + [ANY] * len(first),
        (normed_two, normed_two, grad_hidden, attended, attended, grad_attn, *first),
        [half, half], [shape((left, HALF, D))] * 2, left, "thin_weight_grads")


SMALL_ROWS = 8


def small_sums(by_logits, by_weights):
    rows = jnp.concatenate([by_logits[:, 0, :], by_weights[:, 0, :]])
    head = lax.broadcasted_iota(jnp.int32, (D, 128), 0) // DH
    select = (head == lax.broadcasted_iota(jnp.int32, (D, 128), 1)).astype(F32)
    sums = jnp.dot(rows, select, precision=lax.Precision.HIGHEST, preferred_element_type=F32)
    groups = [sums[r : r + SMALL_ROWS, :] for r in range(0, 2 * H, SMALL_ROWS)]
    return jnp.concatenate(groups + [jnp.zeros((SMALL_ROWS, D - 128 * len(groups)), F32)], axis=1)


def project_weights_kernel(count, waits, core, nt_kept, nt_sent, *refs):
    grads, small, (kept, sent) = refs[:count], refs[count : -2 - waits], refs[-2:]
    for i, each in enumerate(grads):
        pl.when(pl.program_id(0) == i)(partial(both_halves, kept, sent, mm, nt_kept, nt_sent, each))
    if small:
        rows = jnp.concatenate([small_sums(*small), jnp.zeros((SMALL_ROWS, D), F32)]).astype(BF16)
        kept[0, HALF:] = rows
        sent[0, HALF:] = rows


def project_weight_grads(core, normed_t, grads, small=(), first=()):
    count, rows = len(grads), HALF + 2 * SMALL_ROWS * (len(small) > 0)
    half = pl.BlockSpec((1, rows, D), lambda i, core: (i, 0, 0))
    return step_call(
        partial(project_weights_kernel, count, len(first)), core, count,
        [rows_half(0), rows_half(1)] + [fixed((LEN, D))] * count + [fixed((H, 1, D))] * len(small) + [ANY] * len(first),
        (normed_t, normed_t, *grads, *small, *first), [half, half], [shape((count, rows, D))] * 2, count, "project_weight_grads")


def split_kernel(waits, mine, kept, came, *refs):
    outs, total = refs[waits:-1], refs[-1]
    total[...] = kept[...].astype(F32) + came[...].astype(F32)
    for c, out in enumerate(outs):
        rows = out.shape[1]
        out[...] = total[:, pl.ds(pl.multiple_of((mine[0] ^ c) * rows, 8), rows), :].astype(BF16)


def split(mine, kept, came, ways, name, first=()):
    count, rows, _ = kept.shape
    block = pl.BlockSpec((1, rows, D), lambda m, mine: (m, 0, 0))
    return step_call(
        partial(split_kernel, len(first)), mine, count, [block, block] + [ANY] * len(first), (kept, came, *first),
        [pl.BlockSpec((1, rows // ways, D), lambda m, mine: (m, 0, 0))] * ways,
        [shape((count, rows // ways, D))] * ways, 0, name, [pltpu.VMEM((1, rows, D), F32)])


def shares_kernel(wide_steps, mine, wide_kept, wide_came, thin_kept, thin_came, wide, *refs):
    thin, total, step = refs[:-1], refs[-1], pl.program_id(0)

    @pl.when(step < wide_steps)
    def of_wide():
        rows = wide.shape[2]
        for m in range(wide_kept.shape[0]):
            sums = wide_kept[m].astype(F32) + wide_came[m].astype(F32)
            for c in range(wide.shape[0]):
                wide[c, m] = sums[c * rows : (c + 1) * rows, :].astype(BF16)

    @pl.when(step >= wide_steps)
    def of_thin():
        total[...] = thin_kept[...].astype(F32) + thin_came[...].astype(F32)
        for c, out in enumerate(thin):
            rows = out.shape[1]
            out[...] = total[:, pl.ds(pl.multiple_of((mine[0] ^ c) * rows, 8), rows), :].astype(BF16)


def shares_of(mine, wide_kept, wide_came, thin_kept, thin_came, plane, line, first):
    count, left = wide_kept.shape[0], thin_kept.shape[0]
    per_step = 2
    steps = count // per_step

    def of_wide(m, mine):
        return jnp.minimum(m, steps - 1)

    half = pl.BlockSpec((per_step, HALF, D), lambda m, mine: (of_wide(m, mine), 0, 0))
    thin_half = fixed((left, HALF, D))
    outs = step_call(
        lambda mine, a, b, c, d, *refs: shares_kernel(steps, mine, a, b, c, d, *refs[len(first) :]), mine, steps + 1,
        [half, half, thin_half, thin_half] + [ANY] * len(first), (wide_kept, wide_came, thin_kept, thin_came, *first),
        [pl.BlockSpec((plane, per_step, HALF // plane, D), lambda m, mine: (0, of_wide(m, mine), 0, 0))]
        + [fixed((left, HALF // line, D))] * line,
        [shape((plane, count, HALF // plane, D))] + [shape((left, HALF // line, D))] * line, 0, "shares",
        [pltpu.VMEM((left, HALF, D), F32)])
    return outs[0], outs[1:]


def plain_call(kernel, operands, mine, out_shape, name, scratch=(), first=(), through=()):
    outs = pl.pallas_call(
        kernel,
        in_specs=[SMEM] + [VMEM] * len(operands) + [ANY] * (len(first) + len(through)),
        out_specs=[VMEM] * len(out_shape) + [ANY] * len(through),
        out_shape=list(out_shape) + [shape(t.shape, t.dtype) for t in through],
        input_output_aliases={1 + len(operands) + len(first) + i: len(out_shape) + i for i in range(len(through))},
        scratch_shapes=list(scratch),
        compiler_params=pltpu.CompilerParams(vmem_limit_bytes=VMEM_LIMIT),
        name=name,
    )(mine, *operands, *first, *through)
    return outs[: len(out_shape)], outs[len(out_shape) :]


def added(refs):
    return sum(ref[...].astype(F32) for ref in refs)


def sum_first(ref):
    return sum(ref[i].astype(F32) for i in range(ref.shape[0]))


def reshare_kernel(line, waits, mine, wide, *refs):
    thin, outs, total = refs[:line], refs[line + waits :], refs[-1]
    total[...] = sum_first(wide)
    for c in range(line):
        rows = outs[c].shape[1]
        outs[c][...] = total[:, pl.ds(pl.multiple_of((mine[1] ^ c) * rows, 8), rows), :].astype(BF16)
    out = outs[line]
    thin_sum, rows = added(thin), out.shape[2]
    for c in range(out.shape[0]):
        out[c] = thin_sum[:, c * rows : (c + 1) * rows, :].astype(BF16)


def reshare(mine, wide, thin, first, through):
    plane, count, rows, _ = wide.shape
    line, (left, thin_rows, _) = len(thin), thin[0].shape
    outs, through = plain_call(
        partial(reshare_kernel, line, len(first) + len(through)), [wide, *thin], mine,
        [shape((count, rows // line, D))] * line + [shape((plane, left, thin_rows // plane, D))], "reshare",
        [pltpu.VMEM((count, rows, D), F32)], first, through)
    return outs[:line], outs[line], through


def piece_kernel(line, waits, mine, thin, *refs):
    wide, out = refs[:line], refs[line + waits]
    count = wide[0].shape[0]
    out[:count] = added(wide).astype(BF16)
    out[count:] = sum_first(thin).astype(BF16)


def piece_of(mine, wide, thin, first, through):
    (count, rows, _), left = wide[0].shape, thin.shape[1]
    (out,), through = plain_call(
        partial(piece_kernel, len(wide), len(first) + len(through)), [thin, *wide], mine,
        [shape((count + left, rows, D))], "piece", (), first, through)
    return out, through


def split_small_kernel(mine, kept, came, *refs):
    outs, total, share = refs[:-2], refs[-2], refs[-1]
    total[...] = kept[0].astype(F32) + came[0].astype(F32)
    rows = share.shape[0] - SMALL_ROWS
    share[rows:] = total[HALF : HALF + SMALL_ROWS, :]
    for c, out in enumerate(outs):
        share[:rows] = total[pl.ds(pl.multiple_of((mine[0] ^ c) * rows, 8), rows), :]
        out[...] = share[...].astype(BF16)


def split_small(mine, kept, came, ways, name):
    rows = HALF // ways + SMALL_ROWS
    outs, _ = plain_call(
        split_small_kernel, [kept, came], mine, [shape((rows, D))] * ways, name,
        [pltpu.VMEM(kept.shape[1:], F32), pltpu.VMEM((rows, D), F32)])
    return outs


def project_reshare_kernel(ways, waits, mine, *refs):
    line, through = waits
    pairs, ones, outs = refs[:ways], refs[ways : 2 * ways], refs[2 * ways + through : 2 * ways + through + line]
    pair, one, share = refs[-3:]
    pair[...] = added(pairs)
    one[...] = added(ones)
    rows = pair.shape[1] // len(outs)
    share[3 * rows :] = one[pair.shape[1] :, :]
    for c, out in enumerate(outs):
        start = pl.multiple_of((mine[1] ^ c) * rows, 8)
        share[:rows] = pair[0, pl.ds(start, rows), :]
        share[rows : 2 * rows] = pair[1, pl.ds(start, rows), :]
        share[2 * rows : 3 * rows] = one[pl.ds(start, rows), :]
        out[...] = share[...].astype(BF16)


def project_reshare(mine, pairs, ones, ways, through):
    rows = 3 * pairs[0].shape[1] // ways + SMALL_ROWS
    return plain_call(
        partial(project_reshare_kernel, len(pairs), (ways, len(through))), [*pairs, *ones], mine,
        [shape((rows, D))] * ways, "project_reshare",
        [pltpu.VMEM(pairs[0].shape, F32), pltpu.VMEM(ones[0].shape, F32), pltpu.VMEM((rows, D), F32)], (), through)


def project_piece_kernel(mine, *refs):
    parts, (out, small, total) = refs[:-3], refs[-3:]
    total[...] = added(parts)
    rows = out.shape[1]
    for m in range(3):
        out[m] = total[m * rows : (m + 1) * rows, :].astype(BF16)
    small[...] = total[3 * rows :, :]


def project_piece(mine, parts):
    rows = parts[0].shape[0]
    (out, small), _ = plain_call(
        project_piece_kernel, list(parts), mine,
        [shape((3, (rows - SMALL_ROWS) // 3, D)), shape((SMALL_ROWS, D), F32)], "project_piece",
        [pltpu.VMEM((rows, D), F32)])
    return out, small


def stack_kernel(count, waits, mine, *refs):
    out, at = refs[count + waits], 0
    for ref in refs[:count]:
        out[at : at + ref.shape[0]] = ref[...]
        at += ref.shape[0]


def stack(mine, parts, name, first=()):
    rows = sum(p.shape[0] for p in parts)
    (out,), _ = plain_call(
        partial(stack_kernel, len(parts), len(first)), list(parts), mine, [shape((rows,) + parts[0].shape[1:])], name,
        (), first)
    return out


def tokens_kernel(waits, at, *refs):
    near, near_came, far, forwarded, out = *refs[:4], refs[4 + waits]
    for i, ref in enumerate((near, near_came, far.at[0], forwarded)):
        out[at[0] ^ i] = ref[...]


def tokens_of(at, came, name, first=()):
    (out,), _ = plain_call(
        partial(tokens_kernel, len(first)), list(came), at, [shape((4,) + came[0].shape)], name, (), first)
    return out


def weigh(out, weight):
    product = out[...] * weight[...].astype(F32)
    return sum(product[:, c : c + 128] for c in range(0, D, 128))


def as_row(weighed):
    return jnp.sum(weighed[...].T, axis=0, keepdims=True)


def spread_kernel(sizes, place, own, other, w_query, w_key, w_value, gain, *refs):
    outs, by_gain, weighed = refs[-5:-2], refs[-2], refs[-1]
    matrix = pl.program_id(0)
    plane, line = sizes
    rows = own.shape[2]

    @pl.when(matrix == 0)
    def zero():
        weighed[...] = jnp.zeros_like(weighed)

    for i, (out, weight) in enumerate(zip(outs, (w_query, w_key, w_value))):

        @pl.when(matrix == i)
        def here():
            for c, pieces in enumerate((own, other)):
                for p in range(plane):
                    for n in range(line):
                        at = (place[0] ^ c) * plane * line + (place[1] ^ p) * line + (place[2] ^ n)
                        out[pl.ds(pl.multiple_of(at * rows, 8), rows), :] = pieces[p * line + n, 0].astype(F32)
            weighed[...] += weigh(out, weight)

    @pl.when(matrix == 2)
    def finish():
        by_gain[...] = as_row(weighed) / gain[...]


def matrix_outs(down, over):
    specs, shapes, begin, places = [], [], 0, []
    for d, o in zip(down, over):
        count = d * o

        def place_of(m, *at, begin=begin, count=count, o=o):
            within = jnp.clip(m - begin, 0, count - 1)
            return (within // o, within % o)

        places.append(place_of)
        specs.append(pl.BlockSpec((D, D), place_of))
        shapes.append(shape((d * D, o * D), F32))
        begin += count
    return specs, shapes, begin, places


def spread(place, sizes, own, other, w_query, w_key, w_value, gain, first):
    out_specs, out_shape, count, _ = matrix_outs((1, 1, 1), (1, 1, 1))
    devices, matrices, rows, _ = own.shape
    block = pl.BlockSpec((devices, 1, rows, D), lambda m, place: (0, m, 0, 0))
    square = fixed((D, D))
    return step_call(
        partial(spread_kernel, sizes), place, count, [block, block, square, square, square, fixed((1, D))] + [ANY] * len(first),
        (own, other, w_query, w_key, w_value, gain, *first),
        out_specs + [fixed((1, D))], out_shape + [shape((1, D), F32)], 0, "spread", [pltpu.VMEM((D, 128), F32)])


def fill_kernel(counts, wide_count, starts, pieces, w_hidden, gain, *refs):
    outs, by_gain, weighed = refs[:3], refs[3], refs[4]
    matrix, begin, rows = pl.program_id(0), 0, pieces.shape[2]

    @pl.when(matrix == 0)
    def zero():
        weighed[...] = jnp.zeros_like(weighed)

    for index, (out, count) in enumerate(zip(outs, counts)):
        for table, low, high in ((0, begin, min(begin + count, wide_count)), (1, max(begin, wide_count), begin + count)):
            if low < high:

                @pl.when((matrix >= low) & (matrix < high))
                def here():
                    for device, start in enumerate(starts[table]):
                        out[start : start + rows, :] = pieces[device, 0].astype(F32)
                    if index == 1:
                        weighed[...] += weigh(out, w_hidden)

        begin += count

    @pl.when(matrix == begin - 1)
    def finish():
        by_gain[...] = as_row(weighed) / gain[...]


def fill(pieces, starts, w_hidden, gain):
    blocks = w_hidden.shape[1] // D
    down, over = (blocks, 1, 1), (1, blocks, 1)
    out_specs, out_shape, count, places = matrix_outs(down, over)
    devices, matrices, rows, _ = pieces.shape
    line = whole((1, D))
    return pl.pallas_call(
        partial(fill_kernel, tuple(d * o for d, o in zip(down, over)), wide_and_thin(blocks)[0], starts),
        grid=(count,),
        in_specs=[pl.BlockSpec((devices, 1, rows, D), lambda m: (0, m, 0, 0)), pl.BlockSpec((D, D), places[1]), line],
        out_specs=out_specs + [line],
        out_shape=out_shape + [shape((1, D), F32)],
        scratch_shapes=[pltpu.VMEM((D, 128), F32)],
        compiler_params=params(),
        name="fill",
    )(pieces, w_hidden, gain)


BOTH = ("rows", "seq")


def swap(values, mask):
    n = lax.axis_size("rows") * lax.axis_size("seq")
    return lax.ppermute(values, BOTH, [(s, s ^ mask) for s in range(n)])


def device_bits():
    n = lax.axis_size("rows") * lax.axis_size("seq")
    return [1 << b for b in range(n.bit_length() - 1)]


def masks(dims):
    return [(c, sum(bit for i, bit in enumerate(dims) if c >> i & 1)) for c in range(1 << len(dims))]


def place(dims):
    me = lax.axis_index(BOTH)
    return sum(((me // bit) % 2) << i for i, bit in enumerate(dims))


def exchange(parts, dims):
    return [swap(part, mask) if mask else part for part, (c, mask) in zip(parts, masks(dims))]


def chip_groups():
    chips = device_bits()[1:]
    plane, line, rows = chips[:2], [], HALF >> 2
    for bit in chips[2:]:
        if rows >> (len(line) + 1) << (len(line) + 1) == rows and (rows >> (len(line) + 1)) % 8 == 0:
            line.append(bit)
    return plane, line, chips[2 + len(line) :]


def finish_sum(total, dims):
    for bit in dims:
        total = (total.astype(F32) + swap(total, bit).astype(F32)).astype(total.dtype)
    return total


def row_starts(first, second):
    starts = []
    for device in range(1 << len(device_bits())):
        row, size = 0, D
        for dims in ([1], first, second):
            size >>= len(dims)
            row += size * sum(((device // bit) % 2) << i for i, bit in enumerate(dims))
        starts.append(row)
    return tuple(starts)


def trade(values, dims):
    n = lax.axis_size("rows") * lax.axis_size("seq")
    groups, found = [], set()
    for device in range(n):
        if device not in found:
            group = [device ^ mask for c, mask in masks(dims)]
            found.update(group)
            groups.append(group)
    return lax.all_to_all(values, BOTH, split_axis=0, concat_axis=0, tiled=True, axis_index_groups=groups)


def widen(mine, values, dims, name, first=()):
    return stack(mine, exchange([values] * (1 << len(dims)), dims), name, first)


def send_far(parts):
    return (*parts[:2], swap(parts[2], 2))


def hand_on(parts):
    mine, near, far = parts
    return mine, swap(near, 1), far, swap(far[1], 1)


def per_device(
    inputs,
    segment_ids,
    gain_one,
    w_query,
    w_key,
    w_value,
    w_out,
    mix_logits,
    mix_weights,
    gain_two,
    w_hidden,
    w_back,
    cotangent,
):
    plane, line, others = chip_groups()
    where = jnp.stack([place([1]), place(plane), place(line)])
    core, spots = where[:1], where[1:]
    mixed = plane + line
    pair_plane, pair_line = mixed[1:3], mixed[:1] + mixed[3:]
    pair_spots = jnp.stack([place(pair_plane), place(pair_line)])
    sizes = (1 << len(plane), 1 << len(line))
    parts, seq = lax.axis_size("seq"), lax.axis_index("seq")
    row_bits, at = device_bits()[: parts.bit_length() - 1], seq.reshape(1)
    ids = lax.dynamic_slice_in_dim(segment_ids, seq, 1, 0)
    gain_one, gain_two = gain_one.reshape(1, D), gain_two.reshape(1, D)
    scale = DH ** -0.5
    mix_l = mix_logits.astype(F32) * scale
    mix_w = mix_weights.astype(F32)

    came = exchange([lax.dynamic_index_in_dim(inputs, seq ^ i, 0, keepdims=False) for i in range(parts)], row_bits)
    near = parts // 2
    begun = project(at, came[:near], 0, gain_one, w_query, w_key, w_value, (), cotangent)
    cots = exchange(begun[8:], row_bits)
    x, normed_t, q, q_t, k, k_t, v, v_t = project(
        at, came[near:], near, gain_one, w_query, w_key, w_value, begun[:8])
    soft, attended = attend(mix_l, mix_w, ids, q_t, k, v_t)
    out, (cot, normed_two, activated, grad_hidden, grad_middle, grad_attn, g, g_t) = feed(
        at, x, attended, cots, w_out, w_hidden, w_back, gain_two
    )
    wide_kept, wide_sent = wide_weight_grads(core, activated, cot, normed_two, grad_hidden)
    thin_kept, thin_sent = thin_weight_grads(core, normed_two, grad_hidden, attended, grad_attn, [wide_kept])
    wide, thin = shares_of(
        spots[1:], wide_kept, swap(wide_sent, 1), thin_kept, swap(thin_sent, 1), sizes[0], sizes[1], [thin_kept])
    grad_q, grad_logits, by_logits = query_grads(mix_w, mix_l, soft, v, g_t, k_t, q_t, [wide, thin[0]])
    wide, thin, far = reshare(spots, trade(wide, plane), exchange(thin, line), [grad_q], out[2:])
    out = send_far((*out[:2], *far))
    grad_k = key_grads(mix_l, grad_logits, q, [wide[0]])
    piece, far = piece_of(spots, exchange(wide, line), trade(thin, plane), [grad_k], out[2:])
    out = hand_on((*out[:2], *far))
    pieces = lax.all_gather(finish_sum(piece, others), BOTH, axis=0)
    pair_kept, pair_sent = project_weight_grads(core, normed_t, [grad_q, grad_k], (), [piece])
    pair = split(pair_spots[:1], pair_kept, swap(pair_sent, 1), sizes[0], "split_pair")
    grad_v, by_weights = value_grads(mix_w, soft, v, g, [piece, pair[0]])
    pair = exchange(pair, pair_plane)
    one_kept, one_sent = project_weight_grads(core, normed_t, [grad_v], [by_logits, by_weights], [*pair[1:], out[1], out[3]])
    one = split_small(pair_spots[:1], one_kept, swap(one_sent, 1), sizes[0], "split_one")
    grad_in = input_grads(
        at, parts, grad_q, grad_k, grad_v, x, grad_middle, w_query, w_key, w_value, gain_one, one[0])
    shares, grad_in = project_reshare(pair_spots, pair, exchange(one, pair_plane), sizes[1], grad_in)
    own, small = project_piece(pair_spots, exchange(shares, pair_line))
    own, small = finish_sum(own, others)[None], finish_sum(small, others)
    block_out = tokens_of(at, out, "block_out")
    grad_in = send_far(grad_in)
    own = widen(spots, own, pair_line, "stack_line", [block_out, grad_in[2]])
    grad_w_back, grad_w_hidden, grad_w_out, grad_gain_two = fill(
        pieces, (row_starts(plane, line), row_starts(line, plane)), w_hidden, gain_two)
    grad_inputs = tokens_of(at, hand_on(grad_in), "grad_inputs", [grad_w_out])
    own = widen(spots, own, pair_plane, "stack_plane", [grad_w_out])
    grad_w_query, grad_w_key, grad_w_value, grad_gain_one = spread(
        jnp.stack([core[0], *pair_spots]), sizes, own, swap(own, 1), w_query, w_key, w_value, gain_one, [grad_w_out])
    small = small[:, : 3 * 128].reshape(SMALL_ROWS, 3, 128).transpose(1, 0, 2).reshape(2, H, 128)[:, :, :H]
    return (
        block_out,
        grad_inputs,
        grad_gain_one.reshape(D),
        grad_w_query,
        grad_w_key,
        grad_w_value,
        grad_w_out,
        small[0].T * scale,
        small[1],
        grad_gain_two.reshape(D),
        grad_w_hidden,
        grad_w_back,
    )


def solution(mesh):
    sharded, copied = P("rows", "seq", None), P()
    in_specs = (sharded, P("rows", None)) + (copied,) * 10 + (sharded,)
    out_specs = (sharded, sharded) + (copied,) * 10
    return jax.shard_map(
        per_device, mesh=mesh, in_specs=in_specs, out_specs=out_specs, check_vma=False
    )
```

```python
from functools import partial

from jax import lax
import jax
import jax.numpy as jnp
from jax.experimental import pallas as pl
from jax.experimental.pallas import tpu as pltpu
from jax.sharding import PartitionSpec as P

D, H, DH, LEN, TILE = 768, 12, 64, 1024, 256
TILES = LEN // TILE
F32, BF16 = jnp.float32, jnp.bfloat16
FORWARD_HEADS, BACKWARD_HEADS = 4, 2
VMEM_LIMIT = 60 * 1024 * 1024
LOG2_E = 1.4426950408889634
MATMUL_FLOPS = 2 * H * 10 * TILE * TILE * D


def span(i):
    return slice(i * TILE, (i + 1) * TILE)


def head_rows(h):
    return slice(h * DH, (h + 1) * DH)


def mm(a, b):
    return jnp.dot(a, b, preferred_element_type=F32)


def whole(shape):
    return pl.BlockSpec(shape, lambda i: (0,) * len(shape), pipeline_mode=pl.Buffered(1))


def some_heads(count, shape):
    return pl.BlockSpec((count,) + shape, lambda i: (i,) + (0,) * len(shape))


SMEM = pl.BlockSpec(memory_space=pltpu.SMEM)


def params():
    return pltpu.CompilerParams(dimension_semantics=("arbitrary",), vmem_limit_bytes=VMEM_LIMIT)


def shape(s, t=BF16):
    return jax.ShapeDtypeStruct(s, t)


def attend_kernel(mix_l, mix_w, id_row, id_col, q_t, k, v_t, soft, out, bias, scaled, acc):
    step = pl.program_id(0)

    @pl.when(step == 0)
    def start():
        acc[...] = jnp.zeros_like(acc)
        for t in range(TILES):
            for u in range(t + 1):
                allowed = id_col[span(u), :] == id_row[:, span(t)]
                if u == t:
                    key = lax.broadcasted_iota(jnp.int32, (TILE, TILE), 0)
                    query = lax.broadcasted_iota(jnp.int32, (TILE, TILE), 1)
                    allowed = allowed & (key <= query)
                bias[span(u), span(t)] = jnp.where(allowed, 0.0, -1e30)

    for i in range(FORWARD_HEADS):
        j = step * FORWARD_HEADS + i
        for h in range(H):
            weight = mix_l[h, j] * LOG2_E
            scaled[i, head_rows(h), :] = (q_t[head_rows(h), :].astype(F32) * weight).astype(BF16)
        for t in reversed(range(TILES)):
            n = (t + 1) * TILE
            logits = mm(k[:n, :], scaled[i, :, span(t)]) + bias[:n, span(t)]
            e = jnp.exp2(logits - jnp.max(logits, axis=0, keepdims=True))
            p = (e * (1.0 / jnp.sum(e, axis=0, keepdims=True))).astype(BF16)
            soft[i, :n, span(t)] = p
            part = mm(v_t[:, :n], p)
            for h in range(H):
                acc[head_rows(h), span(t)] += part[head_rows(h), :] * mix_w[j, h]

    @pl.when(step == H // FORWARD_HEADS - 1)
    def finish():
        for t in range(TILES):
            out[span(t), :] = acc[:, span(t)].T.astype(BF16)


def attend(mix_l, mix_w, ids, q_t, k, v_t):
    heads = FORWARD_HEADS
    return pl.pallas_call(
        attend_kernel,
        grid=(H // heads,),
        in_specs=[SMEM, SMEM, whole((1, LEN)), whole((LEN, 1)), whole((D, LEN)), whole((LEN, D)), whole((D, LEN))],
        out_specs=[some_heads(heads, (LEN, LEN)), whole((LEN, D))],
        out_shape=[shape((H, LEN, LEN)), shape((LEN, D))],
        scratch_shapes=[
            pltpu.VMEM((LEN, LEN), F32), pltpu.VMEM((heads, D, LEN), BF16), pltpu.VMEM((D, LEN), F32)
        ],
        compiler_params=params(),
        cost_estimate=pl.CostEstimate(flops=MATMUL_FLOPS // 4, bytes_accessed=LEN * LEN, transcendentals=0),
        name="attend",
    )(mix_l, mix_w, ids.reshape(1, LEN), ids.reshape(LEN, 1), q_t, k, v_t)


def head_row(weight_of):
    head = lax.broadcasted_iota(jnp.int32, (1, D), 1) // DH
    row = jnp.full((1, D), weight_of(0), F32)
    for h in range(1, H):
        row = jnp.where(head == h, weight_of(h), row)
    return row


def value_grads_kernel(mix_w, soft, v, g, *rest):
    out, mix_grad, acc = rest[-3:]
    step = pl.program_id(0)

    @pl.when(step == 0)
    def start():
        acc[...] = jnp.zeros_like(acc)

    for i in range(BACKWARD_HEADS):
        total = jnp.zeros((1, D), F32)
        mix_row = head_row(lambda h: mix_w[step * BACKWARD_HEADS + i, h])
        for u in range(TILES):
            part = mm(soft[i, span(u), u * TILE :], g[u * TILE :, :])
            acc[span(u), :] += part * mix_row
            total = total + jnp.sum(part * v[span(u), :].astype(F32), axis=0, keepdims=True)
        mix_grad[i] = total

    @pl.when(step == H // BACKWARD_HEADS - 1)
    def finish():
        out[...] = acc[...].astype(BF16)


def query_grads_kernel(heads, mix_w, mix_l, soft, v, g_t, k_t, q_t, *rest):
    before, (out, grad_logits, mix_grad, acc, scaled) = rest[0], rest[-5:]
    step = pl.program_id(0)
    first_head = heads[0] + step * BACKWARD_HEADS

    @pl.when(step == 0)
    def start():
        acc[...] = before[...] if heads[0] else jnp.zeros_like(acc)

    for i in range(BACKWARD_HEADS):
        j = first_head + i
        for h in range(H):
            scaled[i, head_rows(h), :] = (g_t[head_rows(h), :].astype(F32) * mix_w[j, h]).astype(BF16)
    order = [(i, t) for i in range(BACKWARD_HEADS) for t in reversed(range(TILES))]

    def grad_soft(i, t):
        return mm(v[: (t + 1) * TILE, :], scaled[i, :, span(t)])

    coming = grad_soft(*order[0])
    total = jnp.zeros((D, 128), F32)
    for at, (i, t) in enumerate(order):
        n = (t + 1) * TILE
        p = soft[i, :n, span(t)].astype(F32)
        weighted = p * coming
        low = (weighted - p * jnp.sum(weighted, axis=0, keepdims=True)).astype(BF16)
        grad_logits[i, :n, span(t)] = low
        if at + 1 < len(order):
            coming = grad_soft(*order[at + 1])
        part = mm(k_t[:, :n], low)
        for h in range(H):
            acc[head_rows(h), span(t)] += part[head_rows(h), :] * mix_l[h, first_head + i]
        product = part * q_t[:, span(t)].astype(F32)
        total = total + product[:, :128] + product[:, 128:]
        if t == 0:
            mix_grad[i] = jnp.sum(total.T, axis=0, keepdims=True)
            total = jnp.zeros((D, 128), F32)

    @pl.when(step == pl.num_programs(0) - 1)
    def finish():
        if heads[1] < H:
            out[...] = acc[...]
        else:
            for t in range(TILES):
                out[span(t), :] = acc[:, span(t)].T.astype(BF16)


def key_grads_kernel(mix_l, grad_logits, q, *rest):
    out, acc = rest[-2:]
    step = pl.program_id(0)

    @pl.when(step == 0)
    def start():
        acc[...] = jnp.zeros_like(acc)

    for i in range(BACKWARD_HEADS):
        mix_row = head_row(lambda h: mix_l[h, step * BACKWARD_HEADS + i])
        for u in range(TILES):
            acc[span(u), :] += mm(grad_logits[i, span(u), u * TILE :], q[u * TILE :, :]) * mix_row

    @pl.when(step == H // BACKWARD_HEADS - 1)
    def finish():
        out[...] = acc[...].astype(BF16)


def back_call(kernel, heads, in_specs, out_specs, out_shape, scratch, matmuls, name):
    def run(*operands):
        *used, first = operands
        return pl.pallas_call(
            kernel,
            grid=(heads // BACKWARD_HEADS,),
            in_specs=in_specs + [pl.BlockSpec(memory_space=pl.ANY)] * len(first),
            out_specs=out_specs,
            out_shape=out_shape,
            scratch_shapes=scratch,
            compiler_params=params(),
            cost_estimate=pl.CostEstimate(
                flops=matmuls * MATMUL_FLOPS * heads // H // 8, bytes_accessed=LEN * LEN, transcendentals=0
            ),
            name=name,
        )(*used, *first)

    return run


ROW, COLUMN = whole((LEN, D)), whole((D, LEN))
PER_HEAD, PER_HEAD_ROW = some_heads(BACKWARD_HEADS, (LEN, LEN)), some_heads(BACKWARD_HEADS, (1, D))


def value_grads(mix_w, soft, v, g, first):
    grads, mix_grad = back_call(
        value_grads_kernel,
        H,
        [SMEM, PER_HEAD, ROW, ROW],
        [ROW, PER_HEAD_ROW],
        [shape((LEN, D)), shape((H, 1, D), F32)],
        [pltpu.VMEM((LEN, D), F32)],
        1,
        "value_grads",
    )(mix_w, soft, v, g, first)
    return grads, mix_grad


def query_grads(mix_w, mix_l, soft, v, g_t, k_t, q_t, first, heads=(0, H), before=()):
    low, high = heads
    count, last = high - low, high == H
    per_head = pl.BlockSpec((BACKWARD_HEADS, LEN, LEN), lambda i: (i + low // BACKWARD_HEADS, 0, 0))
    grads, grad_logits, mix_grad = back_call(
        partial(query_grads_kernel, heads),
        count,
        [SMEM, SMEM, per_head, ROW, COLUMN, COLUMN, COLUMN] + [COLUMN] * len(before),
        [ROW if last else COLUMN, PER_HEAD, PER_HEAD_ROW],
        [shape((LEN, D)) if last else shape((D, LEN), F32), shape((count, LEN, LEN)), shape((count, 1, D), F32)],
        [pltpu.VMEM((D, LEN), F32), pltpu.VMEM((BACKWARD_HEADS, D, LEN), BF16)],
        2,
        "query_grads",
    )(mix_w, mix_l, soft, v, g_t, k_t, q_t, *before, first)
    return grads, grad_logits, mix_grad


def key_grads(mix_l, grad_logits, q, first):
    return back_call(
        key_grads_kernel, H, [SMEM, PER_HEAD, ROW], ROW, shape((LEN, D)), [pltpu.VMEM((LEN, D), F32)], 1,
        "key_grads",
    )(mix_l, grad_logits, q, first)


epsilon = 1e-06
GELU_SCALE = 0.7978845608028654
GELU_CUBIC = 0.044715
FEED_COLUMNS = 768
COST_SHARE = 4
HALF = D // 2
ANY = pl.BlockSpec(memory_space=pl.ANY)
VMEM = pl.BlockSpec(memory_space=pltpu.VMEM)


def against(left, right):
    return lax.dot_general(left, right, (((1,), (1,)), ((), ())), preferred_element_type=F32)


def across(left, right):
    return lax.dot_general(left, right, (((0,), (0,)), ((), ())), preferred_element_type=F32)


def inverse_rms(values):
    return lax.rsqrt(jnp.mean(values * values, axis=-1, keepdims=True) + epsilon)


def cost(matrices):
    return pl.CostEstimate(flops=int(matrices * LEN * D * D) // COST_SHARE, bytes_accessed=LEN * D, transcendentals=0)


def fixed(s):
    return pl.BlockSpec(s, lambda i, at: (0,) * len(s), pipeline_mode=pl.Buffered(1))


def tokens(rows, shift=0):
    return pl.BlockSpec((rows, D), lambda i, at: (at[0] ^ (i + shift), 0))


def tokens_t(columns, shift=0):
    return pl.BlockSpec((D, columns), lambda i, at: (0, at[0] ^ (i + shift)))


def step_call(kernel, at, steps, in_specs, operands, out_specs, out_shape, matrices, name, scratch=(), aliases=None):
    return pl.pallas_call(
        kernel,
        grid_spec=pltpu.PrefetchScalarGridSpec(
            num_scalar_prefetch=1, grid=(steps,), in_specs=in_specs, out_specs=out_specs, scratch_shapes=list(scratch)),
        out_shape=out_shape,
        input_output_aliases=aliases or {},
        compiler_params=params(),
        cost_estimate=cost(matrices),
        name=name,
    )(at, *operands)


def chosen(refs, step):
    values = refs[0][...]
    for i, ref in enumerate(refs[1:]):
        values = jnp.where(step == i + 1, ref[...], values)
    return values


def write_parts(outs, step, values):
    for i, out in enumerate(outs[:-1]):

        @pl.when(step == i)
        def write():
            out[...] = values

    far = outs[-1].shape[0]
    for i in range(far):

        @pl.when(step == len(outs) - 1 + i)
        def write_far():
            outs[-1][i] = values


def part_outs(parts, rows):
    near = parts // 2
    specs = [fixed((rows, D))] * near + [fixed((parts - near, rows, D))]
    return specs, [shape((rows, D))] * near + [shape((parts - near, rows, D))]


def project_kernel(steps, waits, shares, at, *refs):
    parts, (gain, w_query, w_key, w_value) = refs[:steps], refs[steps : steps + 4]
    rest = refs[steps + 4 + waits :]
    cotangent, rest = (rest[0], rest[1:]) if shares else (None, rest)
    row, normed_t, q, q_t, k, k_t, v, v_t = rest[:8]
    step = pl.program_id(0)
    low = chosen(parts, step)
    row[...] = low
    values = low.astype(F32)
    normed = (values * inverse_rms(values) * gain[...]).astype(BF16)
    normed_t[...] = normed.T
    for weight, out, out_t in ((w_query, q, q_t), (w_key, k, k_t), (w_value, v, v_t)):
        part = mm(normed, weight[...]).astype(BF16)
        out[...] = part
        out_t[...] = part.T
    if shares:

        @pl.when(step == 0)
        def lay_out():
            for i, out in enumerate(rest[8:]):
                out[...] = cotangent[at[0] ^ i]


def project(at, parts, shift, gain, w_query, w_key, w_value, before=(), cotangent=None):
    count, rows = len(parts), parts[0].shape[0]
    square, ways = fixed((D, D)), 0 if cotangent is None else cotangent.shape[0]
    row, column = (tokens(rows, shift), shape((LEN, D))), (tokens_t(rows, shift), shape((D, LEN)))
    outs = [row, column, row, column, row, column, row, column] + [(fixed((rows, D)), shape((rows, D)))] * ways
    start = 1 + count + 4
    return step_call(
        partial(project_kernel, count, len(before), ways > 0), at, count,
        [fixed((rows, D))] * count + [fixed((1, D)), square, square, square] + [ANY] * len(before)
        + [fixed((ways, rows, D))] * (ways > 0),
        (*parts, gain, w_query, w_key, w_value, *before) + ((cotangent,) if ways else ()),
        [o[0] for o in outs], [o[1] for o in outs], 3 * count / 4, "project",
        aliases={start + i: i for i in range(len(before))})


def feed_kernel(parts, at, x, attended, *refs):
    refs, both = refs[:-1], refs[-1]
    cots, (w_out, w_hidden, w_back, gain), rest = refs[:parts], refs[parts : parts + 4], refs[parts + 4 :]
    outs, (cot_row, normed_two, activated, grad_hidden, grad_middle, grad_attn, g, g_t) = rest[:-8], rest[-8:]
    step = pl.program_id(0)
    scale = gain[...]
    rows = cots[0].shape[0]
    spots = [pl.ds(pl.multiple_of(((at[0] ^ i) % 2) * rows, rows), rows) for i in range(2)]
    for i in range(2):
        both[spots[i], :] = chosen(cots[i::2], step)
    cotangent = both[...]
    cot_row[...] = cotangent
    middle = x[...].astype(F32) + mm(attended[...], w_out[...])
    inverse = inverse_rms(middle)
    n2 = (middle * inverse * scale).astype(BF16)
    normed_two[...] = n2
    total = middle
    grad_n2 = jnp.zeros_like(middle)
    width = FEED_COLUMNS
    for c in range(w_hidden.shape[1] // width):
        cols = slice(c * width, (c + 1) * width)
        hidden = mm(n2, w_hidden[:, cols])
        grad_act = against(cotangent, w_back[cols, :])
        squared = hidden * hidden
        tanh = jnp.tanh(GELU_SCALE * hidden * (1.0 + GELU_CUBIC * squared))
        half = 0.5 + 0.5 * tanh
        act = (hidden * half).astype(BF16)
        activated[:, cols] = act
        slope = half + (0.5 * GELU_SCALE) * hidden * (1.0 - tanh * tanh) * (1.0 + 3.0 * GELU_CUBIC * squared)
        grad = (grad_act * slope).astype(BF16)
        grad_hidden[:, cols] = grad
        total = total + mm(act, w_back[cols, :])
        grad_n2 = grad_n2 + against(grad, w_hidden[:, cols])
    both[...] = total.astype(BF16)
    near, far = outs[:-1], outs[-1]

    @pl.when(step == 0)
    def write_near():
        for i in range(2):
            near[i][...] = both[spots[i], :]

    @pl.when(step == 1)
    def write_far():
        for i in range(2):
            far[i] = both[spots[i], :]

    weighted = grad_n2 * scale
    mean = jnp.mean(weighted * middle, axis=-1, keepdims=True)
    grad_mid = cotangent.astype(F32) + inverse * weighted - middle * (inverse * inverse * inverse * mean)
    grad_middle[...] = grad_mid
    grad_low = grad_mid.astype(BF16)
    grad_attn[...] = grad_low
    grad = against(grad_low, w_out[...]).astype(BF16)
    g[...] = grad
    g_t[...] = grad.T


def feed(at, x, attended, cots, w_out, w_hidden, w_back, gain):
    ff, parts, rows = w_hidden.shape[1], len(cots), cots[0].shape[0]
    def pair(i, at):
        return (at[0] // 2) ^ i

    two = pl.BlockSpec((2 * rows, D), lambda i, at: (pair(i, at), 0))
    tile = (two, shape((LEN, D)))
    wide = (pl.BlockSpec((2 * rows, ff), lambda i, at: (pair(i, at), 0)), shape((LEN, ff)))
    outs = list(zip(*part_outs(parts, rows))) + [
        tile, tile, wide, wide, (two, shape((LEN, D), F32)), tile, tile,
        (pl.BlockSpec((D, 2 * rows), lambda i, at: (0, pair(i, at))), shape((D, LEN)))]
    found = step_call(
        partial(feed_kernel, parts), at, parts // 2,
        [two, two] + [fixed((rows, D))] * parts
        + [fixed((D, D)), fixed((D, ff)), fixed((ff, D)), fixed((1, D))],
        (x, attended, *cots, w_out, w_hidden, w_back, gain), [o[0] for o in outs], [o[1] for o in outs],
        2 + 4 * ff // D, "feed", [pltpu.VMEM((2 * rows, D), BF16)])
    return found[:-8], found[-8:]


def input_kernel(parts, at, grad_q, grad_k, grad_v, x, grad_middle, w_query, w_key, w_value, gain, first, *outs):
    upstream = against(grad_q[...], w_query[...]) + against(grad_k[...], w_key[...]) + against(grad_v[...], w_value[...])
    values = x[...].astype(F32)
    inverse = inverse_rms(values)
    weighted = upstream * gain[...]
    mean = jnp.mean(weighted * values, axis=-1, keepdims=True)
    low = (grad_middle[...] + inverse * weighted - values * (inverse * inverse * inverse * mean)).astype(BF16)
    write_parts(outs, pl.program_id(0), low)


def input_grads(at, parts, grad_q, grad_k, grad_v, x, grad_middle, w_query, w_key, w_value, gain, first):
    rows, square = LEN // parts, fixed((D, D))
    return step_call(
        partial(input_kernel, parts), at, parts, [tokens(rows)] * 5 + [square, square, square, fixed((1, D)), ANY],
        (grad_q, grad_k, grad_v, x, grad_middle, w_query, w_key, w_value, gain, first),
        *part_outs(parts, rows), 3, "input_grads")


def both_halves(kept, sent, product, left_kept, left_sent, right):
    kept[0, :HALF] = product(left_kept[...], right[...]).astype(BF16)
    sent[0, :HALF] = product(left_sent[...], right[...]).astype(BF16)


def wide_kernel(backs, core, act_kept, act_sent, cot, n2_kept, n2_sent, grad_hidden, kept, sent):
    step = pl.program_id(0)
    pl.when(step < backs)(partial(both_halves, kept, sent, across, act_kept, act_sent, cot))
    pl.when(step >= backs)(partial(both_halves, kept, sent, across, n2_kept, n2_sent, grad_hidden))


def thin_kernel(hiddens, core, n2_kept, n2_sent, grad_hidden, att_kept, att_sent, grad_attn, *refs):
    step, (kept, sent) = pl.program_id(0), refs[-2:]
    pl.when(step < hiddens)(partial(both_halves, kept, sent, across, n2_kept, n2_sent, grad_hidden))
    pl.when(step >= hiddens)(partial(both_halves, kept, sent, across, att_kept, att_sent, grad_attn))


def columns_half(other, at=lambda i: 0):
    return pl.BlockSpec((LEN, HALF), lambda i, core: (0, 2 * at(i) + (core[0] ^ other)))


def rows_half(other):
    return pl.BlockSpec((HALF, LEN), lambda i, core: (core[0] ^ other, 0))


def wide_and_thin(blocks):
    count = 2 * blocks + 1
    return 2 * count // 3, count - 2 * count // 3


def wide_weight_grads(core, activated, cot, normed_two, grad_hidden):
    blocks = activated.shape[1] // D
    count, _ = wide_and_thin(blocks)
    row, half = fixed((LEN, D)), pl.BlockSpec((1, HALF, D), lambda i, core: (i, 0, 0))

    def back(i):
        return jnp.minimum(i, blocks - 1)

    return step_call(
        partial(wide_kernel, blocks), core, count,
        [columns_half(0, back), columns_half(1, back), row, columns_half(0), columns_half(1),
         pl.BlockSpec((LEN, D), lambda i, core: (0, jnp.maximum(i - blocks, 0)))],
        (activated, activated, cot, normed_two, normed_two, grad_hidden),
        [half, half], [shape((count, HALF, D))] * 2, count, "wide_weight_grads")


def thin_weight_grads(core, normed_two, grad_hidden, attended, grad_attn, first):
    blocks = grad_hidden.shape[1] // D
    count, left = wide_and_thin(blocks)
    row, half = fixed((LEN, D)), pl.BlockSpec((1, HALF, D), lambda i, core: (i, 0, 0))
    return step_call(
        partial(thin_kernel, left - 1), core, left,
        [columns_half(0), columns_half(1),
         pl.BlockSpec((LEN, D), lambda i, core: (0, jnp.minimum(i + count - blocks, blocks - 1))),
         columns_half(0), columns_half(1), row] + [ANY] * len(first),
        (normed_two, normed_two, grad_hidden, attended, attended, grad_attn, *first),
        [half, half], [shape((left, HALF, D))] * 2, left, "thin_weight_grads")


SMALL_ROWS = 8


def small_sums(by_logits, by_weights):
    rows = jnp.concatenate([by_logits[:, 0, :], by_weights[:, 0, :]])
    head = lax.broadcasted_iota(jnp.int32, (D, 128), 0) // DH
    select = (head == lax.broadcasted_iota(jnp.int32, (D, 128), 1)).astype(F32)
    sums = jnp.dot(rows, select, precision=lax.Precision.HIGHEST, preferred_element_type=F32)
    groups = [sums[r : r + SMALL_ROWS, :] for r in range(0, 2 * H, SMALL_ROWS)]
    return jnp.concatenate(groups + [jnp.zeros((SMALL_ROWS, D - 128 * len(groups)), F32)], axis=1)


def project_weights_kernel(count, waits, core, nt_kept, nt_sent, *refs):
    grads, small, (kept, sent) = refs[:count], refs[count : -2 - waits], refs[-2:]
    for i, each in enumerate(grads):
        pl.when(pl.program_id(0) == i)(partial(both_halves, kept, sent, mm, nt_kept, nt_sent, each))
    if small:
        rows = jnp.concatenate([small_sums(*small), jnp.zeros((SMALL_ROWS, D), F32)]).astype(BF16)
        kept[0, HALF:] = rows
        sent[0, HALF:] = rows


def project_weight_grads(core, normed_t, grads, small=(), first=()):
    count, rows = len(grads), HALF + 2 * SMALL_ROWS * (len(small) > 0)
    half = pl.BlockSpec((1, rows, D), lambda i, core: (i, 0, 0))
    return step_call(
        partial(project_weights_kernel, count, len(first)), core, count,
        [rows_half(0), rows_half(1)] + [fixed((LEN, D))] * count + [fixed((H, 1, D))] * len(small) + [ANY] * len(first),
        (normed_t, normed_t, *grads, *small, *first), [half, half], [shape((count, rows, D))] * 2, count, "project_weight_grads")


def split_kernel(waits, mine, kept, came, *refs):
    outs, total = refs[waits:-1], refs[-1]
    total[...] = kept[...].astype(F32) + came[...].astype(F32)
    for c, out in enumerate(outs):
        rows = out.shape[1]
        out[...] = total[:, pl.ds(pl.multiple_of((mine[0] ^ c) * rows, 8), rows), :].astype(BF16)


def split(mine, kept, came, ways, name, first=()):
    count, rows, _ = kept.shape
    block = pl.BlockSpec((1, rows, D), lambda m, mine: (m, 0, 0))
    return step_call(
        partial(split_kernel, len(first)), mine, count, [block, block] + [ANY] * len(first), (kept, came, *first),
        [pl.BlockSpec((1, rows // ways, D), lambda m, mine: (m, 0, 0))] * ways,
        [shape((count, rows // ways, D))] * ways, 0, name, [pltpu.VMEM((1, rows, D), F32)])


def shares_kernel(wide_steps, mine, wide_kept, wide_came, thin_kept, thin_came, wide, *refs):
    thin, total, step = refs[:-1], refs[-1], pl.program_id(0)

    @pl.when(step < wide_steps)
    def of_wide():
        rows = wide.shape[2]
        for m in range(wide_kept.shape[0]):
            sums = wide_kept[m].astype(F32) + wide_came[m].astype(F32)
            for c in range(wide.shape[0]):
                wide[c, m] = sums[c * rows : (c + 1) * rows, :].astype(BF16)

    @pl.when(step >= wide_steps)
    def of_thin():
        total[...] = thin_kept[...].astype(F32) + thin_came[...].astype(F32)
        for c, out in enumerate(thin):
            rows = out.shape[1]
            out[...] = total[:, pl.ds(pl.multiple_of((mine[0] ^ c) * rows, 8), rows), :].astype(BF16)


def shares_of(mine, wide_kept, wide_came, thin_kept, thin_came, plane, line, first):
    count, left = wide_kept.shape[0], thin_kept.shape[0]
    per_step = 2
    steps = count // per_step

    def of_wide(m, mine):
        return jnp.minimum(m, steps - 1)

    half = pl.BlockSpec((per_step, HALF, D), lambda m, mine: (of_wide(m, mine), 0, 0))
    thin_half = fixed((left, HALF, D))
    outs = step_call(
        lambda mine, a, b, c, d, *refs: shares_kernel(steps, mine, a, b, c, d, *refs[len(first) :]), mine, steps + 1,
        [half, half, thin_half, thin_half] + [ANY] * len(first), (wide_kept, wide_came, thin_kept, thin_came, *first),
        [pl.BlockSpec((plane, per_step, HALF // plane, D), lambda m, mine: (0, of_wide(m, mine), 0, 0))]
        + [fixed((left, HALF // line, D))] * line,
        [shape((plane, count, HALF // plane, D))] + [shape((left, HALF // line, D))] * line, 0, "shares",
        [pltpu.VMEM((left, HALF, D), F32)])
    return outs[0], outs[1:]


def plain_call(kernel, operands, mine, out_shape, name, scratch=(), first=(), through=()):
    outs = pl.pallas_call(
        kernel,
        in_specs=[SMEM] + [VMEM] * len(operands) + [ANY] * (len(first) + len(through)),
        out_specs=[VMEM] * len(out_shape) + [ANY] * len(through),
        out_shape=list(out_shape) + [shape(t.shape, t.dtype) for t in through],
        input_output_aliases={1 + len(operands) + len(first) + i: len(out_shape) + i for i in range(len(through))},
        scratch_shapes=list(scratch),
        compiler_params=pltpu.CompilerParams(vmem_limit_bytes=VMEM_LIMIT),
        name=name,
    )(mine, *operands, *first, *through)
    return outs[: len(out_shape)], outs[len(out_shape) :]


def added(refs):
    return sum(ref[...].astype(F32) for ref in refs)


def sum_first(ref):
    return sum(ref[i].astype(F32) for i in range(ref.shape[0]))


def reshare_kernel(line, waits, mine, wide, *refs):
    thin, outs, total = refs[:line], refs[line + waits :], refs[-1]
    total[...] = sum_first(wide)
    for c in range(line):
        rows = outs[c].shape[1]
        outs[c][...] = total[:, pl.ds(pl.multiple_of((mine[1] ^ c) * rows, 8), rows), :].astype(BF16)
    out = outs[line]
    thin_sum, rows = added(thin), out.shape[2]
    for c in range(out.shape[0]):
        out[c] = thin_sum[:, c * rows : (c + 1) * rows, :].astype(BF16)


def reshare(mine, wide, thin, first, through):
    plane, count, rows, _ = wide.shape
    line, (left, thin_rows, _) = len(thin), thin[0].shape
    outs, through = plain_call(
        partial(reshare_kernel, line, len(first) + len(through)), [wide, *thin], mine,
        [shape((count, rows // line, D))] * line + [shape((plane, left, thin_rows // plane, D))], "reshare",
        [pltpu.VMEM((count, rows, D), F32)], first, through)
    return outs[:line], outs[line], through


def piece_kernel(line, waits, mine, thin, *refs):
    wide, out = refs[:line], refs[line + waits]
    count = wide[0].shape[0]
    out[:count] = added(wide).astype(BF16)
    out[count:] = sum_first(thin).astype(BF16)


def piece_of(mine, wide, thin, first, through):
    (count, rows, _), left = wide[0].shape, thin.shape[1]
    (out,), through = plain_call(
        partial(piece_kernel, len(wide), len(first) + len(through)), [thin, *wide], mine,
        [shape((count + left, rows, D))], "piece", (), first, through)
    return out, through


def split_small_kernel(mine, kept, came, *refs):
    outs, total, share = refs[:-2], refs[-2], refs[-1]
    total[...] = kept[0].astype(F32) + came[0].astype(F32)
    rows = share.shape[0] - SMALL_ROWS
    share[rows:] = total[HALF : HALF + SMALL_ROWS, :]
    for c, out in enumerate(outs):
        share[:rows] = total[pl.ds(pl.multiple_of((mine[0] ^ c) * rows, 8), rows), :]
        out[...] = share[...].astype(BF16)


def split_small(mine, kept, came, ways, name):
    rows = HALF // ways + SMALL_ROWS
    outs, _ = plain_call(
        split_small_kernel, [kept, came], mine, [shape((rows, D))] * ways, name,
        [pltpu.VMEM(kept.shape[1:], F32), pltpu.VMEM((rows, D), F32)])
    return outs


def project_reshare_kernel(ways, waits, mine, *refs):
    line, through = waits
    pairs, ones, outs = refs[:ways], refs[ways : 2 * ways], refs[2 * ways + through : 2 * ways + through + line]
    pair, one, share = refs[-3:]
    pair[...] = added(pairs)
    one[...] = added(ones)
    rows = pair.shape[1] // len(outs)
    share[3 * rows :] = one[pair.shape[1] :, :]
    for c, out in enumerate(outs):
        start = pl.multiple_of((mine[1] ^ c) * rows, 8)
        share[:rows] = pair[0, pl.ds(start, rows), :]
        share[rows : 2 * rows] = pair[1, pl.ds(start, rows), :]
        share[2 * rows : 3 * rows] = one[pl.ds(start, rows), :]
        out[...] = share[...].astype(BF16)


def project_reshare(mine, pairs, ones, ways, through):
    rows = 3 * pairs[0].shape[1] // ways + SMALL_ROWS
    return plain_call(
        partial(project_reshare_kernel, len(pairs), (ways, len(through))), [*pairs, *ones], mine,
        [shape((rows, D))] * ways, "project_reshare",
        [pltpu.VMEM(pairs[0].shape, F32), pltpu.VMEM(ones[0].shape, F32), pltpu.VMEM((rows, D), F32)], (), through)


def project_piece_kernel(mine, *refs):
    parts, (out, by_logits, by_weights, total) = refs[:-4], refs[-4:]
    total[...] = added(parts)
    rows = out.shape[1]
    for m in range(3):
        out[m] = total[m * rows : (m + 1) * rows, :].astype(BF16)
    small = total[3 * rows :, :]
    groups = [small[:, g * 128 : g * 128 + H] for g in range(3)]
    by_logits[...] = jnp.concatenate([groups[0], groups[1][:4]])
    by_weights[...] = jnp.concatenate([groups[1][4:], groups[2]])


def project_piece(mine, parts):
    rows = parts[0].shape[0]
    outs, _ = plain_call(
        project_piece_kernel, list(parts), mine,
        [shape((3, (rows - SMALL_ROWS) // 3, D))] + [shape((H, H), F32)] * 2, "project_piece",
        [pltpu.VMEM((rows, D), F32)])
    return outs


def stack_kernel(count, waits, mine, *refs):
    out, at = refs[count + waits], 0
    for ref in refs[:count]:
        out[at : at + ref.shape[0]] = ref[...]
        at += ref.shape[0]


def stack(mine, parts, name, first=()):
    rows = sum(p.shape[0] for p in parts)
    (out,), _ = plain_call(
        partial(stack_kernel, len(parts), len(first)), list(parts), mine, [shape((rows,) + parts[0].shape[1:])], name,
        (), first)
    return out


def tokens_kernel(waits, at, *refs):
    near, near_came, far, forwarded, out = *refs[:4], refs[4 + waits]
    for i, ref in enumerate((near, near_came, far.at[0], forwarded)):
        out[at[0] ^ i] = ref[...]


def tokens_of(at, came, name, first=()):
    (out,), _ = plain_call(
        partial(tokens_kernel, len(first)), list(came), at, [shape((4,) + came[0].shape)], name, (), first)
    return out


def weigh(out, weight):
    product = out[...] * weight[...].astype(F32)
    return sum(product[:, c : c + 128] for c in range(0, D, 128))


def as_row(weighed):
    return jnp.sum(weighed[...].T, axis=0, keepdims=True)


def spread_kernel(sizes, place, own, other, w_query, w_key, w_value, gain, *refs):
    outs, by_gain, weighed = refs[-5:-2], refs[-2], refs[-1]
    matrix = pl.program_id(0)
    plane, line = sizes
    rows = own.shape[2]

    @pl.when(matrix == 0)
    def zero():
        weighed[...] = jnp.zeros_like(weighed)

    for i, (out, weight) in enumerate(zip(outs, (w_query, w_key, w_value))):

        @pl.when(matrix == i)
        def here():
            for c, pieces in enumerate((own, other)):
                for p in range(plane):
                    for n in range(line):
                        of_plane, of_line = n % 2 + 2 * (p % 2), p // 2 + 2 * (n // 2)
                        at = (place[0] ^ c) * plane * line + (place[1] ^ of_plane) * line + (place[2] ^ of_line)
                        out[pl.ds(pl.multiple_of(at * rows, 8), rows), :] = pieces[p * line + n, 0].astype(F32)
            weighed[...] += weigh(out, weight)

    @pl.when(matrix == 2)
    def finish():
        by_gain[...] = (as_row(weighed) / gain[...])[0]


def matrix_outs(down, over):
    specs, shapes, begin, places = [], [], 0, []
    for d, o in zip(down, over):
        count = d * o

        def place_of(m, *at, begin=begin, count=count, o=o):
            within = jnp.clip(m - begin, 0, count - 1)
            return (within // o, within % o)

        places.append(place_of)
        specs.append(pl.BlockSpec((D, D), place_of))
        shapes.append(shape((d * D, o * D), F32))
        begin += count
    return specs, shapes, begin, places


def spread(place, sizes, own, other, w_query, w_key, w_value, gain, first):
    out_specs, out_shape, count, _ = matrix_outs((1, 1, 1), (1, 1, 1))
    devices, matrices, rows, _ = own.shape
    block = pl.BlockSpec((devices, 1, rows, D), lambda m, place: (0, m, 0, 0))
    square = fixed((D, D))
    return step_call(
        partial(spread_kernel, sizes), place, count, [block, block, square, square, square, fixed((1, D))] + [ANY] * len(first),
        (own, other, w_query, w_key, w_value, gain, *first),
        out_specs + [fixed((D,))], out_shape + [shape((D,), F32)], 0, "spread", [pltpu.VMEM((D, 128), F32)])


def fill_kernel(counts, wide_count, starts, pieces, w_hidden, gain, *refs):
    outs, by_gain, weighed = refs[:3], refs[3], refs[4]
    matrix, begin, rows = pl.program_id(0), 0, pieces.shape[2]

    @pl.when(matrix == 0)
    def zero():
        weighed[...] = jnp.zeros_like(weighed)

    for index, (out, count) in enumerate(zip(outs, counts)):
        for table, low, high in ((0, begin, min(begin + count, wide_count)), (1, max(begin, wide_count), begin + count)):
            if low < high:

                @pl.when((matrix >= low) & (matrix < high))
                def here():
                    for device, start in enumerate(starts[table]):
                        out[start : start + rows, :] = pieces[device, 0].astype(F32)
                    if index == 1:
                        weighed[...] += weigh(out, w_hidden)

        begin += count

    @pl.when(matrix == begin - 1)
    def finish():
        by_gain[...] = (as_row(weighed) / gain[...])[0]


def fill(pieces, starts, w_hidden, gain):
    blocks = w_hidden.shape[1] // D
    down, over = (blocks, 1, 1), (1, blocks, 1)
    out_specs, out_shape, count, places = matrix_outs(down, over)
    devices, matrices, rows, _ = pieces.shape
    line = whole((1, D))
    return pl.pallas_call(
        partial(fill_kernel, tuple(d * o for d, o in zip(down, over)), wide_and_thin(blocks)[0], starts),
        grid=(count,),
        in_specs=[pl.BlockSpec((devices, 1, rows, D), lambda m: (0, m, 0, 0)), pl.BlockSpec((D, D), places[1]), line],
        out_specs=out_specs + [whole((D,))],
        out_shape=out_shape + [shape((D,), F32)],
        scratch_shapes=[pltpu.VMEM((D, 128), F32)],
        compiler_params=params(),
        name="fill",
    )(pieces, w_hidden, gain)


BOTH = ("rows", "seq")


def swap(values, mask):
    n = lax.axis_size("rows") * lax.axis_size("seq")
    return lax.ppermute(values, BOTH, [(s, s ^ mask) for s in range(n)])


def device_bits():
    n = lax.axis_size("rows") * lax.axis_size("seq")
    return [1 << b for b in range(n.bit_length() - 1)]


def masks(dims):
    return [(c, sum(bit for i, bit in enumerate(dims) if c >> i & 1)) for c in range(1 << len(dims))]


def place(dims):
    me = lax.axis_index(BOTH)
    return sum(((me // bit) % 2) << i for i, bit in enumerate(dims))


def exchange(parts, dims):
    return [swap(part, mask) if mask else part for part, (c, mask) in zip(parts, masks(dims))]


def chip_groups():
    chips = device_bits()[1:]
    plane, line, rows = chips[:2], [], HALF >> 2
    for bit in chips[2:]:
        if rows >> (len(line) + 1) << (len(line) + 1) == rows and (rows >> (len(line) + 1)) % 8 == 0:
            line.append(bit)
    return plane, line, chips[2 + len(line) :]


def finish_sum(total, dims):
    for bit in dims:
        total = (total.astype(F32) + swap(total, bit).astype(F32)).astype(total.dtype)
    return total


def row_starts(first, second):
    starts = []
    for device in range(1 << len(device_bits())):
        row, size = 0, D
        for dims in ([1], first, second):
            size >>= len(dims)
            row += size * sum(((device // bit) % 2) << i for i, bit in enumerate(dims))
        starts.append(row)
    return tuple(starts)


def trade(values, dims):
    n = lax.axis_size("rows") * lax.axis_size("seq")
    groups, found = [], set()
    for device in range(n):
        if device not in found:
            group = [device ^ mask for c, mask in masks(dims)]
            found.update(group)
            groups.append(group)
    return lax.all_to_all(values, BOTH, split_axis=0, concat_axis=0, tiled=True, axis_index_groups=groups)


def widen(mine, values, dims, name, first=()):
    return stack(mine, exchange([values] * (1 << len(dims)), dims), name, first)


def send_far(parts):
    return (*parts[:2], swap(parts[2], 2))


def hand_on(parts):
    mine, near, far = parts
    return mine, swap(near, 1), far, swap(far[1], 1)


def per_device(
    inputs,
    segment_ids,
    gain_one,
    w_query,
    w_key,
    w_value,
    w_out,
    mix_logits,
    mix_weights,
    gain_two,
    w_hidden,
    w_back,
    cotangent,
):
    plane, line, others = chip_groups()
    where = jnp.stack([place([1]), place(plane), place(line)])
    core, spots = where[:1], where[1:]
    mixed = plane + line
    late_plane, early_line = mixed[1:3], mixed[:1] + mixed[3:]
    sizes = (1 << len(plane), 1 << len(line))
    parts, seq = lax.axis_size("seq"), lax.axis_index("seq")
    row_bits, at = device_bits()[: parts.bit_length() - 1], seq.reshape(1)
    ids = lax.dynamic_slice_in_dim(segment_ids, seq, 1, 0)
    gain_one, gain_two = gain_one.reshape(1, D), gain_two.reshape(1, D)
    scale = DH ** -0.5
    mix_l = mix_logits.astype(F32) * scale
    mix_w = mix_weights.astype(F32)

    came = exchange([lax.dynamic_index_in_dim(inputs, seq ^ i, 0, keepdims=False) for i in range(parts)], row_bits)
    near = parts // 2
    begun = project(at, came[:near], 0, gain_one, w_query, w_key, w_value, (), cotangent)
    cots = exchange(begun[8:], row_bits)
    x, normed_t, q, q_t, k, k_t, v, v_t = project(
        at, came[near:], near, gain_one, w_query, w_key, w_value, begun[:8])
    soft, attended = attend(mix_l, mix_w, ids, q_t, k, v_t)
    out, (cot, normed_two, activated, grad_hidden, grad_middle, grad_attn, g, g_t) = feed(
        at, x, attended, cots, w_out, w_hidden, w_back, gain_two
    )
    wide_kept, wide_sent = wide_weight_grads(core, activated, cot, normed_two, grad_hidden)
    thin_kept, thin_sent = thin_weight_grads(core, normed_two, grad_hidden, attended, grad_attn, [wide_kept])
    wide, thin = shares_of(
        spots[1:], wide_kept, swap(wide_sent, 1), thin_kept, swap(thin_sent, 1), sizes[0], sizes[1], [thin_kept])
    grad_q, grad_logits, by_logits = query_grads(mix_w, mix_l, soft, v, g_t, k_t, q_t, [wide, thin[0]])
    wide, thin, far = reshare(spots, trade(wide, plane), exchange(thin, line), [grad_q], out[2:])
    out = send_far((*out[:2], *far))
    grad_k = key_grads(mix_l, grad_logits, q, [wide[0]])
    piece, far = piece_of(spots, exchange(wide, line), trade(thin, plane), [grad_k], out[2:])
    out = hand_on((*out[:2], *far))
    pieces = lax.all_gather(finish_sum(piece, others), BOTH, axis=0)
    pair_kept, pair_sent = project_weight_grads(core, normed_t, [grad_q, grad_k], (), [piece])
    pair = split(spots[:1], pair_kept, swap(pair_sent, 1), sizes[0], "split_pair")
    grad_v, by_weights = value_grads(mix_w, soft, v, g, [piece, pair[0]])
    pair = exchange(pair, plane)
    one_kept, one_sent = project_weight_grads(core, normed_t, [grad_v], [by_logits, by_weights], [*pair[1:], out[1], out[3]])
    one = split_small(spots[:1], one_kept, swap(one_sent, 1), sizes[0], "split_one")
    grad_in = input_grads(
        at, parts, grad_q, grad_k, grad_v, x, grad_middle, w_query, w_key, w_value, gain_one, one[0])
    shares, grad_in = project_reshare(spots, pair, exchange(one, plane), sizes[1], grad_in)
    own, by_logits, by_weights = [finish_sum(a, others) for a in project_piece(spots, exchange(shares, line))]
    block_out = tokens_of(at, out, "block_out")
    grad_in = send_far(grad_in)
    own = widen(spots, own[None], early_line, "stack_line", [block_out, grad_in[2]])
    grad_w_back, grad_w_hidden, grad_w_out, grad_gain_two = fill(
        pieces, (row_starts(plane, line), row_starts(line, plane)), w_hidden, gain_two)
    grad_inputs = tokens_of(at, hand_on(grad_in), "grad_inputs", [grad_w_out])
    own = widen(spots, own, late_plane, "stack_plane", [grad_w_out])
    grad_w_query, grad_w_key, grad_w_value, grad_gain_one = spread(
        where, sizes, own, swap(own, 1), w_query, w_key, w_value, gain_one, [grad_w_out])
    return (
        block_out,
        grad_inputs,
        grad_gain_one,
        grad_w_query,
        grad_w_key,
        grad_w_value,
        grad_w_out,
        by_logits.T * scale,
        by_weights,
        grad_gain_two,
        grad_w_hidden,
        grad_w_back,
    )


def solution(mesh):
    sharded, copied = P("rows", "seq", None), P()
    in_specs = (sharded, P("rows", None)) + (copied,) * 10 + (sharded,)
    out_specs = (sharded, sharded) + (copied,) * 10
    return jax.shard_map(
        per_device, mesh=mesh, in_specs=in_specs, out_specs=out_specs, check_vma=False
    )
```

```python
from functools import partial

from jax import lax
import jax
import jax.numpy as jnp
from jax.experimental import pallas as pl
from jax.experimental.pallas import tpu as pltpu
from jax.sharding import PartitionSpec as P

D, H, DH, LEN, TILE = 768, 12, 64, 1024, 256
TILES = LEN // TILE
F32, BF16 = jnp.float32, jnp.bfloat16
FORWARD_HEADS, BACKWARD_HEADS = 4, 2
VMEM_LIMIT = 65480 * 1024
LOG2_E = 1.4426950408889634
MATMUL_FLOPS = 2 * H * 10 * TILE * TILE * D


def span(i):
    return slice(i * TILE, (i + 1) * TILE)


def head_rows(h):
    return slice(h * DH, (h + 1) * DH)


def mm(a, b):
    return jnp.dot(a, b, preferred_element_type=F32)


def whole(shape):
    return pl.BlockSpec(shape, lambda i: (0,) * len(shape), pipeline_mode=pl.Buffered(1))


def some_heads(count, shape):
    return pl.BlockSpec((count,) + shape, lambda i: (i,) + (0,) * len(shape))


SMEM = pl.BlockSpec(memory_space=pltpu.SMEM)


def params():
    return pltpu.CompilerParams(dimension_semantics=("arbitrary",), vmem_limit_bytes=VMEM_LIMIT)


def shape(s, t=BF16):
    return jax.ShapeDtypeStruct(s, t)


def attend_kernel(mix_l, mix_w, id_row, id_col, q_t, k, v_t, soft, out, bias, scaled, acc):
    step = pl.program_id(0)

    @pl.when(step == 0)
    def start():
        acc[...] = jnp.zeros_like(acc)
        for t in range(TILES):
            for u in range(t + 1):
                allowed = id_col[span(u), :] == id_row[:, span(t)]
                if u == t:
                    key = lax.broadcasted_iota(jnp.int32, (TILE, TILE), 0)
                    query = lax.broadcasted_iota(jnp.int32, (TILE, TILE), 1)
                    allowed = allowed & (key <= query)
                bias[span(u), span(t)] = jnp.where(allowed, 0.0, -1e30)

    for i in range(FORWARD_HEADS):
        j = step * FORWARD_HEADS + i
        for h in range(H):
            weight = mix_l[h, j] * LOG2_E
            scaled[i, head_rows(h), :] = (q_t[head_rows(h), :].astype(F32) * weight).astype(BF16)
        for t in reversed(range(TILES)):
            n = (t + 1) * TILE
            logits = mm(k[:n, :], scaled[i, :, span(t)]) + bias[:n, span(t)]
            e = jnp.exp2(logits - jnp.max(logits, axis=0, keepdims=True))
            p = (e * (1.0 / jnp.sum(e, axis=0, keepdims=True))).astype(BF16)
            soft[i, :n, span(t)] = p
            part = mm(v_t[:, :n], p)
            for h in range(H):
                acc[head_rows(h), span(t)] += part[head_rows(h), :] * mix_w[j, h]

    @pl.when(step == H // FORWARD_HEADS - 1)
    def finish():
        for t in range(TILES):
            out[span(t), :] = acc[:, span(t)].T.astype(BF16)


def attend(mix_l, mix_w, ids, q_t, k, v_t):
    heads = FORWARD_HEADS
    return pl.pallas_call(
        attend_kernel,
        grid=(H // heads,),
        in_specs=[SMEM, SMEM, whole((1, LEN)), whole((LEN, 1)), whole((D, LEN)), whole((LEN, D)), whole((D, LEN))],
        out_specs=[some_heads(heads, (LEN, LEN)), whole((LEN, D))],
        out_shape=[shape((H, LEN, LEN)), shape((LEN, D))],
        scratch_shapes=[
            pltpu.VMEM((LEN, LEN), F32), pltpu.VMEM((heads, D, LEN), BF16), pltpu.VMEM((D, LEN), F32)
        ],
        compiler_params=params(),
        cost_estimate=pl.CostEstimate(flops=MATMUL_FLOPS // 4, bytes_accessed=LEN * LEN, transcendentals=0),
        name="attend",
    )(mix_l, mix_w, ids.reshape(1, LEN), ids.reshape(LEN, 1), q_t, k, v_t)


def head_row(weight_of):
    head = lax.broadcasted_iota(jnp.int32, (1, D), 1) // DH
    row = jnp.full((1, D), weight_of(0), F32)
    for h in range(1, H):
        row = jnp.where(head == h, weight_of(h), row)
    return row


def value_grads_kernel(mix_w, soft, v, g, *rest):
    out, mix_grad, acc = rest[-3:]
    step = pl.program_id(0)

    @pl.when(step == 0)
    def start():
        acc[...] = jnp.zeros_like(acc)

    for i in range(BACKWARD_HEADS):
        total = jnp.zeros((1, D), F32)
        mix_row = head_row(lambda h: mix_w[step * BACKWARD_HEADS + i, h])
        for u in range(TILES):
            part = mm(soft[i, span(u), u * TILE :], g[u * TILE :, :])
            acc[span(u), :] += part * mix_row
            total = total + jnp.sum(part * v[span(u), :].astype(F32), axis=0, keepdims=True)
        mix_grad[i] = total

    @pl.when(step == H // BACKWARD_HEADS - 1)
    def finish():
        out[...] = acc[...].astype(BF16)


def query_grads_kernel(heads, mix_w, mix_l, soft, v, g_t, k_t, q_t, *rest):
    before, (out, grad_logits, mix_grad, acc, scaled) = rest[0], rest[-5:]
    step = pl.program_id(0)
    first_head = heads[0] + step * BACKWARD_HEADS

    @pl.when(step == 0)
    def start():
        acc[...] = before[...] if heads[0] else jnp.zeros_like(acc)

    for i in range(BACKWARD_HEADS):
        j = first_head + i
        for h in range(H):
            scaled[i, head_rows(h), :] = (g_t[head_rows(h), :].astype(F32) * mix_w[j, h]).astype(BF16)
    order = [(i, t) for i in range(BACKWARD_HEADS) for t in reversed(range(TILES))]

    def grad_soft(i, t):
        return mm(v[: (t + 1) * TILE, :], scaled[i, :, span(t)])

    coming = grad_soft(*order[0])
    total = jnp.zeros((D, 128), F32)
    for at, (i, t) in enumerate(order):
        n = (t + 1) * TILE
        p = soft[i, :n, span(t)].astype(F32)
        weighted = p * coming
        low = (weighted - p * jnp.sum(weighted, axis=0, keepdims=True)).astype(BF16)
        grad_logits[i, :n, span(t)] = low
        if at + 1 < len(order):
            coming = grad_soft(*order[at + 1])
        part = mm(k_t[:, :n], low)
        for h in range(H):
            acc[head_rows(h), span(t)] += part[head_rows(h), :] * mix_l[h, first_head + i]
        product = part * q_t[:, span(t)].astype(F32)
        total = total + product[:, :128] + product[:, 128:]
        if t == 0:
            mix_grad[i] = jnp.sum(total.T, axis=0, keepdims=True)
            total = jnp.zeros((D, 128), F32)

    @pl.when(step == pl.num_programs(0) - 1)
    def finish():
        if heads[1] < H:
            out[...] = acc[...]
        else:
            for t in range(TILES):
                out[span(t), :] = acc[:, span(t)].T.astype(BF16)


def key_grads_kernel(mix_l, grad_logits, q, *rest):
    out, acc = rest[-2:]
    step = pl.program_id(0)

    @pl.when(step == 0)
    def start():
        acc[...] = jnp.zeros_like(acc)

    for i in range(BACKWARD_HEADS):
        mix_row = head_row(lambda h: mix_l[h, step * BACKWARD_HEADS + i])
        for u in range(TILES):
            acc[span(u), :] += mm(grad_logits[i, span(u), u * TILE :], q[u * TILE :, :]) * mix_row

    @pl.when(step == H // BACKWARD_HEADS - 1)
    def finish():
        out[...] = acc[...].astype(BF16)


def back_call(kernel, heads, in_specs, out_specs, out_shape, scratch, matmuls, name):
    def run(*operands):
        *used, first = operands
        return pl.pallas_call(
            kernel,
            grid=(heads // BACKWARD_HEADS,),
            in_specs=in_specs + [pl.BlockSpec(memory_space=pl.ANY)] * len(first),
            out_specs=out_specs,
            out_shape=out_shape,
            scratch_shapes=scratch,
            compiler_params=params(),
            cost_estimate=pl.CostEstimate(
                flops=matmuls * MATMUL_FLOPS * heads // H // 8, bytes_accessed=LEN * LEN, transcendentals=0
            ),
            name=name,
        )(*used, *first)

    return run


ROW, COLUMN = whole((LEN, D)), whole((D, LEN))
PER_HEAD, PER_HEAD_ROW = some_heads(BACKWARD_HEADS, (LEN, LEN)), some_heads(BACKWARD_HEADS, (1, D))


def value_grads(mix_w, soft, v, g, first):
    grads, mix_grad = back_call(
        value_grads_kernel,
        H,
        [SMEM, PER_HEAD, ROW, ROW],
        [ROW, PER_HEAD_ROW],
        [shape((LEN, D)), shape((H, 1, D), F32)],
        [pltpu.VMEM((LEN, D), F32)],
        1,
        "value_grads",
    )(mix_w, soft, v, g, first)
    return grads, mix_grad


def query_grads(mix_w, mix_l, soft, v, g_t, k_t, q_t, first, heads=(0, H), before=()):
    low, high = heads
    count, last = high - low, high == H
    per_head = pl.BlockSpec((BACKWARD_HEADS, LEN, LEN), lambda i: (i + low // BACKWARD_HEADS, 0, 0))
    grads, grad_logits, mix_grad = back_call(
        partial(query_grads_kernel, heads),
        count,
        [SMEM, SMEM, per_head, ROW, COLUMN, COLUMN, COLUMN] + [COLUMN] * len(before),
        [ROW if last else COLUMN, PER_HEAD, PER_HEAD_ROW],
        [shape((LEN, D)) if last else shape((D, LEN), F32), shape((count, LEN, LEN)), shape((count, 1, D), F32)],
        [pltpu.VMEM((D, LEN), F32), pltpu.VMEM((BACKWARD_HEADS, D, LEN), BF16)],
        2,
        "query_grads",
    )(mix_w, mix_l, soft, v, g_t, k_t, q_t, *before, first)
    return grads, grad_logits, mix_grad


def key_grads(mix_l, grad_logits, q, first):
    return back_call(
        key_grads_kernel, H, [SMEM, PER_HEAD, ROW], ROW, shape((LEN, D)), [pltpu.VMEM((LEN, D), F32)], 1,
        "key_grads",
    )(mix_l, grad_logits, q, first)


epsilon = 1e-06
GELU_SCALE = 0.7978845608028654
GELU_CUBIC = 0.044715
FEED_COLUMNS = 768
COST_SHARE = 4
HALF = D // 2
ANY = pl.BlockSpec(memory_space=pl.ANY)
VMEM = pl.BlockSpec(memory_space=pltpu.VMEM)


def against(left, right):
    return lax.dot_general(left, right, (((1,), (1,)), ((), ())), preferred_element_type=F32)


def across(left, right):
    return lax.dot_general(left, right, (((0,), (0,)), ((), ())), preferred_element_type=F32)


def inverse_rms(values):
    return lax.rsqrt(jnp.mean(values * values, axis=-1, keepdims=True) + epsilon)


def cost(matrices):
    return pl.CostEstimate(flops=int(matrices * LEN * D * D) // COST_SHARE, bytes_accessed=LEN * D, transcendentals=0)


def fixed(s):
    return pl.BlockSpec(s, lambda i, at: (0,) * len(s), pipeline_mode=pl.Buffered(1))


def tokens(rows, shift=0):
    return pl.BlockSpec((rows, D), lambda i, at: (at[0] ^ (i + shift), 0))


def tokens_t(columns, shift=0):
    return pl.BlockSpec((D, columns), lambda i, at: (0, at[0] ^ (i + shift)))


def step_call(kernel, at, steps, in_specs, operands, out_specs, out_shape, matrices, name, scratch=(), aliases=None):
    return pl.pallas_call(
        kernel,
        grid_spec=pltpu.PrefetchScalarGridSpec(
            num_scalar_prefetch=1, grid=(steps,), in_specs=in_specs, out_specs=out_specs, scratch_shapes=list(scratch)),
        out_shape=out_shape,
        input_output_aliases=aliases or {},
        compiler_params=params(),
        cost_estimate=cost(matrices),
        name=name,
    )(at, *operands)


def chosen(refs, step):
    values = refs[0][...]
    for i, ref in enumerate(refs[1:]):
        values = jnp.where(step == i + 1, ref[...], values)
    return values


def write_parts(outs, step, values):
    for i, out in enumerate(outs[:-1]):

        @pl.when(step == i)
        def write():
            out[...] = values

    far = outs[-1].shape[0]
    for i in range(far):

        @pl.when(step == len(outs) - 1 + i)
        def write_far():
            outs[-1][i] = values


def part_outs(parts, rows):
    near = parts // 2
    specs = [fixed((rows, D))] * near + [fixed((parts - near, rows, D))]
    return specs, [shape((rows, D))] * near + [shape((parts - near, rows, D))]


def project_kernel(steps, waits, shares, at, *refs):
    parts, (gain, w_query, w_key, w_value) = refs[:steps], refs[steps : steps + 4]
    rest = refs[steps + 4 + waits :]
    cotangent, rest = (rest[0], rest[1:]) if shares else (None, rest)
    row, normed_t, q, q_t, k, k_t, v, v_t = rest[:8]
    step = pl.program_id(0)
    low = chosen(parts, step)
    row[...] = low
    values = low.astype(F32)
    normed = (values * inverse_rms(values) * gain[...]).astype(BF16)
    normed_t[...] = normed.T
    for weight, out, out_t in ((w_query, q, q_t), (w_key, k, k_t), (w_value, v, v_t)):
        part = mm(normed, weight[...]).astype(BF16)
        out[...] = part
        out_t[...] = part.T
    if shares:

        @pl.when(step == 0)
        def lay_out():
            for i, out in enumerate(rest[8:]):
                out[...] = cotangent[at[0] ^ i]


def project(at, parts, shift, gain, w_query, w_key, w_value, before=(), cotangent=None):
    count, rows = len(parts), parts[0].shape[0]
    square, ways = fixed((D, D)), 0 if cotangent is None else cotangent.shape[0]
    row, column = (tokens(rows, shift), shape((LEN, D))), (tokens_t(rows, shift), shape((D, LEN)))
    outs = [row, column, row, column, row, column, row, column] + [(fixed((rows, D)), shape((rows, D)))] * ways
    start = 1 + count + 4
    return step_call(
        partial(project_kernel, count, len(before), ways > 0), at, count,
        [fixed((rows, D))] * count + [fixed((1, D)), square, square, square] + [ANY] * len(before)
        + [fixed((ways, rows, D))] * (ways > 0),
        (*parts, gain, w_query, w_key, w_value, *before) + ((cotangent,) if ways else ()),
        [o[0] for o in outs], [o[1] for o in outs], 3 * count / 4, "project",
        aliases={start + i: i for i in range(len(before))})


def feed_kernel(parts, at, x, attended, *refs):
    refs, both = refs[:-1], refs[-1]
    cots, (w_out, w_hidden, w_back, gain), rest = refs[:parts], refs[parts : parts + 4], refs[parts + 4 :]
    outs, (cot_row, normed_two, activated, grad_hidden, grad_middle, grad_attn, g, g_t) = rest[:-8], rest[-8:]
    step = pl.program_id(0)
    scale = gain[...]
    rows = cots[0].shape[0]
    spots = [pl.ds(pl.multiple_of(((at[0] ^ i) % 2) * rows, rows), rows) for i in range(2)]
    for i in range(2):
        both[spots[i], :] = chosen(cots[i::2], step)
    cotangent = both[...]
    cot_row[...] = cotangent
    middle = x[...].astype(F32) + mm(attended[...], w_out[...])
    inverse = inverse_rms(middle)
    n2 = (middle * inverse * scale).astype(BF16)
    normed_two[...] = n2
    total = middle
    grad_n2 = jnp.zeros_like(middle)
    width = FEED_COLUMNS
    for c in range(w_hidden.shape[1] // width):
        cols = slice(c * width, (c + 1) * width)
        hidden = mm(n2, w_hidden[:, cols])
        grad_act = against(cotangent, w_back[cols, :])
        squared = hidden * hidden
        tanh = jnp.tanh(GELU_SCALE * hidden * (1.0 + GELU_CUBIC * squared))
        half = 0.5 + 0.5 * tanh
        act = (hidden * half).astype(BF16)
        activated[:, cols] = act
        slope = half + (0.5 * GELU_SCALE) * hidden * (1.0 - tanh * tanh) * (1.0 + 3.0 * GELU_CUBIC * squared)
        grad = (grad_act * slope).astype(BF16)
        grad_hidden[:, cols] = grad
        total = total + mm(act, w_back[cols, :])
        grad_n2 = grad_n2 + against(grad, w_hidden[:, cols])
    both[...] = total.astype(BF16)
    near, far = outs[:-1], outs[-1]

    @pl.when(step == 0)
    def write_near():
        for i in range(2):
            near[i][...] = both[spots[i], :]

    @pl.when(step == 1)
    def write_far():
        for i in range(2):
            far[i] = both[spots[i], :]

    weighted = grad_n2 * scale
    mean = jnp.mean(weighted * middle, axis=-1, keepdims=True)
    grad_mid = cotangent.astype(F32) + inverse * weighted - middle * (inverse * inverse * inverse * mean)
    grad_middle[...] = grad_mid
    grad_low = grad_mid.astype(BF16)
    grad_attn[...] = grad_low
    grad = against(grad_low, w_out[...]).astype(BF16)
    g[...] = grad
    g_t[...] = grad.T


def feed(at, x, attended, cots, w_out, w_hidden, w_back, gain):
    ff, parts, rows = w_hidden.shape[1], len(cots), cots[0].shape[0]
    def pair(i, at):
        return (at[0] // 2) ^ i

    two = pl.BlockSpec((2 * rows, D), lambda i, at: (pair(i, at), 0))
    tile = (two, shape((LEN, D)))
    wide = (pl.BlockSpec((2 * rows, ff), lambda i, at: (pair(i, at), 0)), shape((LEN, ff)))
    outs = list(zip(*part_outs(parts, rows))) + [
        tile, tile, wide, wide, (two, shape((LEN, D), F32)), tile, tile,
        (pl.BlockSpec((D, 2 * rows), lambda i, at: (0, pair(i, at))), shape((D, LEN)))]
    found = step_call(
        partial(feed_kernel, parts), at, parts // 2,
        [two, two] + [fixed((rows, D))] * parts
        + [fixed((D, D)), fixed((D, ff)), fixed((ff, D)), fixed((1, D))],
        (x, attended, *cots, w_out, w_hidden, w_back, gain), [o[0] for o in outs], [o[1] for o in outs],
        2 + 4 * ff // D, "feed", [pltpu.VMEM((2 * rows, D), BF16)])
    return found[:-8], found[-8:]


def input_kernel(parts, at, grad_q, grad_k, grad_v, x, grad_middle, w_query, w_key, w_value, gain, first, *outs):
    upstream = against(grad_q[...], w_query[...]) + against(grad_k[...], w_key[...]) + against(grad_v[...], w_value[...])
    values = x[...].astype(F32)
    inverse = inverse_rms(values)
    weighted = upstream * gain[...]
    mean = jnp.mean(weighted * values, axis=-1, keepdims=True)
    low = (grad_middle[...] + inverse * weighted - values * (inverse * inverse * inverse * mean)).astype(BF16)
    write_parts(outs, pl.program_id(0), low)


def input_grads(at, parts, grad_q, grad_k, grad_v, x, grad_middle, w_query, w_key, w_value, gain, first):
    rows, square = LEN // parts, fixed((D, D))
    return step_call(
        partial(input_kernel, parts), at, parts, [tokens(rows)] * 5 + [square, square, square, fixed((1, D)), ANY],
        (grad_q, grad_k, grad_v, x, grad_middle, w_query, w_key, w_value, gain, first),
        *part_outs(parts, rows), 3, "input_grads")


def both_halves(kept, sent, product, left_kept, left_sent, right):
    kept[0, :HALF] = product(left_kept[...], right[...]).astype(BF16)
    sent[0, :HALF] = product(left_sent[...], right[...]).astype(BF16)


def wide_kernel(backs, core, act_kept, act_sent, cot, n2_kept, n2_sent, grad_hidden, kept, sent):
    step = pl.program_id(0)
    pl.when(step < backs)(partial(both_halves, kept, sent, across, act_kept, act_sent, cot))
    pl.when(step >= backs)(partial(both_halves, kept, sent, across, n2_kept, n2_sent, grad_hidden))


def thin_kernel(hiddens, core, n2_kept, n2_sent, grad_hidden, att_kept, att_sent, grad_attn, *refs):
    step, (kept, sent) = pl.program_id(0), refs[-2:]
    pl.when(step < hiddens)(partial(both_halves, kept, sent, across, n2_kept, n2_sent, grad_hidden))
    pl.when(step >= hiddens)(partial(both_halves, kept, sent, across, att_kept, att_sent, grad_attn))


def columns_half(other, at=lambda i: 0):
    return pl.BlockSpec((LEN, HALF), lambda i, core: (0, 2 * at(i) + (core[0] ^ other)))


def rows_half(other):
    return pl.BlockSpec((HALF, LEN), lambda i, core: (core[0] ^ other, 0))


def wide_and_thin(blocks):
    count = 2 * blocks + 1
    return 2 * count // 3, count - 2 * count // 3


def wide_weight_grads(core, activated, cot, normed_two, grad_hidden):
    blocks = activated.shape[1] // D
    count, _ = wide_and_thin(blocks)
    row, half = fixed((LEN, D)), pl.BlockSpec((1, HALF, D), lambda i, core: (i, 0, 0))

    def back(i):
        return jnp.minimum(i, blocks - 1)

    return step_call(
        partial(wide_kernel, blocks), core, count,
        [columns_half(0, back), columns_half(1, back), row, columns_half(0), columns_half(1),
         pl.BlockSpec((LEN, D), lambda i, core: (0, jnp.maximum(i - blocks, 0)))],
        (activated, activated, cot, normed_two, normed_two, grad_hidden),
        [half, half], [shape((count, HALF, D))] * 2, count, "wide_weight_grads")


def thin_weight_grads(core, normed_two, grad_hidden, attended, grad_attn, first):
    blocks = grad_hidden.shape[1] // D
    count, left = wide_and_thin(blocks)
    row, half = fixed((LEN, D)), pl.BlockSpec((1, HALF, D), lambda i, core: (i, 0, 0))
    return step_call(
        partial(thin_kernel, left - 1), core, left,
        [columns_half(0), columns_half(1),
         pl.BlockSpec((LEN, D), lambda i, core: (0, jnp.minimum(i + count - blocks, blocks - 1))),
         columns_half(0), columns_half(1), row] + [ANY] * len(first),
        (normed_two, normed_two, grad_hidden, attended, attended, grad_attn, *first),
        [half, half], [shape((left, HALF, D))] * 2, left, "thin_weight_grads")


SMALL_ROWS = 8


def small_sums(by_logits, by_weights):
    rows = jnp.concatenate([by_logits[:, 0, :], by_weights[:, 0, :]])
    head = lax.broadcasted_iota(jnp.int32, (D, 128), 0) // DH
    select = (head == lax.broadcasted_iota(jnp.int32, (D, 128), 1)).astype(F32)
    sums = jnp.dot(rows, select, precision=lax.Precision.HIGHEST, preferred_element_type=F32)
    groups = [sums[r : r + SMALL_ROWS, :] for r in range(0, 2 * H, SMALL_ROWS)]
    return jnp.concatenate(groups + [jnp.zeros((SMALL_ROWS, D - 128 * len(groups)), F32)], axis=1)


def project_weights_kernel(count, waits, core, nt_kept, nt_sent, *refs):
    grads, small, (kept, sent) = refs[:count], refs[count : -2 - waits], refs[-2:]
    for i, each in enumerate(grads):
        pl.when(pl.program_id(0) == i)(partial(both_halves, kept, sent, mm, nt_kept, nt_sent, each))
    if small:
        rows = jnp.concatenate([small_sums(*small), jnp.zeros((SMALL_ROWS, D), F32)]).astype(BF16)
        kept[0, HALF:] = rows
        sent[0, HALF:] = rows


def project_weight_grads(core, normed_t, grads, small=(), first=()):
    count, rows = len(grads), HALF + 2 * SMALL_ROWS * (len(small) > 0)
    half = pl.BlockSpec((1, rows, D), lambda i, core: (i, 0, 0))
    return step_call(
        partial(project_weights_kernel, count, len(first)), core, count,
        [rows_half(0), rows_half(1)] + [fixed((LEN, D))] * count + [fixed((H, 1, D))] * len(small) + [ANY] * len(first),
        (normed_t, normed_t, *grads, *small, *first), [half, half], [shape((count, rows, D))] * 2, count, "project_weight_grads")


def split_kernel(waits, mine, kept, came, *refs):
    outs, total = refs[waits:-1], refs[-1]
    total[...] = kept[...].astype(F32) + came[...].astype(F32)
    for c, out in enumerate(outs):
        rows = out.shape[1]
        out[...] = total[:, pl.ds(pl.multiple_of((mine[0] ^ c) * rows, 8), rows), :].astype(BF16)


def split(mine, kept, came, ways, name, first=()):
    count, rows, _ = kept.shape
    block = pl.BlockSpec((1, rows, D), lambda m, mine: (m, 0, 0))
    return step_call(
        partial(split_kernel, len(first)), mine, count, [block, block] + [ANY] * len(first), (kept, came, *first),
        [pl.BlockSpec((1, rows // ways, D), lambda m, mine: (m, 0, 0))] * ways,
        [shape((count, rows // ways, D))] * ways, 0, name, [pltpu.VMEM((1, rows, D), F32)])


def shares_kernel(wide_steps, mine, wide_kept, wide_came, thin_kept, thin_came, wide, *refs):
    thin, total, step = refs[:-1], refs[-1], pl.program_id(0)

    @pl.when(step < wide_steps)
    def of_wide():
        rows = wide.shape[2]
        for m in range(wide_kept.shape[0]):
            sums = wide_kept[m].astype(F32) + wide_came[m].astype(F32)
            for c in range(wide.shape[0]):
                wide[c, m] = sums[c * rows : (c + 1) * rows, :].astype(BF16)

    @pl.when(step >= wide_steps)
    def of_thin():
        total[...] = thin_kept[...].astype(F32) + thin_came[...].astype(F32)
        for c, out in enumerate(thin):
            rows = out.shape[1]
            out[...] = total[:, pl.ds(pl.multiple_of((mine[0] ^ c) * rows, 8), rows), :].astype(BF16)


def shares_of(mine, wide_kept, wide_came, thin_kept, thin_came, plane, line, first):
    count, left = wide_kept.shape[0], thin_kept.shape[0]
    per_step = 2
    steps = count // per_step

    def of_wide(m, mine):
        return jnp.minimum(m, steps - 1)

    half = pl.BlockSpec((per_step, HALF, D), lambda m, mine: (of_wide(m, mine), 0, 0))
    thin_half = fixed((left, HALF, D))
    outs = step_call(
        lambda mine, a, b, c, d, *refs: shares_kernel(steps, mine, a, b, c, d, *refs[len(first) :]), mine, steps + 1,
        [half, half, thin_half, thin_half] + [ANY] * len(first), (wide_kept, wide_came, thin_kept, thin_came, *first),
        [pl.BlockSpec((plane, per_step, HALF // plane, D), lambda m, mine: (0, of_wide(m, mine), 0, 0))]
        + [fixed((left, HALF // line, D))] * line,
        [shape((plane, count, HALF // plane, D))] + [shape((left, HALF // line, D))] * line, 0, "shares",
        [pltpu.VMEM((left, HALF, D), F32)])
    return outs[0], outs[1:]


def plain_call(kernel, operands, mine, out_shape, name, scratch=(), first=(), through=()):
    outs = pl.pallas_call(
        kernel,
        in_specs=[SMEM] + [VMEM] * len(operands) + [ANY] * (len(first) + len(through)),
        out_specs=[VMEM] * len(out_shape) + [ANY] * len(through),
        out_shape=list(out_shape) + [shape(t.shape, t.dtype) for t in through],
        input_output_aliases={1 + len(operands) + len(first) + i: len(out_shape) + i for i in range(len(through))},
        scratch_shapes=list(scratch),
        compiler_params=pltpu.CompilerParams(vmem_limit_bytes=VMEM_LIMIT),
        name=name,
    )(mine, *operands, *first, *through)
    return outs[: len(out_shape)], outs[len(out_shape) :]


def added(refs):
    return sum(ref[...].astype(F32) for ref in refs)


def sum_first(ref):
    return sum(ref[i].astype(F32) for i in range(ref.shape[0]))


def reshare_kernel(line, waits, mine, wide, *refs):
    thin, outs, total = refs[:line], refs[line + waits :], refs[-1]
    total[...] = sum_first(wide)
    for c in range(line):
        rows = outs[c].shape[1]
        outs[c][...] = total[:, pl.ds(pl.multiple_of((mine[1] ^ c) * rows, 8), rows), :].astype(BF16)
    out = outs[line]
    thin_sum, rows = added(thin), out.shape[2]
    for c in range(out.shape[0]):
        out[c] = thin_sum[:, c * rows : (c + 1) * rows, :].astype(BF16)


def reshare(mine, wide, thin, first, through):
    plane, count, rows, _ = wide.shape
    line, (left, thin_rows, _) = len(thin), thin[0].shape
    outs, through = plain_call(
        partial(reshare_kernel, line, len(first) + len(through)), [wide, *thin], mine,
        [shape((count, rows // line, D))] * line + [shape((plane, left, thin_rows // plane, D))], "reshare",
        [pltpu.VMEM((count, rows, D), F32)], first, through)
    return outs[:line], outs[line], through


def piece_kernel(line, waits, mine, thin, *refs):
    wide, out = refs[:line], refs[line + waits]
    count = wide[0].shape[0]
    out[:count] = added(wide).astype(BF16)
    out[count:] = sum_first(thin).astype(BF16)


def piece_of(mine, wide, thin, first, through):
    (count, rows, _), left = wide[0].shape, thin.shape[1]
    (out,), through = plain_call(
        partial(piece_kernel, len(wide), len(first) + len(through)), [thin, *wide], mine,
        [shape((count + left, rows, D))], "piece", (), first, through)
    return out, through


def split_small_kernel(mine, kept, came, *refs):
    outs, total, share = refs[:-2], refs[-2], refs[-1]
    total[...] = kept[0].astype(F32) + came[0].astype(F32)
    rows = share.shape[0] - SMALL_ROWS
    share[rows:] = total[HALF : HALF + SMALL_ROWS, :]
    for c, out in enumerate(outs):
        share[:rows] = total[pl.ds(pl.multiple_of((mine[0] ^ c) * rows, 8), rows), :]
        out[...] = share[...].astype(BF16)


def split_small(mine, kept, came, ways, name):
    rows = HALF // ways + SMALL_ROWS
    outs, _ = plain_call(
        split_small_kernel, [kept, came], mine, [shape((rows, D))] * ways, name,
        [pltpu.VMEM(kept.shape[1:], F32), pltpu.VMEM((rows, D), F32)])
    return outs


def project_reshare_kernel(ways, waits, mine, *refs):
    line, through = waits
    pairs, ones, outs = refs[:ways], refs[ways : 2 * ways], refs[2 * ways + through : 2 * ways + through + line]
    pair, one, share = refs[-3:]
    pair[...] = added(pairs)
    one[...] = added(ones)
    rows = pair.shape[1] // len(outs)
    share[3 * rows :] = one[pair.shape[1] :, :]
    for c, out in enumerate(outs):
        start = pl.multiple_of((mine[1] ^ c) * rows, 8)
        share[:rows] = pair[0, pl.ds(start, rows), :]
        share[rows : 2 * rows] = pair[1, pl.ds(start, rows), :]
        share[2 * rows : 3 * rows] = one[pl.ds(start, rows), :]
        out[...] = share[...].astype(BF16)


def project_reshare(mine, pairs, ones, ways, through):
    rows = 3 * pairs[0].shape[1] // ways + SMALL_ROWS
    return plain_call(
        partial(project_reshare_kernel, len(pairs), (ways, len(through))), [*pairs, *ones], mine,
        [shape((rows, D))] * ways, "project_reshare",
        [pltpu.VMEM(pairs[0].shape, F32), pltpu.VMEM(ones[0].shape, F32), pltpu.VMEM((rows, D), F32)], (), through)


def project_piece_kernel(mine, *refs):
    parts, (out, by_logits, by_weights, total) = refs[:-4], refs[-4:]
    total[...] = added(parts)
    rows = out.shape[1]
    for m in range(3):
        out[m] = total[m * rows : (m + 1) * rows, :].astype(BF16)
    small = total[3 * rows :, :]
    groups = [small[:, g * 128 : g * 128 + H] for g in range(3)]
    eye = lax.broadcasted_iota(jnp.int32, (H, H), 0) == lax.broadcasted_iota(jnp.int32, (H, H), 1)
    by_logits[...] = lax.dot_general(
        jnp.concatenate([groups[0], groups[1][:4]]), jnp.where(eye, DH ** -0.5, 0.0), (((0,), (0,)), ((), ())),
        precision=lax.Precision.HIGHEST, preferred_element_type=F32)
    by_weights[...] = jnp.concatenate([groups[1][4:], groups[2]])


def project_piece(mine, parts):
    rows = parts[0].shape[0]
    outs, _ = plain_call(
        project_piece_kernel, list(parts), mine,
        [shape((3, (rows - SMALL_ROWS) // 3, D))] + [shape((H, H), F32)] * 2, "project_piece",
        [pltpu.VMEM((rows, D), F32)])
    return outs


def stack_kernel(count, waits, mine, *refs):
    out, at = refs[count + waits], 0
    for ref in refs[:count]:
        out[at : at + ref.shape[0]] = ref[...]
        at += ref.shape[0]


def stack(mine, parts, name, first=()):
    rows = sum(p.shape[0] for p in parts)
    (out,), _ = plain_call(
        partial(stack_kernel, len(parts), len(first)), list(parts), mine, [shape((rows,) + parts[0].shape[1:])], name,
        (), first)
    return out


def tokens_kernel(waits, at, *refs):
    near, near_came, far, forwarded, out = *refs[:4], refs[4 + waits]
    for i, ref in enumerate((near, near_came, far.at[0], forwarded)):
        out[at[0] ^ i] = ref[...]


def tokens_of(at, came, name, first=(), through=()):
    (out,), through = plain_call(
        partial(tokens_kernel, len(first) + len(through)), list(came), at, [shape((4,) + came[0].shape)], name, (), first,
        through)
    return (out, *through) if through else out


def weigh(out, weight):
    product = out[...] * weight[...].astype(F32)
    return sum(product[:, c : c + 128] for c in range(0, D, 128))


def as_row(weighed):
    return jnp.sum(weighed[...].T, axis=0, keepdims=True)


def spread_kernel(sizes, place, own, other, w_query, w_key, w_value, gain, *refs):
    outs, by_gain, weighed = refs[-5:-2], refs[-2], refs[-1]
    matrix = pl.program_id(0)
    plane, line = sizes
    rows = own.shape[2]

    @pl.when(matrix == 0)
    def zero():
        weighed[...] = jnp.zeros_like(weighed)

    for i, (out, weight) in enumerate(zip(outs, (w_query, w_key, w_value))):

        @pl.when(matrix == i)
        def here():
            for c, pieces in enumerate((own, other)):
                for p in range(plane):
                    for n in range(line):
                        of_plane, of_line = n % 2 + 2 * (p % 2), p // 2 + 2 * (n // 2)
                        at = (place[0] ^ c) * plane * line + (place[1] ^ of_plane) * line + (place[2] ^ of_line)
                        out[pl.ds(pl.multiple_of(at * rows, 8), rows), :] = pieces[p * line + n, 0].astype(F32)
            weighed[...] += weigh(out, weight)

    @pl.when(matrix == 2)
    def finish():
        by_gain[...] = (as_row(weighed) / gain[...])[0]


def matrix_outs(down, over):
    specs, shapes, begin, places = [], [], 0, []
    for d, o in zip(down, over):
        count = d * o

        def place_of(m, *at, begin=begin, count=count, o=o):
            within = jnp.clip(m - begin, 0, count - 1)
            return (within // o, within % o)

        places.append(place_of)
        specs.append(pl.BlockSpec((D, D), place_of))
        shapes.append(shape((d * D, o * D), F32))
        begin += count
    return specs, shapes, begin, places


def spread(place, sizes, own, other, w_query, w_key, w_value, gain, first):
    out_specs, out_shape, count, _ = matrix_outs((1, 1, 1), (1, 1, 1))
    devices, matrices, rows, _ = own.shape
    block = pl.BlockSpec((devices, 1, rows, D), lambda m, place: (0, m, 0, 0))
    square = fixed((D, D))
    return step_call(
        partial(spread_kernel, sizes), place, count, [block, block, square, square, square, fixed((1, D))] + [ANY] * len(first),
        (own, other, w_query, w_key, w_value, gain, *first),
        out_specs + [fixed((D,))], out_shape + [shape((D,), F32)], 0, "spread", [pltpu.VMEM((D, 128), F32)])


def fill_kernel(counts, wide_count, starts, pieces, w_hidden, gain, *refs):
    outs, by_gain, weighed = refs[:3], refs[3], refs[4]
    matrix, begin, rows = pl.program_id(0), 0, pieces.shape[2]

    @pl.when(matrix == 0)
    def zero():
        weighed[...] = jnp.zeros_like(weighed)

    for index, (out, count) in enumerate(zip(outs, counts)):
        for table, low, high in ((0, begin, min(begin + count, wide_count)), (1, max(begin, wide_count), begin + count)):
            if low < high:

                @pl.when((matrix >= low) & (matrix < high))
                def here():
                    for device, start in enumerate(starts[table]):
                        out[start : start + rows, :] = pieces[device, 0].astype(F32)
                    if index == 1:
                        weighed[...] += weigh(out, w_hidden)

        begin += count

    @pl.when(matrix == begin - 1)
    def finish():
        by_gain[...] = (as_row(weighed) / gain[...])[0]


def fill(pieces, starts, w_hidden, gain):
    blocks = w_hidden.shape[1] // D
    down, over = (blocks, 1, 1), (1, blocks, 1)
    out_specs, out_shape, count, places = matrix_outs(down, over)
    devices, matrices, rows, _ = pieces.shape
    line = whole((1, D))
    return pl.pallas_call(
        partial(fill_kernel, tuple(d * o for d, o in zip(down, over)), wide_and_thin(blocks)[0], starts),
        grid=(count,),
        in_specs=[pl.BlockSpec((devices, 1, rows, D), lambda m: (0, m, 0, 0)), pl.BlockSpec((D, D), places[1]), line],
        out_specs=out_specs + [whole((D,))],
        out_shape=out_shape + [shape((D,), F32)],
        scratch_shapes=[pltpu.VMEM((D, 128), F32)],
        compiler_params=params(),
        name="fill",
    )(pieces, w_hidden, gain)


BOTH = ("rows", "seq")


def swap(values, mask):
    n = lax.axis_size("rows") * lax.axis_size("seq")
    return lax.ppermute(values, BOTH, [(s, s ^ mask) for s in range(n)])


def device_bits():
    n = lax.axis_size("rows") * lax.axis_size("seq")
    return [1 << b for b in range(n.bit_length() - 1)]


def masks(dims):
    return [(c, sum(bit for i, bit in enumerate(dims) if c >> i & 1)) for c in range(1 << len(dims))]


def place(dims):
    me = lax.axis_index(BOTH)
    return sum(((me // bit) % 2) << i for i, bit in enumerate(dims))


def exchange(parts, dims):
    return [swap(part, mask) if mask else part for part, (c, mask) in zip(parts, masks(dims))]


def chip_groups():
    chips = device_bits()[1:]
    plane, line, rows = chips[:2], [], HALF >> 2
    for bit in chips[2:]:
        if rows >> (len(line) + 1) << (len(line) + 1) == rows and (rows >> (len(line) + 1)) % 8 == 0:
            line.append(bit)
    return plane, line, chips[2 + len(line) :]


def finish_sum(total, dims):
    for bit in dims:
        total = (total.astype(F32) + swap(total, bit).astype(F32)).astype(total.dtype)
    return total


def row_starts(first, second):
    starts = []
    for device in range(1 << len(device_bits())):
        row, size = 0, D
        for dims in ([1], first, second):
            size >>= len(dims)
            row += size * sum(((device // bit) % 2) << i for i, bit in enumerate(dims))
        starts.append(row)
    return tuple(starts)


def trade(values, dims):
    n = lax.axis_size("rows") * lax.axis_size("seq")
    groups, found = [], set()
    for device in range(n):
        if device not in found:
            group = [device ^ mask for c, mask in masks(dims)]
            found.update(group)
            groups.append(group)
    return lax.all_to_all(values, BOTH, split_axis=0, concat_axis=0, tiled=True, axis_index_groups=groups)


def widen(mine, values, dims, name, first=()):
    return stack(mine, exchange([values] * (1 << len(dims)), dims), name, first)


def send_far(parts):
    return (*parts[:2], swap(parts[2], 2))


def hand_on(parts):
    mine, near, far = parts
    return mine, swap(near, 1), far, swap(far[1], 1)


def per_device(
    inputs,
    segment_ids,
    gain_one,
    w_query,
    w_key,
    w_value,
    w_out,
    mix_logits,
    mix_weights,
    gain_two,
    w_hidden,
    w_back,
    cotangent,
):
    plane, line, others = chip_groups()
    where = jnp.stack([place([1]), place(plane), place(line)])
    core, spots = where[:1], where[1:]
    mixed = plane + line
    late_plane, early_line = mixed[1:3], mixed[:1] + mixed[3:]
    sizes = (1 << len(plane), 1 << len(line))
    parts, seq = lax.axis_size("seq"), lax.axis_index("seq")
    row_bits, at = device_bits()[: parts.bit_length() - 1], seq.reshape(1)
    ids = lax.dynamic_slice_in_dim(segment_ids, seq, 1, 0)
    gain_one, gain_two = gain_one.reshape(1, D), gain_two.reshape(1, D)
    scale = DH ** -0.5
    mix_l = mix_logits.astype(F32) * scale
    mix_w = mix_weights.astype(F32)

    came = exchange([lax.dynamic_index_in_dim(inputs, seq ^ i, 0, keepdims=False) for i in range(parts)], row_bits)
    near = parts // 2
    begun = project(at, came[:near], 0, gain_one, w_query, w_key, w_value, (), cotangent)
    cots = exchange(begun[8:], row_bits)
    x, normed_t, q, q_t, k, k_t, v, v_t = project(
        at, came[near:], near, gain_one, w_query, w_key, w_value, begun[:8])
    soft, attended = attend(mix_l, mix_w, ids, q_t, k, v_t)
    out, (cot, normed_two, activated, grad_hidden, grad_middle, grad_attn, g, g_t) = feed(
        at, x, attended, cots, w_out, w_hidden, w_back, gain_two
    )
    wide_kept, wide_sent = wide_weight_grads(core, activated, cot, normed_two, grad_hidden)
    thin_kept, thin_sent = thin_weight_grads(core, normed_two, grad_hidden, attended, grad_attn, [wide_kept])
    wide, thin = shares_of(
        spots[1:], wide_kept, swap(wide_sent, 1), thin_kept, swap(thin_sent, 1), sizes[0], sizes[1], [thin_kept])
    grad_q, grad_logits, by_logits = query_grads(mix_w, mix_l, soft, v, g_t, k_t, q_t, [wide, thin[0]])
    wide, thin, far = reshare(spots, trade(wide, plane), exchange(thin, line), [grad_q], out[2:])
    out = send_far((*out[:2], *far))
    grad_k = key_grads(mix_l, grad_logits, q, [wide[0]])
    piece, far = piece_of(spots, exchange(wide, line), trade(thin, plane), [grad_k], out[2:])
    out = hand_on((*out[:2], *far))
    pieces = lax.all_gather(finish_sum(piece, others), BOTH, axis=0)
    pair_kept, pair_sent = project_weight_grads(core, normed_t, [grad_q, grad_k], (), [piece])
    pair = split(spots[:1], pair_kept, swap(pair_sent, 1), sizes[0], "split_pair")
    grad_v, by_weights = value_grads(mix_w, soft, v, g, [piece, pair[0]])
    pair = exchange(pair, plane)
    one_kept, one_sent = project_weight_grads(core, normed_t, [grad_v], [by_logits, by_weights], [*pair[1:], out[1], out[3]])
    one = split_small(spots[:1], one_kept, swap(one_sent, 1), sizes[0], "split_one")
    grad_in = input_grads(
        at, parts, grad_q, grad_k, grad_v, x, grad_middle, w_query, w_key, w_value, gain_one, one[0])
    shares, grad_in = project_reshare(spots, pair, exchange(one, plane), sizes[1], grad_in)
    own, by_logits, by_weights = [finish_sum(a, others) for a in project_piece(spots, exchange(shares, line))]
    grad_in = send_far(grad_in)
    block_out, far = tokens_of(at, out, "block_out", [own], grad_in[2:])
    grad_inputs = tokens_of(at, hand_on((*grad_in[:2], far)), "grad_inputs")
    own = widen(spots, own[None], early_line, "stack_line", [grad_inputs])
    grad_w_back, grad_w_hidden, grad_w_out, grad_gain_two = fill(
        pieces, (row_starts(plane, line), row_starts(line, plane)), w_hidden, gain_two)
    own = widen(spots, own, late_plane, "stack_plane", [grad_w_out])
    grad_w_query, grad_w_key, grad_w_value, grad_gain_one = spread(
        where, sizes, own, swap(own, 1), w_query, w_key, w_value, gain_one, [grad_w_out])
    return (
        block_out,
        grad_inputs,
        grad_gain_one,
        grad_w_query,
        grad_w_key,
        grad_w_value,
        grad_w_out,
        by_logits,
        by_weights,
        grad_gain_two,
        grad_w_hidden,
        grad_w_back,
    )


def solution(mesh):
    sharded, copied = P("rows", "seq", None), P()
    in_specs = (sharded, P("rows", None)) + (copied,) * 10 + (sharded,)
    out_specs = (sharded, sharded) + (copied,) * 10
    return jax.shard_map(
        per_device, mesh=mesh, in_specs=in_specs, out_specs=out_specs, check_vma=False
    )
```

```python
from functools import partial

from jax import lax
import jax
import jax.numpy as jnp
from jax.experimental import pallas as pl
from jax.experimental.pallas import tpu as pltpu
from jax.sharding import PartitionSpec as P

D, H, DH, LEN, TILE = 768, 12, 64, 1024, 256
TILES = LEN // TILE
F32, BF16 = jnp.float32, jnp.bfloat16
FORWARD_HEADS, BACKWARD_HEADS = 4, 2
VMEM_LIMIT = 65480 * 1024
LOG2_E = 1.4426950408889634
MATMUL_FLOPS = 2 * H * 10 * TILE * TILE * D


def span(i):
    return slice(i * TILE, (i + 1) * TILE)


def head_rows(h):
    return slice(h * DH, (h + 1) * DH)


def mm(a, b):
    return jnp.dot(a, b, preferred_element_type=F32)


def whole(shape):
    return pl.BlockSpec(shape, lambda i: (0,) * len(shape), pipeline_mode=pl.Buffered(1))


def some_heads(count, shape):
    return pl.BlockSpec((count,) + shape, lambda i: (i,) + (0,) * len(shape))


SMEM = pl.BlockSpec(memory_space=pltpu.SMEM)


def params():
    return pltpu.CompilerParams(dimension_semantics=("arbitrary",), vmem_limit_bytes=VMEM_LIMIT)


def shape(s, t=BF16):
    return jax.ShapeDtypeStruct(s, t)


def attend_kernel(mix_l, mix_w, id_row, id_col, q_t, k, v_t, soft, out, bias, scaled, acc):
    step = pl.program_id(0)

    @pl.when(step == 0)
    def start():
        acc[...] = jnp.zeros_like(acc)
        for t in range(TILES):
            for u in range(t + 1):
                allowed = id_col[span(u), :] == id_row[:, span(t)]
                if u == t:
                    key = lax.broadcasted_iota(jnp.int32, (TILE, TILE), 0)
                    query = lax.broadcasted_iota(jnp.int32, (TILE, TILE), 1)
                    allowed = allowed & (key <= query)
                bias[span(u), span(t)] = jnp.where(allowed, 0.0, -1e30)

    for i in range(FORWARD_HEADS):
        j = step * FORWARD_HEADS + i
        for h in range(H):
            weight = mix_l[h, j] * LOG2_E
            scaled[i, head_rows(h), :] = (q_t[head_rows(h), :].astype(F32) * weight).astype(BF16)
        for t in reversed(range(TILES)):
            n = (t + 1) * TILE
            logits = mm(k[:n, :], scaled[i, :, span(t)]) + bias[:n, span(t)]
            e = jnp.exp2(logits - jnp.max(logits, axis=0, keepdims=True))
            p = (e * (1.0 / jnp.sum(e, axis=0, keepdims=True))).astype(BF16)
            soft[i, :n, span(t)] = p
            part = mm(v_t[:, :n], p)
            for h in range(H):
                acc[head_rows(h), span(t)] += part[head_rows(h), :] * mix_w[j, h]

    @pl.when(step == H // FORWARD_HEADS - 1)
    def finish():
        for t in range(TILES):
            out[span(t), :] = acc[:, span(t)].T.astype(BF16)


def attend(mix_l, mix_w, ids, q_t, k, v_t):
    heads = FORWARD_HEADS
    return pl.pallas_call(
        attend_kernel,
        grid=(H // heads,),
        in_specs=[SMEM, SMEM, whole((1, LEN)), whole((LEN, 1)), whole((D, LEN)), whole((LEN, D)), whole((D, LEN))],
        out_specs=[some_heads(heads, (LEN, LEN)), whole((LEN, D))],
        out_shape=[shape((H, LEN, LEN)), shape((LEN, D))],
        scratch_shapes=[
            pltpu.VMEM((LEN, LEN), F32), pltpu.VMEM((heads, D, LEN), BF16), pltpu.VMEM((D, LEN), F32)
        ],
        compiler_params=params(),
        cost_estimate=pl.CostEstimate(flops=MATMUL_FLOPS // 4, bytes_accessed=LEN * LEN, transcendentals=0),
        name="attend",
    )(mix_l, mix_w, ids.reshape(1, LEN), ids.reshape(LEN, 1), q_t, k, v_t)


def head_row(weight_of):
    head = lax.broadcasted_iota(jnp.int32, (1, D), 1) // DH
    row = jnp.full((1, D), weight_of(0), F32)
    for h in range(1, H):
        row = jnp.where(head == h, weight_of(h), row)
    return row


def value_grads_kernel(mix_w, soft, v, g, *rest):
    out, mix_grad, acc = rest[-3:]
    step = pl.program_id(0)

    @pl.when(step == 0)
    def start():
        acc[...] = jnp.zeros_like(acc)

    for i in range(BACKWARD_HEADS):
        total = jnp.zeros((1, D), F32)
        mix_row = head_row(lambda h: mix_w[step * BACKWARD_HEADS + i, h])
        for u in range(TILES):
            part = mm(soft[i, span(u), u * TILE :], g[u * TILE :, :])
            acc[span(u), :] += part * mix_row
            total = total + jnp.sum(part * v[span(u), :].astype(F32), axis=0, keepdims=True)
        mix_grad[i] = total

    @pl.when(step == H // BACKWARD_HEADS - 1)
    def finish():
        out[...] = acc[...].astype(BF16)


def query_grads_kernel(heads, mix_w, mix_l, soft, v, g_t, k_t, q_t, *rest):
    before, (out, grad_logits, mix_grad, acc, scaled) = rest[0], rest[-5:]
    step = pl.program_id(0)
    first_head = heads[0] + step * BACKWARD_HEADS

    @pl.when(step == 0)
    def start():
        acc[...] = before[...] if heads[0] else jnp.zeros_like(acc)

    for i in range(BACKWARD_HEADS):
        j = first_head + i
        for h in range(H):
            scaled[i, head_rows(h), :] = (g_t[head_rows(h), :].astype(F32) * mix_w[j, h]).astype(BF16)
    order = [(i, t) for i in range(BACKWARD_HEADS) for t in reversed(range(TILES))]

    def grad_soft(i, t):
        return mm(v[: (t + 1) * TILE, :], scaled[i, :, span(t)])

    coming = grad_soft(*order[0])
    total = jnp.zeros((D, 128), F32)
    for at, (i, t) in enumerate(order):
        n = (t + 1) * TILE
        p = soft[i, :n, span(t)].astype(F32)
        weighted = p * coming
        low = (weighted - p * jnp.sum(weighted, axis=0, keepdims=True)).astype(BF16)
        grad_logits[i, :n, span(t)] = low
        if at + 1 < len(order):
            coming = grad_soft(*order[at + 1])
        part = mm(k_t[:, :n], low)
        for h in range(H):
            acc[head_rows(h), span(t)] += part[head_rows(h), :] * mix_l[h, first_head + i]
        product = part * q_t[:, span(t)].astype(F32)
        total = total + product[:, :128] + product[:, 128:]
        if t == 0:
            mix_grad[i] = jnp.sum(total.T, axis=0, keepdims=True)
            total = jnp.zeros((D, 128), F32)

    @pl.when(step == pl.num_programs(0) - 1)
    def finish():
        if heads[1] < H:
            out[...] = acc[...]
        else:
            for t in range(TILES):
                out[span(t), :] = acc[:, span(t)].T.astype(BF16)


def key_grads_kernel(mix_l, grad_logits, q, *rest):
    out, acc = rest[-2:]
    step = pl.program_id(0)

    @pl.when(step == 0)
    def start():
        acc[...] = jnp.zeros_like(acc)

    for i in range(BACKWARD_HEADS):
        mix_row = head_row(lambda h: mix_l[h, step * BACKWARD_HEADS + i])
        for u in range(TILES):
            acc[span(u), :] += mm(grad_logits[i, span(u), u * TILE :], q[u * TILE :, :]) * mix_row

    @pl.when(step == H // BACKWARD_HEADS - 1)
    def finish():
        out[...] = acc[...].astype(BF16)


def back_call(kernel, heads, in_specs, out_specs, out_shape, scratch, matmuls, name):
    def run(*operands):
        *used, first = operands
        return pl.pallas_call(
            kernel,
            grid=(heads // BACKWARD_HEADS,),
            in_specs=in_specs + [pl.BlockSpec(memory_space=pl.ANY)] * len(first),
            out_specs=out_specs,
            out_shape=out_shape,
            scratch_shapes=scratch,
            compiler_params=params(),
            cost_estimate=pl.CostEstimate(
                flops=matmuls * MATMUL_FLOPS * heads // H // 8, bytes_accessed=LEN * LEN, transcendentals=0
            ),
            name=name,
        )(*used, *first)

    return run


ROW, COLUMN = whole((LEN, D)), whole((D, LEN))
PER_HEAD, PER_HEAD_ROW = some_heads(BACKWARD_HEADS, (LEN, LEN)), some_heads(BACKWARD_HEADS, (1, D))


def value_grads(mix_w, soft, v, g, first):
    grads, mix_grad = back_call(
        value_grads_kernel,
        H,
        [SMEM, PER_HEAD, ROW, ROW],
        [ROW, PER_HEAD_ROW],
        [shape((LEN, D)), shape((H, 1, D), F32)],
        [pltpu.VMEM((LEN, D), F32)],
        1,
        "value_grads",
    )(mix_w, soft, v, g, first)
    return grads, mix_grad


def query_grads(mix_w, mix_l, soft, v, g_t, k_t, q_t, first, heads=(0, H), before=()):
    low, high = heads
    count, last = high - low, high == H
    per_head = pl.BlockSpec((BACKWARD_HEADS, LEN, LEN), lambda i: (i + low // BACKWARD_HEADS, 0, 0))
    grads, grad_logits, mix_grad = back_call(
        partial(query_grads_kernel, heads),
        count,
        [SMEM, SMEM, per_head, ROW, COLUMN, COLUMN, COLUMN] + [COLUMN] * len(before),
        [ROW if last else COLUMN, PER_HEAD, PER_HEAD_ROW],
        [shape((LEN, D)) if last else shape((D, LEN), F32), shape((count, LEN, LEN)), shape((count, 1, D), F32)],
        [pltpu.VMEM((D, LEN), F32), pltpu.VMEM((BACKWARD_HEADS, D, LEN), BF16)],
        2,
        "query_grads",
    )(mix_w, mix_l, soft, v, g_t, k_t, q_t, *before, first)
    return grads, grad_logits, mix_grad


def key_grads(mix_l, grad_logits, q, first):
    return back_call(
        key_grads_kernel, H, [SMEM, PER_HEAD, ROW], ROW, shape((LEN, D)), [pltpu.VMEM((LEN, D), F32)], 1,
        "key_grads",
    )(mix_l, grad_logits, q, first)


epsilon = 1e-06
GELU_SCALE = 0.7978845608028654
GELU_CUBIC = 0.044715
FEED_COLUMNS = 768
COST_SHARE = 4
HALF = D // 2
ANY = pl.BlockSpec(memory_space=pl.ANY)
VMEM = pl.BlockSpec(memory_space=pltpu.VMEM)


def against(left, right):
    return lax.dot_general(left, right, (((1,), (1,)), ((), ())), preferred_element_type=F32)


def across(left, right):
    return lax.dot_general(left, right, (((0,), (0,)), ((), ())), preferred_element_type=F32)


def inverse_rms(values):
    return lax.rsqrt(jnp.mean(values * values, axis=-1, keepdims=True) + epsilon)


def cost(matrices):
    return pl.CostEstimate(flops=int(matrices * LEN * D * D) // COST_SHARE, bytes_accessed=LEN * D, transcendentals=0)


def fixed(s):
    return pl.BlockSpec(s, lambda i, at: (0,) * len(s), pipeline_mode=pl.Buffered(1))


def tokens(rows, shift=0):
    return pl.BlockSpec((rows, D), lambda i, at: (at[0] ^ (i + shift), 0))


def tokens_t(columns, shift=0):
    return pl.BlockSpec((D, columns), lambda i, at: (0, at[0] ^ (i + shift)))


def step_call(kernel, at, steps, in_specs, operands, out_specs, out_shape, matrices, name, scratch=(), aliases=None):
    return pl.pallas_call(
        kernel,
        grid_spec=pltpu.PrefetchScalarGridSpec(
            num_scalar_prefetch=1, grid=(steps,), in_specs=in_specs, out_specs=out_specs, scratch_shapes=list(scratch)),
        out_shape=out_shape,
        input_output_aliases=aliases or {},
        compiler_params=params(),
        cost_estimate=cost(matrices),
        name=name,
    )(at, *operands)


def chosen(refs, step):
    values = refs[0][...]
    for i, ref in enumerate(refs[1:]):
        values = jnp.where(step == i + 1, ref[...], values)
    return values


def write_parts(outs, step, values):
    for i, out in enumerate(outs[:-1]):

        @pl.when(step == i)
        def write():
            out[...] = values

    far = outs[-1].shape[0]
    for i in range(far):

        @pl.when(step == len(outs) - 1 + i)
        def write_far():
            outs[-1][i] = values


def part_outs(parts, rows):
    near = parts // 2
    specs = [fixed((rows, D))] * near + [fixed((parts - near, rows, D))]
    return specs, [shape((rows, D))] * near + [shape((parts - near, rows, D))]


def project_kernel(steps, waits, shares, at, *refs):
    parts, (gain, w_query, w_key, w_value) = refs[:steps], refs[steps : steps + 4]
    rest = refs[steps + 4 + waits :]
    cotangent, rest = (rest[0], rest[1:]) if shares else (None, rest)
    row, normed_t, q, q_t, k, k_t, v, v_t = rest[:8]
    step = pl.program_id(0)
    low = chosen(parts, step)
    row[...] = low
    values = low.astype(F32)
    normed = (values * inverse_rms(values) * gain[...]).astype(BF16)
    normed_t[...] = normed.T
    for weight, out, out_t in ((w_query, q, q_t), (w_key, k, k_t), (w_value, v, v_t)):
        part = mm(normed, weight[...]).astype(BF16)
        out[...] = part
        out_t[...] = part.T
    if shares:

        @pl.when(step == 0)
        def lay_out():
            for i, out in enumerate(rest[8:]):
                out[...] = cotangent[at[0] ^ i]


def project(at, parts, shift, gain, w_query, w_key, w_value, before=(), cotangent=None):
    count, rows = len(parts), parts[0].shape[0]
    square, ways = fixed((D, D)), 0 if cotangent is None else cotangent.shape[0]
    row, column = (tokens(rows, shift), shape((LEN, D))), (tokens_t(rows, shift), shape((D, LEN)))
    outs = [row, column, row, column, row, column, row, column] + [(fixed((rows, D)), shape((rows, D)))] * ways
    start = 1 + count + 4
    return step_call(
        partial(project_kernel, count, len(before), ways > 0), at, count,
        [fixed((rows, D))] * count + [fixed((1, D)), square, square, square] + [ANY] * len(before)
        + [fixed((ways, rows, D))] * (ways > 0),
        (*parts, gain, w_query, w_key, w_value, *before) + ((cotangent,) if ways else ()),
        [o[0] for o in outs], [o[1] for o in outs], 3 * count / 4, "project",
        aliases={start + i: i for i in range(len(before))})


def feed_kernel(parts, at, x, attended, *refs):
    refs, both = refs[:-1], refs[-1]
    cots, (w_out, w_hidden, w_back, gain), rest = refs[:parts], refs[parts : parts + 4], refs[parts + 4 :]
    outs, (cot_row, normed_two, activated, grad_hidden, grad_middle, grad_attn, g, g_t) = rest[:-8], rest[-8:]
    step = pl.program_id(0)
    scale = gain[...]
    rows = cots[0].shape[0]
    spots = [pl.ds(pl.multiple_of(((at[0] ^ i) % 2) * rows, rows), rows) for i in range(2)]
    for i in range(2):
        both[spots[i], :] = chosen(cots[i::2], step)
    cotangent = both[...]
    cot_row[...] = cotangent
    middle = x[...].astype(F32) + mm(attended[...], w_out[...])
    inverse = inverse_rms(middle)
    n2 = (middle * inverse * scale).astype(BF16)
    normed_two[...] = n2
    total = middle
    grad_n2 = jnp.zeros_like(middle)
    width = FEED_COLUMNS
    for c in range(w_hidden.shape[1] // width):
        cols = slice(c * width, (c + 1) * width)
        hidden = mm(n2, w_hidden[:, cols])
        grad_act = against(cotangent, w_back[cols, :])
        squared = hidden * hidden
        tanh = jnp.tanh(GELU_SCALE * hidden * (1.0 + GELU_CUBIC * squared))
        half = 0.5 + 0.5 * tanh
        act = (hidden * half).astype(BF16)
        activated[:, cols] = act
        slope = half + (0.5 * GELU_SCALE) * hidden * (1.0 - tanh * tanh) * (1.0 + 3.0 * GELU_CUBIC * squared)
        grad = (grad_act * slope).astype(BF16)
        grad_hidden[:, cols] = grad
        total = total + mm(act, w_back[cols, :])
        grad_n2 = grad_n2 + against(grad, w_hidden[:, cols])
    both[...] = total.astype(BF16)
    near, far = outs[:-1], outs[-1]

    @pl.when(step == 0)
    def write_near():
        for i in range(2):
            near[i][...] = both[spots[i], :]

    @pl.when(step == 1)
    def write_far():
        for i in range(2):
            far[i] = both[spots[i], :]

    weighted = grad_n2 * scale
    mean = jnp.mean(weighted * middle, axis=-1, keepdims=True)
    grad_mid = cotangent.astype(F32) + inverse * weighted - middle * (inverse * inverse * inverse * mean)
    grad_middle[...] = grad_mid
    grad_low = grad_mid.astype(BF16)
    grad_attn[...] = grad_low
    grad = against(grad_low, w_out[...]).astype(BF16)
    g[...] = grad
    g_t[...] = grad.T


def feed(at, x, attended, cots, w_out, w_hidden, w_back, gain):
    ff, parts, rows = w_hidden.shape[1], len(cots), cots[0].shape[0]
    def pair(i, at):
        return (at[0] // 2) ^ i

    two = pl.BlockSpec((2 * rows, D), lambda i, at: (pair(i, at), 0))
    tile = (two, shape((LEN, D)))
    wide = (pl.BlockSpec((2 * rows, ff), lambda i, at: (pair(i, at), 0)), shape((LEN, ff)))
    outs = list(zip(*part_outs(parts, rows))) + [
        tile, tile, wide, wide, (two, shape((LEN, D), F32)), tile, tile,
        (pl.BlockSpec((D, 2 * rows), lambda i, at: (0, pair(i, at))), shape((D, LEN)))]
    found = step_call(
        partial(feed_kernel, parts), at, parts // 2,
        [two, two] + [fixed((rows, D))] * parts
        + [fixed((D, D)), fixed((D, ff)), fixed((ff, D)), fixed((1, D))],
        (x, attended, *cots, w_out, w_hidden, w_back, gain), [o[0] for o in outs], [o[1] for o in outs],
        2 + 4 * ff // D, "feed", [pltpu.VMEM((2 * rows, D), BF16)])
    return found[:-8], found[-8:]


def input_kernel(parts, at, grad_q, grad_k, grad_v, x, grad_middle, w_query, w_key, w_value, gain, first, *outs):
    upstream = against(grad_q[...], w_query[...]) + against(grad_k[...], w_key[...]) + against(grad_v[...], w_value[...])
    values = x[...].astype(F32)
    inverse = inverse_rms(values)
    weighted = upstream * gain[...]
    mean = jnp.mean(weighted * values, axis=-1, keepdims=True)
    low = (grad_middle[...] + inverse * weighted - values * (inverse * inverse * inverse * mean)).astype(BF16)
    write_parts(outs, pl.program_id(0), low)


def input_grads(at, parts, grad_q, grad_k, grad_v, x, grad_middle, w_query, w_key, w_value, gain, first):
    rows, square = LEN // parts, fixed((D, D))
    return step_call(
        partial(input_kernel, parts), at, parts, [tokens(rows)] * 5 + [square, square, square, fixed((1, D)), ANY],
        (grad_q, grad_k, grad_v, x, grad_middle, w_query, w_key, w_value, gain, first),
        *part_outs(parts, rows), 3, "input_grads")


def both_halves(kept, sent, product, left_kept, left_sent, right):
    kept[0, :HALF] = product(left_kept[...], right[...]).astype(BF16)
    sent[0, :HALF] = product(left_sent[...], right[...]).astype(BF16)


def wide_kernel(backs, core, act_kept, act_sent, cot, n2_kept, n2_sent, grad_hidden, kept, sent):
    step = pl.program_id(0)
    pl.when(step < backs)(partial(both_halves, kept, sent, across, act_kept, act_sent, cot))
    pl.when(step >= backs)(partial(both_halves, kept, sent, across, n2_kept, n2_sent, grad_hidden))


def thin_kernel(hiddens, core, n2_kept, n2_sent, grad_hidden, att_kept, att_sent, grad_attn, *refs):
    step, (kept, sent) = pl.program_id(0), refs[-2:]
    pl.when(step < hiddens)(partial(both_halves, kept, sent, across, n2_kept, n2_sent, grad_hidden))
    pl.when(step >= hiddens)(partial(both_halves, kept, sent, across, att_kept, att_sent, grad_attn))


def columns_half(other, at=lambda i: 0):
    return pl.BlockSpec((LEN, HALF), lambda i, core: (0, 2 * at(i) + (core[0] ^ other)))


def rows_half(other):
    return pl.BlockSpec((HALF, LEN), lambda i, core: (core[0] ^ other, 0))


def wide_and_thin(blocks):
    count = 2 * blocks + 1
    return 2 * count // 3, count - 2 * count // 3


def wide_weight_grads(core, activated, cot, normed_two, grad_hidden):
    blocks = activated.shape[1] // D
    count, _ = wide_and_thin(blocks)
    row, half = fixed((LEN, D)), pl.BlockSpec((1, HALF, D), lambda i, core: (i, 0, 0))

    def back(i):
        return jnp.minimum(i, blocks - 1)

    return step_call(
        partial(wide_kernel, blocks), core, count,
        [columns_half(0, back), columns_half(1, back), row, columns_half(0), columns_half(1),
         pl.BlockSpec((LEN, D), lambda i, core: (0, jnp.maximum(i - blocks, 0)))],
        (activated, activated, cot, normed_two, normed_two, grad_hidden),
        [half, half], [shape((count, HALF, D))] * 2, count, "wide_weight_grads")


def thin_weight_grads(core, normed_two, grad_hidden, attended, grad_attn, first):
    blocks = grad_hidden.shape[1] // D
    count, left = wide_and_thin(blocks)
    row, half = fixed((LEN, D)), pl.BlockSpec((1, HALF, D), lambda i, core: (i, 0, 0))
    return step_call(
        partial(thin_kernel, left - 1), core, left,
        [columns_half(0), columns_half(1),
         pl.BlockSpec((LEN, D), lambda i, core: (0, jnp.minimum(i + count - blocks, blocks - 1))),
         columns_half(0), columns_half(1), row] + [ANY] * len(first),
        (normed_two, normed_two, grad_hidden, attended, attended, grad_attn, *first),
        [half, half], [shape((left, HALF, D))] * 2, left, "thin_weight_grads")


SMALL_ROWS = 8


def small_sums(by_logits, by_weights):
    rows = jnp.concatenate([by_logits[:, 0, :], by_weights[:, 0, :]])
    head = lax.broadcasted_iota(jnp.int32, (D, 128), 0) // DH
    select = (head == lax.broadcasted_iota(jnp.int32, (D, 128), 1)).astype(F32)
    sums = jnp.dot(rows, select, precision=lax.Precision.HIGHEST, preferred_element_type=F32)
    groups = [sums[r : r + SMALL_ROWS, :] for r in range(0, 2 * H, SMALL_ROWS)]
    return jnp.concatenate(groups + [jnp.zeros((SMALL_ROWS, D - 128 * len(groups)), F32)], axis=1)


def project_weights_kernel(count, waits, core, nt_kept, nt_sent, *refs):
    grads, small, (kept, sent) = refs[:count], refs[count : -2 - waits], refs[-2:]
    for i, each in enumerate(grads):
        pl.when(pl.program_id(0) == i)(partial(both_halves, kept, sent, mm, nt_kept, nt_sent, each))
    if small:
        rows = jnp.concatenate([small_sums(*small), jnp.zeros((SMALL_ROWS, D), F32)]).astype(BF16)
        kept[0, HALF:] = rows
        sent[0, HALF:] = rows


def project_weight_grads(core, normed_t, grads, small=(), first=()):
    count, rows = len(grads), HALF + 2 * SMALL_ROWS * (len(small) > 0)
    half = pl.BlockSpec((1, rows, D), lambda i, core: (i, 0, 0))
    return step_call(
        partial(project_weights_kernel, count, len(first)), core, count,
        [rows_half(0), rows_half(1)] + [fixed((LEN, D))] * count + [fixed((H, 1, D))] * len(small) + [ANY] * len(first),
        (normed_t, normed_t, *grads, *small, *first), [half, half], [shape((count, rows, D))] * 2, count, "project_weight_grads")


def split_kernel(waits, mine, kept, came, *refs):
    outs, total = refs[waits:-1], refs[-1]
    total[...] = kept[...].astype(F32) + came[...].astype(F32)
    for c, out in enumerate(outs):
        rows = out.shape[1]
        out[...] = total[:, pl.ds(pl.multiple_of((mine[0] ^ c) * rows, 8), rows), :].astype(BF16)


def split(mine, kept, came, ways, name, first=()):
    count, rows, _ = kept.shape
    block = pl.BlockSpec((1, rows, D), lambda m, mine: (m, 0, 0))
    return step_call(
        partial(split_kernel, len(first)), mine, count, [block, block] + [ANY] * len(first), (kept, came, *first),
        [pl.BlockSpec((1, rows // ways, D), lambda m, mine: (m, 0, 0))] * ways,
        [shape((count, rows // ways, D))] * ways, 0, name, [pltpu.VMEM((1, rows, D), F32)])


def shares_kernel(wide_steps, mine, wide_kept, wide_came, thin_kept, thin_came, wide, *refs):
    thin, total, step = refs[:-1], refs[-1], pl.program_id(0)

    @pl.when(step < wide_steps)
    def of_wide():
        rows = wide.shape[2]
        for m in range(wide_kept.shape[0]):
            sums = wide_kept[m].astype(F32) + wide_came[m].astype(F32)
            for c in range(wide.shape[0]):
                wide[c, m] = sums[c * rows : (c + 1) * rows, :].astype(BF16)

    @pl.when(step >= wide_steps)
    def of_thin():
        total[...] = thin_kept[...].astype(F32) + thin_came[...].astype(F32)
        for c, out in enumerate(thin):
            rows = out.shape[1]
            out[...] = total[:, pl.ds(pl.multiple_of((mine[0] ^ c) * rows, 8), rows), :].astype(BF16)


def shares_of(mine, wide_kept, wide_came, thin_kept, thin_came, plane, line, first):
    count, left = wide_kept.shape[0], thin_kept.shape[0]
    per_step = 2
    steps = count // per_step

    def of_wide(m, mine):
        return jnp.minimum(m, steps - 1)

    half = pl.BlockSpec((per_step, HALF, D), lambda m, mine: (of_wide(m, mine), 0, 0))
    thin_half = fixed((left, HALF, D))
    outs = step_call(
        lambda mine, a, b, c, d, *refs: shares_kernel(steps, mine, a, b, c, d, *refs[len(first) :]), mine, steps + 1,
        [half, half, thin_half, thin_half] + [ANY] * len(first), (wide_kept, wide_came, thin_kept, thin_came, *first),
        [pl.BlockSpec((plane, per_step, HALF // plane, D), lambda m, mine: (0, of_wide(m, mine), 0, 0))]
        + [fixed((left, HALF // line, D))] * line,
        [shape((plane, count, HALF // plane, D))] + [shape((left, HALF // line, D))] * line, 0, "shares",
        [pltpu.VMEM((left, HALF, D), F32)])
    return outs[0], outs[1:]


def plain_call(kernel, operands, mine, out_shape, name, scratch=(), first=(), through=()):
    outs = pl.pallas_call(
        kernel,
        in_specs=[SMEM] + [VMEM] * len(operands) + [ANY] * (len(first) + len(through)),
        out_specs=[VMEM] * len(out_shape) + [ANY] * len(through),
        out_shape=list(out_shape) + [shape(t.shape, t.dtype) for t in through],
        input_output_aliases={1 + len(operands) + len(first) + i: len(out_shape) + i for i in range(len(through))},
        scratch_shapes=list(scratch),
        compiler_params=pltpu.CompilerParams(vmem_limit_bytes=VMEM_LIMIT),
        name=name,
    )(mine, *operands, *first, *through)
    return outs[: len(out_shape)], outs[len(out_shape) :]


def added(refs):
    return sum(ref[...].astype(F32) for ref in refs)


def sum_first(ref):
    return sum(ref[i].astype(F32) for i in range(ref.shape[0]))


def reshare_kernel(line, waits, mine, wide, *refs):
    thin, outs, total = refs[:line], refs[line + waits :], refs[-1]
    total[...] = sum_first(wide)
    for c in range(line):
        rows = outs[c].shape[1]
        outs[c][...] = total[:, pl.ds(pl.multiple_of((mine[1] ^ c) * rows, 8), rows), :].astype(BF16)
    out = outs[line]
    thin_sum, rows = added(thin), out.shape[2]
    for c in range(out.shape[0]):
        out[c] = thin_sum[:, c * rows : (c + 1) * rows, :].astype(BF16)


def reshare(mine, wide, thin, first, through):
    plane, count, rows, _ = wide.shape
    line, (left, thin_rows, _) = len(thin), thin[0].shape
    outs, through = plain_call(
        partial(reshare_kernel, line, len(first) + len(through)), [wide, *thin], mine,
        [shape((count, rows // line, D))] * line + [shape((plane, left, thin_rows // plane, D))], "reshare",
        [pltpu.VMEM((count, rows, D), F32)], first, through)
    return outs[:line], outs[line], through


def piece_kernel(line, waits, mine, thin, *refs):
    wide, out = refs[:line], refs[line + waits]
    count = wide[0].shape[0]
    out[:count] = added(wide).astype(BF16)
    out[count:] = sum_first(thin).astype(BF16)


def piece_of(mine, wide, thin, first, through):
    (count, rows, _), left = wide[0].shape, thin.shape[1]
    (out,), through = plain_call(
        partial(piece_kernel, len(wide), len(first) + len(through)), [thin, *wide], mine,
        [shape((count + left, rows, D))], "piece", (), first, through)
    return out, through


def split_small_kernel(mine, kept, came, *refs):
    outs, total, share = refs[:-2], refs[-2], refs[-1]
    total[...] = kept[0].astype(F32) + came[0].astype(F32)
    rows = share.shape[0] - SMALL_ROWS
    share[rows:] = total[HALF : HALF + SMALL_ROWS, :]
    for c, out in enumerate(outs):
        share[:rows] = total[pl.ds(pl.multiple_of((mine[0] ^ c) * rows, 8), rows), :]
        out[...] = share[...].astype(BF16)


def split_small(mine, kept, came, ways, name):
    rows = HALF // ways + SMALL_ROWS
    outs, _ = plain_call(
        split_small_kernel, [kept, came], mine, [shape((rows, D))] * ways, name,
        [pltpu.VMEM(kept.shape[1:], F32), pltpu.VMEM((rows, D), F32)])
    return outs


def project_reshare_kernel(ways, waits, mine, *refs):
    line, through = waits
    pairs, ones, outs = refs[:ways], refs[ways : 2 * ways], refs[2 * ways + through : 2 * ways + through + line]
    pair, one, share = refs[-3:]
    pair[...] = added(pairs)
    one[...] = added(ones)
    rows = pair.shape[1] // len(outs)
    share[3 * rows :] = one[pair.shape[1] :, :]
    for c, out in enumerate(outs):
        start = pl.multiple_of((mine[1] ^ c) * rows, 8)
        share[:rows] = pair[0, pl.ds(start, rows), :]
        share[rows : 2 * rows] = pair[1, pl.ds(start, rows), :]
        share[2 * rows : 3 * rows] = one[pl.ds(start, rows), :]
        out[...] = share[...].astype(BF16)


def project_reshare(mine, pairs, ones, ways, through):
    rows = 3 * pairs[0].shape[1] // ways + SMALL_ROWS
    return plain_call(
        partial(project_reshare_kernel, len(pairs), (ways, len(through))), [*pairs, *ones], mine,
        [shape((rows, D))] * ways, "project_reshare",
        [pltpu.VMEM(pairs[0].shape, F32), pltpu.VMEM(ones[0].shape, F32), pltpu.VMEM((rows, D), F32)], (), through)


def project_piece_kernel(mine, *refs):
    parts, (out, by_logits, by_weights, total) = refs[:-4], refs[-4:]
    total[...] = added(parts)
    rows = out.shape[1]
    for m in range(3):
        out[m] = total[m * rows : (m + 1) * rows, :].astype(BF16)
    small = total[3 * rows :, :]
    groups = [small[:, g * 128 : g * 128 + H] for g in range(3)]
    eye = lax.broadcasted_iota(jnp.int32, (H, H), 0) == lax.broadcasted_iota(jnp.int32, (H, H), 1)
    by_logits[...] = lax.dot_general(
        jnp.concatenate([groups[0], groups[1][:4]]), jnp.where(eye, DH ** -0.5, 0.0), (((0,), (0,)), ((), ())),
        precision=lax.Precision.HIGHEST, preferred_element_type=F32)
    by_weights[...] = jnp.concatenate([groups[1][4:], groups[2]])


def project_piece(mine, parts):
    rows = parts[0].shape[0]
    outs, _ = plain_call(
        project_piece_kernel, list(parts), mine,
        [shape((3, (rows - SMALL_ROWS) // 3, D))] + [shape((H, H), F32)] * 2, "project_piece",
        [pltpu.VMEM((rows, D), F32)])
    return outs


def stack_kernel(count, waits, mine, *refs):
    out, at = refs[count + waits], 0
    for ref in refs[:count]:
        out[at : at + ref.shape[0]] = ref[...]
        at += ref.shape[0]


def stack(mine, parts, name, first=(), through=()):
    rows = sum(p.shape[0] for p in parts)
    (out,), through = plain_call(
        partial(stack_kernel, len(parts), len(first) + len(through)), list(parts), mine,
        [shape((rows,) + parts[0].shape[1:])], name, (), first, through)
    return (out, *through) if through else out


def tokens_kernel(waits, at, *refs):
    near, near_came, far, forwarded, out = *refs[:4], refs[4 + waits]
    for i, ref in enumerate((near, near_came, far.at[0], forwarded)):
        out[at[0] ^ i] = ref[...]


def tokens_of(at, came, name, first=(), through=()):
    (out,), through = plain_call(
        partial(tokens_kernel, len(first) + len(through)), list(came), at, [shape((4,) + came[0].shape)], name, (), first,
        through)
    return (out, *through) if through else out


def weigh(out, weight):
    product = out[...] * weight[...].astype(F32)
    return sum(product[:, c : c + 128] for c in range(0, D, 128))


def as_row(weighed):
    return jnp.sum(weighed[...].T, axis=0, keepdims=True)


def spread_kernel(sizes, place, own, other, w_query, w_key, w_value, gain, *refs):
    outs, by_gain, weighed = refs[-5:-2], refs[-2], refs[-1]
    matrix = pl.program_id(0)
    plane, line = sizes
    rows = own.shape[2]

    @pl.when(matrix == 0)
    def zero():
        weighed[...] = jnp.zeros_like(weighed)

    for i, (out, weight) in enumerate(zip(outs, (w_query, w_key, w_value))):

        @pl.when(matrix == i)
        def here():
            for c, pieces in enumerate((own, other)):
                for p in range(plane):
                    for n in range(line):
                        of_plane, of_line = n % 2 + 2 * (p % 2), p // 2 + 2 * (n // 2)
                        at = (place[0] ^ c) * plane * line + (place[1] ^ of_plane) * line + (place[2] ^ of_line)
                        out[pl.ds(pl.multiple_of(at * rows, 8), rows), :] = pieces[p * line + n, 0].astype(F32)
            weighed[...] += weigh(out, weight)

    @pl.when(matrix == 2)
    def finish():
        by_gain[...] = (as_row(weighed) / gain[...])[0]


def matrix_outs(down, over):
    specs, shapes, begin, places = [], [], 0, []
    for d, o in zip(down, over):
        count = d * o

        def place_of(m, *at, begin=begin, count=count, o=o):
            within = jnp.clip(m - begin, 0, count - 1)
            return (within // o, within % o)

        places.append(place_of)
        specs.append(pl.BlockSpec((D, D), place_of))
        shapes.append(shape((d * D, o * D), F32))
        begin += count
    return specs, shapes, begin, places


def spread(place, sizes, own, other, w_query, w_key, w_value, gain, first):
    out_specs, out_shape, count, _ = matrix_outs((1, 1, 1), (1, 1, 1))
    devices, matrices, rows, _ = own.shape
    block = pl.BlockSpec((devices, 1, rows, D), lambda m, place: (0, m, 0, 0))
    square = fixed((D, D))
    return step_call(
        partial(spread_kernel, sizes), place, count, [block, block, square, square, square, fixed((1, D))] + [ANY] * len(first),
        (own, other, w_query, w_key, w_value, gain, *first),
        out_specs + [fixed((D,))], out_shape + [shape((D,), F32)], 0, "spread", [pltpu.VMEM((D, 128), F32)])


def fill_kernel(counts, wide_count, starts, pieces, w_hidden, gain, *refs):
    refs = refs[-5:]
    outs, by_gain, weighed = refs[:3], refs[3], refs[4]
    matrix, begin, rows = pl.program_id(0), 0, pieces.shape[2]

    @pl.when(matrix == 0)
    def zero():
        weighed[...] = jnp.zeros_like(weighed)

    for index, (out, count) in enumerate(zip(outs, counts)):
        for table, low, high in ((0, begin, min(begin + count, wide_count)), (1, max(begin, wide_count), begin + count)):
            if low < high:

                @pl.when((matrix >= low) & (matrix < high))
                def here():
                    for device, start in enumerate(starts[table]):
                        out[start : start + rows, :] = pieces[device, 0].astype(F32)
                    if index == 1:
                        weighed[...] += weigh(out, w_hidden)

        begin += count

    @pl.when(matrix == begin - 1)
    def finish():
        by_gain[...] = (as_row(weighed) / gain[...])[0]


def fill(pieces, starts, w_hidden, gain, first):
    blocks = w_hidden.shape[1] // D
    down, over = (blocks, 1, 1), (1, blocks, 1)
    out_specs, out_shape, count, places = matrix_outs(down, over)
    devices, matrices, rows, _ = pieces.shape
    line = whole((1, D))
    return pl.pallas_call(
        partial(fill_kernel, tuple(d * o for d, o in zip(down, over)), wide_and_thin(blocks)[0], starts),
        grid=(count,),
        in_specs=[pl.BlockSpec((devices, 1, rows, D), lambda m: (0, m, 0, 0)), pl.BlockSpec((D, D), places[1]), line]
        + [ANY] * len(first),
        out_specs=out_specs + [whole((D,))],
        out_shape=out_shape + [shape((D,), F32)],
        scratch_shapes=[pltpu.VMEM((D, 128), F32)],
        compiler_params=params(),
        name="fill",
    )(pieces, w_hidden, gain, *first)


BOTH = ("rows", "seq")


def swap(values, mask):
    n = lax.axis_size("rows") * lax.axis_size("seq")
    return lax.ppermute(values, BOTH, [(s, s ^ mask) for s in range(n)])


def device_bits():
    n = lax.axis_size("rows") * lax.axis_size("seq")
    return [1 << b for b in range(n.bit_length() - 1)]


def masks(dims):
    return [(c, sum(bit for i, bit in enumerate(dims) if c >> i & 1)) for c in range(1 << len(dims))]


def place(dims):
    me = lax.axis_index(BOTH)
    return sum(((me // bit) % 2) << i for i, bit in enumerate(dims))


def exchange(parts, dims):
    return [swap(part, mask) if mask else part for part, (c, mask) in zip(parts, masks(dims))]


def chip_groups():
    chips = device_bits()[1:]
    plane, line, rows = chips[:2], [], HALF >> 2
    for bit in chips[2:]:
        if rows >> (len(line) + 1) << (len(line) + 1) == rows and (rows >> (len(line) + 1)) % 8 == 0:
            line.append(bit)
    return plane, line, chips[2 + len(line) :]


def finish_sum(total, dims):
    for bit in dims:
        total = (total.astype(F32) + swap(total, bit).astype(F32)).astype(total.dtype)
    return total


def row_starts(first, second):
    starts = []
    for device in range(1 << len(device_bits())):
        row, size = 0, D
        for dims in ([1], first, second):
            size >>= len(dims)
            row += size * sum(((device // bit) % 2) << i for i, bit in enumerate(dims))
        starts.append(row)
    return tuple(starts)


def trade(values, dims):
    n = lax.axis_size("rows") * lax.axis_size("seq")
    groups, found = [], set()
    for device in range(n):
        if device not in found:
            group = [device ^ mask for c, mask in masks(dims)]
            found.update(group)
            groups.append(group)
    return lax.all_to_all(values, BOTH, split_axis=0, concat_axis=0, tiled=True, axis_index_groups=groups)


def widen(mine, values, dims, name, first=(), through=()):
    return stack(mine, exchange([values] * (1 << len(dims)), dims), name, first, through)


def send_far(parts):
    return (*parts[:2], swap(parts[2], 2))


def hand_on(parts):
    mine, near, far = parts
    return mine, swap(near, 1), far, swap(far[1], 1)


def per_device(
    inputs,
    segment_ids,
    gain_one,
    w_query,
    w_key,
    w_value,
    w_out,
    mix_logits,
    mix_weights,
    gain_two,
    w_hidden,
    w_back,
    cotangent,
):
    plane, line, others = chip_groups()
    where = jnp.stack([place([1]), place(plane), place(line)])
    core, spots = where[:1], where[1:]
    mixed = plane + line
    late_plane, early_line = mixed[1:3], mixed[:1] + mixed[3:]
    sizes = (1 << len(plane), 1 << len(line))
    parts, seq = lax.axis_size("seq"), lax.axis_index("seq")
    row_bits, at = device_bits()[: parts.bit_length() - 1], seq.reshape(1)
    ids = lax.dynamic_slice_in_dim(segment_ids, seq, 1, 0)
    gain_one, gain_two = gain_one.reshape(1, D), gain_two.reshape(1, D)
    scale = DH ** -0.5
    mix_l = mix_logits.astype(F32) * scale
    mix_w = mix_weights.astype(F32)

    came = exchange([lax.dynamic_index_in_dim(inputs, seq ^ i, 0, keepdims=False) for i in range(parts)], row_bits)
    near = parts // 2
    begun = project(at, came[:near], 0, gain_one, w_query, w_key, w_value, (), cotangent)
    cots = exchange(begun[8:], row_bits)
    x, normed_t, q, q_t, k, k_t, v, v_t = project(
        at, came[near:], near, gain_one, w_query, w_key, w_value, begun[:8])
    soft, attended = attend(mix_l, mix_w, ids, q_t, k, v_t)
    out, (cot, normed_two, activated, grad_hidden, grad_middle, grad_attn, g, g_t) = feed(
        at, x, attended, cots, w_out, w_hidden, w_back, gain_two
    )
    wide_kept, wide_sent = wide_weight_grads(core, activated, cot, normed_two, grad_hidden)
    thin_kept, thin_sent = thin_weight_grads(core, normed_two, grad_hidden, attended, grad_attn, [wide_kept])
    wide, thin = shares_of(
        spots[1:], wide_kept, swap(wide_sent, 1), thin_kept, swap(thin_sent, 1), sizes[0], sizes[1], [thin_kept])
    grad_q, grad_logits, by_logits = query_grads(mix_w, mix_l, soft, v, g_t, k_t, q_t, [wide, thin[0]])
    wide, thin, _ = reshare(spots, trade(wide, plane), exchange(thin, line), [grad_q], [])
    grad_k = key_grads(mix_l, grad_logits, q, [wide[0]])
    piece, _ = piece_of(spots, exchange(wide, line), trade(thin, plane), [grad_k], [])
    pieces = lax.all_gather(finish_sum(piece, others), BOTH, axis=0)
    pair_kept, pair_sent = project_weight_grads(core, normed_t, [grad_q, grad_k], (), [piece])
    pair = split(spots[:1], pair_kept, swap(pair_sent, 1), sizes[0], "split_pair")
    grad_v, by_weights = value_grads(mix_w, soft, v, g, [piece, pair[0]])
    pair = exchange(pair, plane)
    one_kept, one_sent = project_weight_grads(core, normed_t, [grad_v], [by_logits, by_weights], pair[1:])
    one = split_small(spots[:1], one_kept, swap(one_sent, 1), sizes[0], "split_one")
    grad_in = input_grads(
        at, parts, grad_q, grad_k, grad_v, x, grad_middle, w_query, w_key, w_value, gain_one, one[0])
    shares, (*grad_in, far) = project_reshare(spots, pair, exchange(one, plane), sizes[1], [*grad_in, out[2]])
    out = hand_on(send_far((*out[:2], far)))
    own, by_logits, by_weights = [finish_sum(a, others) for a in project_piece(spots, exchange(shares, line))]
    block_out = tokens_of(at, out, "block_out", [own])
    own, *grad_in = widen(spots, own[None], early_line, "stack_line", [block_out], grad_in)
    grad_in = send_far(grad_in)
    grad_w_back, grad_w_hidden, grad_w_out, grad_gain_two = fill(
        pieces, (row_starts(plane, line), row_starts(line, plane)), w_hidden, gain_two, [own])
    own = widen(spots, own, late_plane, "stack_plane", [grad_w_out, grad_in[2]])
    grad_inputs = tokens_of(at, hand_on(grad_in), "grad_inputs", [own])
    grad_w_query, grad_w_key, grad_w_value, grad_gain_one = spread(
        where, sizes, own, swap(own, 1), w_query, w_key, w_value, gain_one, [grad_inputs])
    return (
        block_out,
        grad_inputs,
        grad_gain_one,
        grad_w_query,
        grad_w_key,
        grad_w_value,
        grad_w_out,
        by_logits,
        by_weights,
        grad_gain_two,
        grad_w_hidden,
        grad_w_back,
    )


def solution(mesh):
    sharded, copied = P("rows", "seq", None), P()
    in_specs = (sharded, P("rows", None)) + (copied,) * 10 + (sharded,)
    out_specs = (sharded, sharded) + (copied,) * 10
    return jax.shard_map(
        per_device, mesh=mesh, in_specs=in_specs, out_specs=out_specs, check_vma=False
    )
```
